32 devices in a mesh: grp: 2 (over x), exp: 16 (over z, y, core).
Axes of the slice: x: 2, y: 2, z: 4, core: 2. Of those that a mesh axis runs over, the one named last changes fastest.
Arguments:
- resid: bfloat16 [32, 2048], P(('grp', 'exp')), parts along dimension 0, may hold values from -6 to 6
- queries: bfloat16 [32, 2048], P(('grp', 'exp')), parts along dimension 0, may hold values from -6 to 6
- incoming_key_value: bfloat16 [32, 512], P(('grp', 'exp')), parts along dimension 0, may hold values from -6 to 6
- key_value_cache: bfloat16 [16, 3072, 512], P('grp', 'exp'), parts along dimension 0, may hold values from -6 to 6
- lengths: int32 [16], P('grp'), parts along dimension 0, may hold values from 384 to 3072, as said below
- norm_scale_vector: float32 [2048], replicated, may hold values from 0.1 to 1.9
- expert_choice: int32 [32, 8], P(('grp', 'exp')), parts along dimension 0, may hold values from 0 to 15, all different within a row; in each aligned block of 16 rows (0 to 15, 16 to 31, ...) at most 16 rows name the same one
- router_probability: float32 [32, 8], P(('grp', 'exp')), parts along dimension 0, may hold values from 0.05 to 1
- gate_weight: bfloat16 [16, 2048, 768], P('exp'), may hold values from -0.125 to 0.125
- up_weight: bfloat16 [16, 2048, 768], P('exp'), may hold values from -0.125 to 0.125
- down_weight: bfloat16 [16, 768, 2048], P('exp'), may hold values from -0.21875 to 0.21875
- adapter_model: bfloat16 [16, 96, 2048], P(None, None, 'exp'), may hold values from -0.41992188 to 0.41992188
- adapter_hidden: bfloat16 [16, 96, 768], P(None, None, 'exp'), may hold values from -0.41992188 to 0.41992188
Outputs:
- layer_out: bfloat16 [32, 2048], P(('grp', 'exp')), parts along dimension 0
The draws below stay inside these ranges and needn't reach their ends.
There are 2 independent parts, one for each index of `grp`. The reference program is written for one: setup_inputs(seed, part) draws one part's arguments, and reference() takes and returns one part's arrays. A program takes and returns all parts, laid end to end along the dimension named above; an argument that names none is the same for every part. Nothing has to cross between parts.
Inputs may be any that keep to these rules, and one draw needn't show every extreme that they name: `lengths`: every sequence keeps at least 384 cached positions, and some sequence has all 3072. `expert_choice`: no expert is named by more than 16 tokens of a group, a bound that some block reaches.
All inputs are finite; a program needn't handle non-finite values.
Results may differ from the reference program's by a relative error of at most 0.0062.
The reference program's roundings to bfloat16 on the way count: a program that leaves them out, or rounds other values in their place, can miss the bound.
Values may be sent and summed in bfloat16 or wider, within the bound.
No kernel may reach another device: no remote copies, remote signals or barrier semaphores. Data moves between devices by JAX's collectives and lax.ppermute only.
A program may use at most 64 MiB of HBM per device.

```python
import math
import jax
import jax.numpy as jnp
import numpy as np
from jax import lax

MODEL_WIDTH = 2048
HIDDEN_UNITS = 768
QUERY_HEADS = 16
KEY_VALUE_HEADS = 2
HEAD_WIDTH = 128
ADAPTER_RANK = 32
TOPK = 8
CACHE_SLOTS = 3072
EXPERT_TOTAL = 16
TOKEN_COUNT = 16
SEQUENCE_COUNT = 8
BLOCK_SLOTS = 192
CAP = 16
N_EXP = 16


def draw_queries(key, part):
    key = jax.random.fold_in(key, 11)
    array_shape = (TOKEN_COUNT, QUERY_HEADS * HEAD_WIDTH)
    base = jnp.clip(jax.random.normal(key, array_shape, jnp.float32), -6.0, 6.0)
    return base.astype(jnp.bfloat16)


def draw_key_value_cache(key, part):
    key = jax.random.fold_in(key, 12)
    array_shape = (SEQUENCE_COUNT, CACHE_SLOTS, 2 * KEY_VALUE_HEADS * HEAD_WIDTH)
    base = jnp.clip(jax.random.normal(key, array_shape, jnp.float32), -6.0, 6.0)
    return base.astype(jnp.bfloat16)


def draw_lengths(key, part):
    key = jax.random.fold_in(key, 13)
    first_key, second_key = jax.random.split(key)
    drawn = jax.random.randint(first_key, (SEQUENCE_COUNT,), CACHE_SLOTS // 8, CACHE_SLOTS + 1, dtype=jnp.int32)
    chosen = jax.random.randint(second_key, (), 0, SEQUENCE_COUNT, dtype=jnp.int32)
    return jnp.where(jnp.arange(SEQUENCE_COUNT, dtype=jnp.int32) == chosen, CACHE_SLOTS, drawn).astype(jnp.int32)


def steps_of(key, extent, pieces, least, largest):
    def one(position, shards_of):
        steps = jax.random.uniform(jax.random.fold_in(jax.random.fold_in(key, 6), position), (shards_of,), jnp.float32, least / len(pieces), largest / len(pieces))
        return jnp.repeat(jnp.exp(steps), extent[position] // shards_of).reshape((-1,) + (1,) * (len(extent) - position - 1))

    loudness = one(*pieces[0])
    for cut in pieces[1:]:
        loudness = loudness * one(*cut)
    return loudness


def assign_block(stream_key, own, number, rows, amount, top, limit, lean):
    sequence = jax.random.permutation(stream_key, amount)
    packed, common = portions_of(amount, rows * top, limit, lean, True), portions_of(amount, rows * top, limit, lean, False)
    places = jnp.arange(amount)

    def named(sizes, turn):
        used = int((sizes > 0).sum())
        fixed = max(1, used // 4)
        moved = fixed + (places - fixed + turn * (used - fixed)) % max(1, amount - fixed)
        return jnp.zeros((amount,), jnp.int32).at[sequence[jnp.where(places < fixed, places, moved)]].set(jnp.asarray(sizes, jnp.int32))

    sizes = jnp.where(number % 4 == 0, named(packed, number // 4), named(common, number - number // 4 - 1))
    mixed = jax.random.permutation(jax.random.fold_in(own, 3), amount)
    giver, sink = mixed[0:amount // 2 * 2:2], mixed[1:amount // 2 * 2:2]
    margin = jnp.minimum(sizes[giver] - 1, limit - sizes[sink]) // 2
    margin = jnp.where((giver == sequence[0]) | (sink == sequence[0]) | (sizes[sink] == 0), 0, jnp.maximum(margin, 0))
    moved = jax.random.randint(jax.random.fold_in(own, 4), (amount // 2,), 0, 1 << 20) % (margin + 1)
    sizes = sizes.at[giver].add(-moved).at[sink].add(moved)
    items = jnp.searchsorted(jnp.cumsum(sizes), jnp.arange(rows * top), side="right").astype(jnp.int32)
    table = items.reshape(top, rows).T
    table = table[jax.random.permutation(jax.random.fold_in(own, 1), rows)]
    turn = jax.random.randint(jax.random.fold_in(own, 2), (rows, 1), 0, top)
    return jnp.take_along_axis(table, (jnp.arange(top)[None, :] + turn) % top, axis=1)


def portions_of(amount, total, bound, lean, full):
    loads = [(1 << 20) // math.isqrt(standing ** lean) + 1 for standing in range(1, amount + 1)]
    largest = bound if full else min(bound, max(-(-total // amount), total * loads[0] // sum(loads)))
    least = 1 if total - largest >= amount - 1 else 0
    given, spare = [largest] + [least] * (amount - 1), total - largest - least * (amount - 1)
    while spare > 0:
        free = [i for i in range(1, amount) if given[i] < largest] or [i for i in range(1, amount) if given[i] < bound]
        whole, budget = sum([loads[i] for i in free]), spare
        for i in free:
            addition = min(bound - given[i], max(1, budget * loads[i] // whole), spare)
            given[i] = given[i] + addition
            spare = spare - addition
    return np.array(given)


def bell_draw(key, dims, spread, most, cuts=(), kind=jnp.bfloat16):
    result = spread * jax.random.normal(key, dims, jnp.float32)
    if cuts:
        result = result * steps_of(key, dims, cuts, -0.22, 0.18)
    return jnp.clip(result, -most, most).astype(kind)


def setup_inputs(seed: int = 0, part: int = 0) -> dict:
    key_of = jax.random.split(jax.random.key(seed), 14)
    part_splits = jax.random.split(jax.random.fold_in(key_of[13], part), 14)
    resid = bell_draw(part_splits[0], (TOKEN_COUNT, MODEL_WIDTH), 1.0, 6.0, ((0, 16),))
    queries = draw_queries(jax.random.fold_in(jax.random.fold_in(key_of[13], part), 71), part)
    incoming_key_value = bell_draw(part_splits[2], (TOKEN_COUNT, 2 * KEY_VALUE_HEADS * HEAD_WIDTH), 1.0, 6.0, ((0, 16),))
    key_value_cache = draw_key_value_cache(jax.random.fold_in(jax.random.fold_in(key_of[13], part), 71), part)
    lengths = draw_lengths(jax.random.fold_in(jax.random.fold_in(key_of[13], part), 71), part)
    norm_scale_vector = jnp.clip(1.0 + 0.18 * jax.random.normal(key_of[5], (MODEL_WIDTH,), jnp.float32), 0.1, 1.9)
    expert_choice_keys = jax.random.split(jax.random.fold_in(part_splits[6], 1), TOKEN_COUNT // TOKEN_COUNT)
    expert_choice_turns = jax.random.permutation(jax.random.fold_in(part_splits[6], 3), TOKEN_COUNT // TOKEN_COUNT)
    expert_choice = jax.vmap(lambda own, number: assign_block(jax.random.fold_in(part_splits[6], 2), own, number, TOKEN_COUNT, EXPERT_TOTAL, TOPK, CAP, 2))(expert_choice_keys, expert_choice_turns).reshape((TOKEN_COUNT, TOPK))
    router_probability = jnp.clip(jnp.exp(math.log(1.0) - 2.9957323 * jax.random.uniform(part_splits[7], (TOKEN_COUNT, TOPK), jnp.float32) ** steps_of(part_splits[7], (TOKEN_COUNT, TOPK), ((0, 16),), -0.2, 0.2)), 0.05, 1.0)
    gate_weight = bell_draw(key_of[8], (EXPERT_TOTAL, MODEL_WIDTH, HIDDEN_UNITS), MODEL_WIDTH ** -0.5, 0.125, ((0, 16),))
    up_weight = bell_draw(key_of[9], (EXPERT_TOTAL, MODEL_WIDTH, HIDDEN_UNITS), MODEL_WIDTH ** -0.5, 0.125, ((0, 16),))
    down_weight = bell_draw(key_of[10], (EXPERT_TOTAL, HIDDEN_UNITS, MODEL_WIDTH), HIDDEN_UNITS ** -0.5, 0.21875, ((0, 16),))
    adapter_model = bell_draw(key_of[11], (EXPERT_TOTAL, 3 * ADAPTER_RANK, MODEL_WIDTH), 0.07, 0.41992188, ((2, 16),))
    adapter_hidden = bell_draw(key_of[12], (EXPERT_TOTAL, 3 * ADAPTER_RANK, HIDDEN_UNITS), 0.07, 0.41992188, ((2, 16),))
    return dict(resid=resid, queries=queries, incoming_key_value=incoming_key_value, key_value_cache=key_value_cache, lengths=lengths, norm_scale_vector=norm_scale_vector, expert_choice=expert_choice, router_probability=router_probability, gate_weight=gate_weight, up_weight=up_weight, down_weight=down_weight, adapter_model=adapter_model, adapter_hidden=adapter_hidden)


floor_score = -1e+30
epsilon = 1e-06

def reference(resid, queries, incoming_key_value, key_value_cache, lengths, norm_scale_vector, expert_choice, router_probability, gate_weight, up_weight, down_weight, adapter_model, adapter_hidden):
    grouped_heads = QUERY_HEADS // KEY_VALUE_HEADS
    key_value_width = KEY_VALUE_HEADS * HEAD_WIDTH
    inv_root = HEAD_WIDTH ** (-0.5)
    query_matrix = queries.astype(jnp.float32).reshape(SEQUENCE_COUNT, 2, KEY_VALUE_HEADS, grouped_heads, HEAD_WIDTH)
    new_all = incoming_key_value.astype(jnp.float32).reshape(SEQUENCE_COUNT, 2, 2 * key_value_width)

    def one_sequence(items):
        query_seq, sequence_cache, length_seq, newest = items
        stored_keys = sequence_cache[:, :key_value_width].astype(jnp.float32).reshape(N_EXP, BLOCK_SLOTS, KEY_VALUE_HEADS, HEAD_WIDTH)
        stored_values = sequence_cache[:, key_value_width:].astype(jnp.float32).reshape(N_EXP, BLOCK_SLOTS, KEY_VALUE_HEADS, HEAD_WIDTH)
        scores = jnp.einsum('pgih,bcgh->bpgic', query_seq, stored_keys) * inv_root
        positions = jnp.arange(CACHE_SLOTS, dtype=jnp.int32).reshape(N_EXP, 1, 1, 1, BLOCK_SLOTS)
        in_range = positions < length_seq
        scores = jnp.where(in_range, scores, floor_score)
        block_max = lax.optimization_barrier(jnp.max(scores, axis=-1))
        weights = jnp.where(in_range, jnp.exp(scores - block_max[..., None]), 0.0).astype(jnp.bfloat16).astype(jnp.float32)
        block_sum = lax.optimization_barrier(jnp.sum(weights, axis=-1))
        block_acc = jnp.einsum('bpgic,bcgh->bpgih', weights, stored_values)
        newest_keys = newest[:, :key_value_width].reshape(2, KEY_VALUE_HEADS, HEAD_WIDTH)
        newest_values = newest[:, key_value_width:].reshape(2, KEY_VALUE_HEADS, HEAD_WIDTH)
        new_scores = jnp.einsum('pgih,jgh->pgij', query_seq, newest_keys) * inv_root
        new_mask = (jnp.arange(2)[None, :] <= jnp.arange(2)[:, None]).reshape(2, 1, 1, 2)
        new_scores = jnp.where(new_mask, new_scores, floor_score)
        new_max = lax.optimization_barrier(jnp.max(new_scores, axis=-1))
        new_weights = jnp.where(new_mask, jnp.exp(new_scores - new_max[..., None]), 0.0).astype(jnp.bfloat16).astype(jnp.float32)
        new_sum = lax.optimization_barrier(jnp.sum(new_weights, axis=-1))
        new_acc = jnp.einsum('pgij,jgh->pgih', new_weights, newest_values)
        highest = jnp.maximum(lax.optimization_barrier(jnp.max(block_max, axis=0)), new_max)
        block_share = jnp.exp(block_max - highest[None])
        fresh_share = jnp.exp(new_max - highest)
        denominator = lax.optimization_barrier(jnp.sum(block_share * block_sum, axis=0)) + fresh_share * new_sum
        numerator = lax.optimization_barrier(jnp.sum(block_share[..., None] * block_acc, axis=0)) + fresh_share[..., None] * new_acc
        return (numerator / denominator[..., None]).reshape(2, QUERY_HEADS * HEAD_WIDTH)
    context = lax.map(one_sequence, (query_matrix, key_value_cache, lengths, new_all)).reshape(TOKEN_COUNT, MODEL_WIDTH)
    hidden = resid.astype(jnp.float32) + context
    normed = (hidden * lax.rsqrt(lax.optimization_barrier(jnp.mean(hidden * hidden, axis=-1, keepdims=True)) + epsilon) * norm_scale_vector).astype(jnp.bfloat16)
    shares = router_probability / lax.optimization_barrier(jnp.sum(router_probability, axis=-1, keepdims=True))
    picks = (expert_choice[:, :, None] == jnp.arange(EXPERT_TOTAL, dtype=jnp.int32)[None, None, :]).astype(jnp.float32)
    gates = lax.optimization_barrier(jnp.sum(shares[:, :, None] * picks, axis=1)).astype(jnp.bfloat16)

    def one_expert(moe, expert_index):
        model_factor = adapter_model[expert_index]
        hidden_factor = adapter_hidden[expert_index]
        gate_fold = (gate_weight[expert_index].astype(jnp.float32) + jnp.dot(model_factor[0:ADAPTER_RANK].T, hidden_factor[0:ADAPTER_RANK], preferred_element_type=jnp.float32)).astype(jnp.bfloat16)
        up_fold = (up_weight[expert_index].astype(jnp.float32) + jnp.dot(model_factor[ADAPTER_RANK:2 * ADAPTER_RANK].T, hidden_factor[ADAPTER_RANK:2 * ADAPTER_RANK], preferred_element_type=jnp.float32)).astype(jnp.bfloat16)
        down_fold = (down_weight[expert_index].astype(jnp.float32) + jnp.dot(hidden_factor[2 * ADAPTER_RANK:3 * ADAPTER_RANK].T, model_factor[2 * ADAPTER_RANK:3 * ADAPTER_RANK], preferred_element_type=jnp.float32)).astype(jnp.bfloat16)
        chosen = jnp.any(expert_choice == expert_index, axis=1)
        order = jnp.argsort(jnp.where(chosen, 0, 1).astype(jnp.int32), stable=True)[:CAP].astype(jnp.int32)
        rows = normed[order]
        weight = gates[order, expert_index].astype(jnp.float32)
        gate_part = jnp.dot(rows, gate_fold, preferred_element_type=jnp.float32)
        up_part = jnp.dot(rows, up_fold, preferred_element_type=jnp.float32)
        act = (jax.nn.silu(gate_part) * up_part).astype(jnp.bfloat16)
        output = jnp.dot(act, down_fold, preferred_element_type=jnp.float32)
        return (moe.at[order].add(output * weight[:, None]), None)
    moe, unused = lax.scan(one_expert, jnp.zeros((TOKEN_COUNT, MODEL_WIDTH), jnp.float32), jnp.arange(EXPERT_TOTAL, dtype=jnp.int32))
    return (hidden + moe).astype(jnp.bfloat16)
```

```python
import functools

import jax
import jax.numpy as jnp
from jax import lax
from jax.experimental import pallas as pl
from jax.experimental.pallas import tpu as pltpu
from jax.sharding import PartitionSpec as P

QUERY_HEADS = 16
KEY_VALUE_HEADS = 2
HEAD_WIDTH = 128
ADAPTER_RANK = 32
GROUPED = QUERY_HEADS // KEY_VALUE_HEADS
KEY_VALUE_WIDTH = KEY_VALUE_HEADS * HEAD_WIDTH
INV_ROOT = HEAD_WIDTH ** (-0.5)
STAT_ROWS = 8
PART_ROWS = QUERY_HEADS + STAT_ROWS

floor_score = -1e30
epsilon = 1e-06

VMEM_LIMIT = 48 * 1024 * 1024
VMEM = pl.BlockSpec(memory_space=pltpu.VMEM)
SMEM = pl.BlockSpec(memory_space=pltpu.SMEM)
PARAMS = pltpu.CompilerParams(vmem_limit_bytes=VMEM_LIMIT)


def iota(shape, dim):
    return lax.broadcasted_iota(jnp.int32, shape, dim)


def attend_kernel(lengths, offset, query, cache, part):
    sequences, block, _ = cache.shape
    rows = 2 * QUERY_HEADS
    first_group = (iota((rows, HEAD_WIDTH), 0) % QUERY_HEADS) < GROUPED
    diagonal = iota((QUERY_HEADS, HEAD_WIDTH), 0) == iota((QUERY_HEADS, HEAD_WIDTH), 1)
    stat_row = iota((STAT_ROWS, HEAD_WIDTH), 0)
    positions = offset[0] + iota((rows, block), 1)

    def step(s, carry):
        both = query[pl.ds(2 * s, 2)].reshape(rows, HEAD_WIDTH)
        zero = jnp.zeros_like(both)
        wide = jnp.concatenate(
            [jnp.where(first_group, both, zero), jnp.where(first_group, zero, both)], axis=1
        )
        keys = cache[s, :, :KEY_VALUE_WIDTH]
        values = cache[s, :, KEY_VALUE_WIDTH:]
        scores = (
            lax.dot_general(
                wide, keys, (((1,), (1,)), ((), ())), preferred_element_type=jnp.float32
            )
            * INV_ROOT
        )
        valid = positions < lengths[s]
        scores = jnp.where(valid, scores, floor_score)
        top = jnp.max(scores, axis=1, keepdims=True)
        weights = jnp.where(valid, jnp.exp(scores - top), 0.0).astype(jnp.bfloat16)
        total = jnp.sum(weights.astype(jnp.float32), axis=1, keepdims=True)
        acc = jnp.dot(weights, values, preferred_element_type=jnp.float32)
        acc = jnp.where(first_group, acc[:, :HEAD_WIDTH], acc[:, HEAD_WIDTH:])
        for p in range(2):
            cut = slice(p * QUERY_HEADS, (p + 1) * QUERY_HEADS)
            part[2 * s + p, :QUERY_HEADS] = acc[cut]
            top_row = jnp.sum(jnp.where(diagonal, top[cut], 0.0), axis=0, keepdims=True)
            sum_row = jnp.sum(jnp.where(diagonal, total[cut], 0.0), axis=0, keepdims=True)
            part[2 * s + p, QUERY_HEADS:] = jnp.where(
                stat_row == 0, top_row, jnp.where(stat_row == 1, sum_row, 0.0)
            )
        return carry

    if sequences <= 8:
        for s in range(sequences):
            step(s, 0)
    else:
        lax.fori_loop(0, sequences, step, 0)


def merge_kernel(
    me, got, query, own, partner, resid, scale, choice, probability, hidden_out, normed_out, gates_out
):
    sources = got.shape[0]
    first_group = iota((QUERY_HEADS, HEAD_WIDTH), 0) < GROUPED

    def by_head(rows, at):
        return jnp.where(first_group, rows[at : at + 1], rows[at + 1 : at + 2])

    q = query[...].astype(jnp.float32)
    own_rows = own[...].astype(jnp.float32)
    partner_rows = partner[...].astype(jnp.float32)
    second = lax.rem(me[0], 2) == 1
    own_score = jnp.sum(q * by_head(own_rows, 0), axis=1, keepdims=True) * INV_ROOT
    partner_score = jnp.sum(q * by_head(partner_rows, 0), axis=1, keepdims=True) * INV_ROOT
    partner_score = jnp.where(second, partner_score, floor_score)
    new_max = jnp.maximum(own_score, partner_score)
    own_weight = jnp.exp(own_score - new_max).astype(jnp.bfloat16).astype(jnp.float32)
    partner_weight = jnp.where(second, jnp.exp(partner_score - new_max), 0.0)
    partner_weight = partner_weight.astype(jnp.bfloat16).astype(jnp.float32)
    new_sum = own_weight + partner_weight
    new_acc = own_weight * by_head(own_rows, 2) + partner_weight * by_head(partner_rows, 2)

    stats = got[:, QUERY_HEADS:, :]
    maxima = stats[:, 0, :].T[:QUERY_HEADS]
    totals = stats[:, 1, :].T[:QUERY_HEADS]
    top = jnp.maximum(jnp.max(maxima, axis=1, keepdims=True), new_max)
    share = jnp.exp(maxima - top)
    fresh = jnp.exp(new_max - top)
    denominator = jnp.sum(share * totals, axis=1, keepdims=True) + fresh * new_sum
    numerator = fresh * new_acc
    for c in range(sources):
        numerator = numerator + share[:, c : c + 1] * got[c, :QUERY_HEADS, :]
    hidden = resid[...].astype(jnp.float32) + numerator / denominator
    width = QUERY_HEADS * HEAD_WIDTH
    squares = jnp.sum(jnp.sum(hidden * hidden, axis=1, keepdims=True), axis=0, keepdims=True)
    normed = hidden * lax.rsqrt(squares / width + epsilon) * scale[...]
    hidden_out[...] = hidden
    normed_out[...] = normed.astype(jnp.bfloat16)

    p = probability[...]
    shares = p / jnp.sum(p, axis=1, keepdims=True)
    lanes = iota(gates_out.shape, 1)
    gates = jnp.zeros(gates_out.shape, jnp.float32)
    for k in range(p.shape[1]):
        gates = gates + jnp.where(choice[:, k : k + 1] == lanes, shares[:, k : k + 1], 0.0)
    gates_out[...] = gates.astype(jnp.bfloat16).astype(jnp.float32)


def dot_pair(value, factor):
    high = value.astype(jnp.bfloat16)
    low = (value - high.astype(jnp.float32)).astype(jnp.bfloat16)
    return jnp.dot(high, factor, preferred_element_type=jnp.float32) + jnp.dot(
        low, factor, preferred_element_type=jnp.float32
    )


def expert_kernel(rows, gate_w, up_w, down_w, model, hidden, out):
    tokens = rows.shape[0]
    x = rows[...].astype(jnp.float32).reshape(tokens, -1).astype(jnp.bfloat16)
    r = ADAPTER_RANK
    mixed = lax.dot_general(
        x, model[: 2 * r], (((1,), (1,)), ((), ())), preferred_element_type=jnp.float32
    )
    gate = jnp.dot(x, gate_w[...], preferred_element_type=jnp.float32)
    gate = gate + dot_pair(mixed[:, :r], hidden[:r])
    up = jnp.dot(x, up_w[...], preferred_element_type=jnp.float32)
    up = up + dot_pair(mixed[:, r:], hidden[r : 2 * r])
    act = (gate / (1.0 + jnp.exp(-gate)) * up).astype(jnp.bfloat16)
    lowered = lax.dot_general(
        act, hidden[2 * r :], (((1,), (1,)), ((), ())), preferred_element_type=jnp.float32
    )
    result = jnp.dot(act, down_w[...], preferred_element_type=jnp.float32)
    result = result + dot_pair(lowered, model[2 * r :])
    for j in range(QUERY_HEADS):
        out[:, j, :] = result[:, j * HEAD_WIDTH : (j + 1) * HEAD_WIDTH]


def finish_kernel(hidden, gates, got, out):
    total = hidden[...]
    for c in range(got.shape[0]):
        total = total + gates[:, c : c + 1] * got[c]
    out[...] = total.astype(jnp.bfloat16)


def call(kernel, shapes, specs, *args):
    return pl.pallas_call(
        kernel,
        out_shape=shapes,
        in_specs=specs,
        out_specs=jax.tree.map(lambda _: VMEM, shapes),
        compiler_params=PARAMS,
    )(*args)


def exchange(parts):
    return lax.all_to_all(parts, "exp", split_axis=0, concat_axis=0, tiled=True)


def body(
    resid,
    queries,
    incoming_key_value,
    key_value_cache,
    lengths,
    norm_scale_vector,
    expert_choice,
    router_probability,
    gate_weight,
    up_weight,
    down_weight,
    adapter_model,
    adapter_hidden,
):
    n = lax.axis_size("exp")
    me = lax.axis_index("exp").astype(jnp.int32)
    heads = (QUERY_HEADS, HEAD_WIDTH)
    shape = jax.ShapeDtypeStruct
    block = key_value_cache.shape[1]

    query = queries.reshape(heads)
    fresh = incoming_key_value.reshape(2 * KEY_VALUE_HEADS, HEAD_WIDTH)
    partner = lax.ppermute(fresh, "exp", [(t, t ^ 1) for t in range(n)])
    all_queries = exchange(jnp.broadcast_to(query[None], (n,) + heads))
    part = call(
        attend_kernel,
        shape((n, PART_ROWS, HEAD_WIDTH), jnp.float32),
        [SMEM, SMEM, VMEM, VMEM],
        lengths,
        (me * block).reshape(1),
        all_queries,
        key_value_cache,
    )
    got = exchange(part)
    hidden, normed, gates = call(
        merge_kernel,
        (
            shape(heads, jnp.float32),
            shape(heads, jnp.bfloat16),
            shape((1, max(n, HEAD_WIDTH)), jnp.float32),
        ),
        [SMEM] + [VMEM] * 8,
        me.reshape(1),
        got,
        query,
        fresh,
        partner,
        resid.reshape(heads),
        norm_scale_vector.reshape(heads),
        expert_choice,
        router_probability,
    )
    rows = exchange(jnp.broadcast_to(normed[None], (n,) + heads))
    model = lax.all_to_all(adapter_model, "exp", split_axis=0, concat_axis=2, tiled=True)
    inner = lax.all_to_all(adapter_hidden, "exp", split_axis=0, concat_axis=2, tiled=True)
    out = call(
        expert_kernel,
        shape((n,) + heads, jnp.float32),
        [VMEM] * 6,
        rows,
        gate_weight[0],
        up_weight[0],
        down_weight[0],
        model[0],
        inner[0],
    )
    final = call(
        finish_kernel, shape(heads, jnp.bfloat16), [VMEM] * 3, hidden, gates, exchange(out)
    )
    return final.reshape(1, QUERY_HEADS * HEAD_WIDTH)


def solution(mesh):
    return jax.shard_map(
        body,
        mesh=mesh,
        in_specs=(
            P(("grp", "exp"), None),
            P(("grp", "exp"), None),
            P(("grp", "exp"), None),
            P("grp", "exp", None),
            P("grp"),
            P(),
            P(("grp", "exp"), None),
            P(("grp", "exp"), None),
            P("exp", None, None),
            P("exp", None, None),
            P("exp", None, None),
            P(None, None, "exp"),
            P(None, None, "exp"),
        ),
        out_specs=P(("grp", "exp"), None),
        check_vma=False,
    )
```

```python
import functools

import jax
import jax.numpy as jnp
from jax import lax
from jax.experimental import pallas as pl
from jax.experimental.pallas import tpu as pltpu
from jax.sharding import PartitionSpec as P

QUERY_HEADS = 16
KEY_VALUE_HEADS = 2
HEAD_WIDTH = 128
ADAPTER_RANK = 32
GROUPED = QUERY_HEADS // KEY_VALUE_HEADS
KEY_VALUE_WIDTH = KEY_VALUE_HEADS * HEAD_WIDTH
WIDTH = QUERY_HEADS * HEAD_WIDTH
INV_ROOT = HEAD_WIDTH ** (-0.5)
NEW_ROW = QUERY_HEADS
GATE_ROW = NEW_ROW + 2 * KEY_VALUE_HEADS
MESSAGE = (2 * QUERY_HEADS, HEAD_WIDTH)
HEADS = (QUERY_HEADS, HEAD_WIDTH)

floor_score = -1e30
epsilon = 1e-06

VMEM = pl.BlockSpec(memory_space=pltpu.VMEM)
SMEM = pl.BlockSpec(memory_space=pltpu.SMEM)
shape = jax.ShapeDtypeStruct


def call(kernel, shapes, specs, *args, limit=8):
    return pl.pallas_call(
        kernel,
        out_shape=shapes,
        in_specs=specs,
        out_specs=jax.tree.map(lambda _: VMEM, shapes),
        compiler_params=pltpu.CompilerParams(vmem_limit_bytes=limit * 1024 * 1024),
    )(*args)


def iota(dims, dim):
    return lax.broadcasted_iota(jnp.int32, dims, dim)


def as_rows(line, rows):
    return jnp.concatenate(
        [line[:, j * HEAD_WIDTH : (j + 1) * HEAD_WIDTH] for j in range(rows)], axis=0
    )


def stages_of(n):
    sizes, stride, found = [], 1, []
    while stride < n:
        size = 4 if n // stride % 4 == 0 else 2
        found.append((stride, size))
        stride *= size
    return found


def swap(value, n, distance):
    return lax.ppermute(value, "exp", [(t, t ^ distance) for t in range(n)])


def join_kernel(*refs):
    out = refs[-1]
    step = refs[0].shape[0]
    for k, ref in enumerate(refs[:-1]):
        out[k * step : (k + 1) * step] = ref[...]


def gather(block, n):
    pieces = [block]
    for index, (stride, size) in enumerate(stages_of(n)):
        if index:
            rows = sum(piece.shape[0] for piece in pieces)
            block = call(
                join_kernel,
                shape((rows,) + block.shape[1:], block.dtype),
                [VMEM] * len(pieces),
                *pieces,
            )
        pieces = [block] + [swap(block, n, k * stride) for k in range(1, size)]
    return pieces


def pack_kernel(query, new, choice, probability, out):
    q = as_rows(query[...].astype(jnp.float32), QUERY_HEADS)
    fresh = as_rows(new[...].astype(jnp.float32), 2 * KEY_VALUE_HEADS)
    p = probability[...]
    shares = p / jnp.sum(p, axis=1, keepdims=True)
    lanes = iota((1, HEAD_WIDTH), 1)
    gates = jnp.zeros((1, HEAD_WIDTH), jnp.float32)
    for k in range(p.shape[1]):
        gates = gates + jnp.where(choice[:, k : k + 1] == lanes, shares[:, k : k + 1], 0.0)
    rest = jnp.zeros((MESSAGE[0] - GATE_ROW - 1, HEAD_WIDTH), jnp.float32)
    out[0] = jnp.concatenate([q, fresh, gates, rest], axis=0).astype(jnp.bfloat16)


def encode(top, total, acc):
    lanes = iota(HEADS, 1)
    stats = jnp.zeros(HEADS, jnp.float32)
    for at, value in ((0, top), (3, total)):
        for k in range(3):
            part = value.astype(jnp.bfloat16).astype(jnp.float32)
            stats = jnp.where(lanes == at + k, part, stats)
            value = value - part
    return jnp.concatenate([acc, stats], axis=0).astype(jnp.bfloat16)


def decode(message):
    value = message.astype(jnp.float32)
    acc, stats = value[:QUERY_HEADS], value[QUERY_HEADS:]
    top = stats[:, 0:1] + stats[:, 1:2] + stats[:, 2:3]
    total = stats[:, 3:4] + stats[:, 4:5] + stats[:, 5:6]
    return top, total, acc


def merged(messages, extra=None):
    parts = [decode(message) for message in messages] + ([extra] if extra else [])
    top = functools.reduce(jnp.maximum, [part[0] for part in parts])
    total, acc = 0.0, 0.0
    for peak, amount, value in parts:
        share = jnp.exp(peak - top)
        total = total + share * amount
        acc = acc + share * value
    return top, total, acc


def attend_kernel(lengths, me, *refs, pieces, outs):
    got, cache, parts = refs[:pieces], refs[pieces], refs[pieces + 1 :]
    sequences, block, _ = cache.shape
    held = got[0].shape[0]
    rows = 2 * QUERY_HEADS
    first_group = (iota((rows, HEAD_WIDTH), 0) % QUERY_HEADS) < GROUPED
    positions = me[0] * block + iota((rows, block), 1)
    for u in range(sequences):
        s = lax.shift_right_logical(me[0], 1) ^ u
        source, at = got[2 * u // held], 2 * u % held
        both = jnp.concatenate([source[at, :QUERY_HEADS], source[at + 1, :QUERY_HEADS]], axis=0)
        zero = jnp.zeros_like(both)
        wide = jnp.concatenate(
            [jnp.where(first_group, both, zero), jnp.where(first_group, zero, both)], axis=1
        )
        keys = cache[s, :, :KEY_VALUE_WIDTH]
        values = cache[s, :, KEY_VALUE_WIDTH:]
        scores = (
            lax.dot_general(
                wide, keys, (((1,), (1,)), ((), ())), preferred_element_type=jnp.float32
            )
            * INV_ROOT
        )
        valid = positions < lengths[s]
        scores = jnp.where(valid, scores, floor_score)
        top = jnp.max(scores, axis=1, keepdims=True)
        weights = jnp.where(valid, jnp.exp(scores - top), 0.0).astype(jnp.bfloat16)
        total = jnp.sum(weights.astype(jnp.float32), axis=1, keepdims=True)
        acc = jnp.dot(weights, values, preferred_element_type=jnp.float32)
        acc = jnp.where(first_group, acc[:, :HEAD_WIDTH], acc[:, HEAD_WIDTH:])
        for p in range(2):
            cut = slice(p * QUERY_HEADS, (p + 1) * QUERY_HEADS)
            slot = 2 * u + p
            parts[slot % outs][slot // outs] = encode(top[cut], total[cut], acc[cut])


def merge_kernel(*refs, pieces, outs):
    got, parts = refs[:pieces], refs[pieces:]
    for slot in range(got[0].shape[0]):
        parts[slot % outs][slot // outs] = encode(*merged([ref[slot] for ref in got]))


def token_kernel(me, own, partner, resid, scale, *refs, pieces):
    got, (hidden_out, normed_out) = refs[:pieces], refs[pieces:]
    first_group = iota(HEADS, 0) < GROUPED

    def by_head(rows, at):
        return jnp.where(first_group, rows[at : at + 1], rows[at + 1 : at + 2])

    mine = own[0].astype(jnp.float32)
    other = partner[0].astype(jnp.float32)
    q = mine[:QUERY_HEADS]
    mine, other = mine[NEW_ROW:GATE_ROW], other[NEW_ROW:GATE_ROW]
    second = me[0] % 2 == 1
    own_score = jnp.sum(q * by_head(mine, 0), axis=1, keepdims=True) * INV_ROOT
    other_score = jnp.sum(q * by_head(other, 0), axis=1, keepdims=True) * INV_ROOT
    other_score = jnp.where(second, other_score, floor_score)
    new_max = jnp.maximum(own_score, other_score)
    own_weight = jnp.exp(own_score - new_max).astype(jnp.bfloat16).astype(jnp.float32)
    other_weight = jnp.where(second, jnp.exp(other_score - new_max), 0.0)
    other_weight = other_weight.astype(jnp.bfloat16).astype(jnp.float32)
    new_acc = own_weight * by_head(mine, 2) + other_weight * by_head(other, 2)
    _, total, acc = merged(
        [ref[0] for ref in got], (new_max, own_weight + other_weight, new_acc)
    )
    hidden = as_rows(resid[...].astype(jnp.float32), QUERY_HEADS) + acc / total
    squares = jnp.sum(jnp.sum(hidden * hidden, axis=1, keepdims=True), axis=0, keepdims=True)
    normed = hidden * lax.rsqrt(squares / WIDTH + epsilon) * scale[...]
    hidden_out[...] = hidden
    normed_out[0] = normed.astype(jnp.bfloat16)


def dot_pair(value, factor, contract):
    high = value.astype(jnp.bfloat16)
    low = (value - high.astype(jnp.float32)).astype(jnp.bfloat16)
    both = lax.dot_general(
        jnp.concatenate([high, low], axis=0),
        factor,
        (((1,), (contract,)), ((), ())),
        preferred_element_type=jnp.float32,
    )
    return both[: value.shape[0]] + both[value.shape[0] :]


def expert_kernel(me, gate_w, up_w, down_w, model, inner, *refs, pieces, outs):
    got, routes, parts = refs[:pieces], refs[pieces : 2 * pieces], refs[2 * pieces :]
    x = jnp.concatenate([ref[...].astype(jnp.float32) for ref in got], axis=0)
    tokens = x.shape[0]
    x = x.reshape(tokens, WIDTH).astype(jnp.bfloat16)
    r = ADAPTER_RANK
    mixed = lax.dot_general(
        x, model[: 2 * r], (((1,), (1,)), ((), ())), preferred_element_type=jnp.float32
    )
    gate = jnp.dot(x, gate_w[...], preferred_element_type=jnp.float32)
    gate = gate + dot_pair(mixed[:, :r], inner[:, :r], 1)
    up = jnp.dot(x, up_w[...], preferred_element_type=jnp.float32)
    up = up + dot_pair(mixed[:, r:], inner[:, r : 2 * r], 1)
    act = (gate / (1.0 + jnp.exp(-gate)) * up).astype(jnp.bfloat16)
    lowered = jnp.dot(act, inner[:, 2 * r : 3 * r], preferred_element_type=jnp.float32)
    result = jnp.dot(act, down_w[...], preferred_element_type=jnp.float32)
    result = result + dot_pair(lowered, model[2 * r :], 0)
    lanes = iota((1, HEAD_WIDTH), 1)
    for slot in range(tokens):
        held = routes[0].shape[0]
        route = routes[slot // held][slot % held][QUERY_HEADS:].astype(jnp.float32)
        route = route[GATE_ROW - QUERY_HEADS : GATE_ROW - QUERY_HEADS + 1]
        share = jnp.sum(jnp.where(lanes == me[0], route, 0.0), axis=1, keepdims=True)
        line = as_rows(result[slot : slot + 1] * share, QUERY_HEADS)
        parts[slot % outs][slot // outs] = line.astype(jnp.bfloat16)


def add_kernel(*refs, pieces, outs):
    got, parts = refs[:pieces], refs[pieces:]
    for slot in range(got[0].shape[0]):
        total = sum(ref[slot].astype(jnp.float32) for ref in got)
        parts[slot % outs][slot // outs] = total.astype(jnp.bfloat16)


def finish_kernel(hidden, *refs):
    got, out = refs[:-1], refs[-1]
    total = hidden[...] + sum(ref[0].astype(jnp.float32) for ref in got)
    line = jnp.concatenate([total[j : j + 1] for j in range(QUERY_HEADS)], axis=1)
    out[...] = line.astype(jnp.bfloat16)


def split_shapes(count, size, dims):
    return tuple(shape((count // size,) + dims, jnp.bfloat16) for _ in range(size))


def scatter(parts, n, kernel, dims):
    found = stages_of(n)
    for index, (stride, size) in enumerate(found):
        pieces = [parts[0]] + [swap(parts[k], n, k * stride) for k in range(1, size)]
        if index + 1 < len(found):
            outs = found[index + 1][1]
            parts = call(
                functools.partial(kernel, pieces=size, outs=outs),
                split_shapes(pieces[0].shape[0], outs, dims),
                [VMEM] * size,
                *pieces,
            )
    return pieces


def lora_pack_kernel(me, model, inner, *outs):
    ranks = model.shape[1]
    for d, out in enumerate(outs):
        at = me[0] ^ d
        out[:ranks] = model[at]
        out[ranks:, :ranks] = inner[at]
        out[ranks:, ranks:] = jnp.zeros((out.shape[0] - ranks, HEAD_WIDTH - ranks), out.dtype)


def lora_join_kernel(me, *refs):
    got, (model, inner) = refs[:-2], refs[-2:]
    ranks = model.shape[0]
    width = inner.shape[0] // len(got)
    for d, ref in enumerate(got):
        at = me[0] ^ d
        model[:, pl.ds(pl.multiple_of(at * HEAD_WIDTH, HEAD_WIDTH), HEAD_WIDTH)] = ref[:ranks]
        inner[pl.ds(pl.multiple_of(at * width, width), width)] = ref[ranks:]


def lora(adapter_model, adapter_hidden, me, n):
    total, ranks, model_width = adapter_model.shape
    inner_width = adapter_hidden.shape[2]
    inner = jnp.transpose(adapter_hidden, (0, 2, 1))
    if model_width != HEAD_WIDTH or inner_width % 16:
        model = lax.all_to_all(adapter_model, "exp", split_axis=0, concat_axis=2, tiled=True)
        inner = lax.all_to_all(inner, "exp", split_axis=0, concat_axis=1, tiled=True)
        return model[0], inner[0]
    packed = call(
        lora_pack_kernel,
        (shape((ranks + inner_width, HEAD_WIDTH), jnp.bfloat16),) * total,
        [SMEM, VMEM, VMEM],
        me,
        adapter_model,
        inner,
    )
    got = [packed[0]] + [swap(packed[d], n, d) for d in range(1, n)]
    return call(
        lora_join_kernel,
        (
            shape((ranks, n * model_width), jnp.bfloat16),
            shape((n * inner_width, HEAD_WIDTH), jnp.bfloat16),
        ),
        [SMEM] + [VMEM] * n,
        me,
        *got,
    )


def body(
    resid,
    queries,
    incoming_key_value,
    key_value_cache,
    lengths,
    norm_scale_vector,
    expert_choice,
    router_probability,
    gate_weight,
    up_weight,
    down_weight,
    adapter_model,
    adapter_hidden,
):
    n = lax.axis_size("exp")
    me = lax.axis_index("exp").astype(jnp.int32).reshape(1)
    first = stages_of(n)[0][1]

    message = call(
        pack_kernel,
        shape((1,) + MESSAGE, jnp.bfloat16),
        [VMEM] * 4,
        queries,
        incoming_key_value,
        expert_choice,
        router_probability,
    )
    partner = None
    pieces = gather(message, n)
    partner = swap(message, n, 1)
    parts = call(
        functools.partial(attend_kernel, pieces=len(pieces), outs=first),
        split_shapes(n, first, MESSAGE),
        [SMEM, SMEM] + [VMEM] * (len(pieces) + 1),
        lengths,
        me,
        *pieces,
        key_value_cache,
    )
    got = scatter(parts, n, merge_kernel, MESSAGE)
    hidden, normed = call(
        functools.partial(token_kernel, pieces=len(got)),
        (shape(HEADS, jnp.float32), shape((1,) + HEADS, jnp.bfloat16)),
        [SMEM] + [VMEM] * (4 + len(got)),
        me,
        message,
        partner,
        resid,
        norm_scale_vector.reshape(HEADS),
        *got,
    )
    rows = gather(normed, n)
    model, inner = lora(adapter_model, adapter_hidden, me, n)
    outs = call(
        functools.partial(expert_kernel, pieces=len(rows), outs=first),
        split_shapes(n, first, HEADS),
        [SMEM] + [VMEM] * (5 + 2 * len(rows)),
        me,
        gate_weight[0],
        up_weight[0],
        down_weight[0],
        model,
        inner,
        *rows,
        *pieces,
        limit=32,
    )
    return call(
        finish_kernel,
        shape((1, WIDTH), jnp.bfloat16),
        [VMEM] * (1 + len(got)),
        hidden,
        *scatter(outs, n, add_kernel, HEADS),
    )


def solution(mesh):
    return jax.shard_map(
        body,
        mesh=mesh,
        in_specs=(
            P(("grp", "exp"), None),
            P(("grp", "exp"), None),
            P(("grp", "exp"), None),
            P("grp", "exp", None),
            P("grp"),
            P(),
            P(("grp", "exp"), None),
            P(("grp", "exp"), None),
            P("exp", None, None),
            P("exp", None, None),
            P("exp", None, None),
            P(None, None, "exp"),
            P(None, None, "exp"),
        ),
        out_specs=P(("grp", "exp"), None),
        check_vma=False,
    )
```

```python
import functools

import jax
import jax.numpy as jnp
from jax import lax
from jax.experimental import pallas as pl
from jax.experimental.pallas import tpu as pltpu
from jax.sharding import PartitionSpec as P

QUERY_HEADS = 16
KEY_VALUE_HEADS = 2
HEAD_WIDTH = 128
ADAPTER_RANK = 32
GROUPED = QUERY_HEADS // KEY_VALUE_HEADS
KEY_VALUE_WIDTH = KEY_VALUE_HEADS * HEAD_WIDTH
WIDTH = QUERY_HEADS * HEAD_WIDTH
INV_ROOT = HEAD_WIDTH ** (-0.5)
NEAR = 4
HEADS = (QUERY_HEADS, HEAD_WIDTH)
PARTIAL = (2 * QUERY_HEADS, HEAD_WIDTH)
RESID_ROW = QUERY_HEADS
NEW_ROW = 2 * QUERY_HEADS
GATE_ROW = NEW_ROW + 2 * KEY_VALUE_HEADS
MESSAGE = (3 * QUERY_HEADS, HEAD_WIDTH)

floor_score = -1e30
epsilon = 1e-06

VMEM = pl.BlockSpec(memory_space=pltpu.VMEM)
SMEM = pl.BlockSpec(memory_space=pltpu.SMEM)
HBM = pl.BlockSpec(memory_space=pltpu.HBM)
ANY = pl.BlockSpec(memory_space=pl.ANY)
shape = jax.ShapeDtypeStruct


def call(kernel, shapes, specs, *args, limit=8, scratch=()):
    return pl.pallas_call(
        kernel,
        out_shape=shapes,
        in_specs=specs,
        out_specs=jax.tree.map(lambda _: VMEM, shapes),
        scratch_shapes=scratch,
        compiler_params=pltpu.CompilerParams(vmem_limit_bytes=limit * 1024 * 1024),
    )(*args)


def iota(dims, dim):
    return lax.broadcasted_iota(jnp.int32, dims, dim)


def place():
    me = lax.axis_index("exp")
    return me, me % NEAR, me // NEAR


def as_rows(line, rows):
    return jnp.concatenate(
        [line[:, j * HEAD_WIDTH : (j + 1) * HEAD_WIDTH] for j in range(rows)], axis=0
    )


def exchange(value, n, near):
    if near:
        groups = [[z * NEAR + l for l in range(NEAR)] for z in range(n // NEAR)]
    else:
        groups = [[z * NEAR + l for z in range(n // NEAR)] for l in range(NEAR)]
    return lax.all_to_all(
        value, "exp", split_axis=0, concat_axis=0, axis_index_groups=groups, tiled=True
    )


def pack_kernel(query, resid, new, choice, probability, out, q_in, r_in, n_in, c_in, p_in, sems):
    copies = [
        pltpu.make_async_copy(source, target, sems.at[k])
        for k, (source, target) in enumerate(
            ((query, q_in), (resid, r_in), (new, n_in), (choice, c_in), (probability, p_in))
        )
    ]
    for copy in copies:
        copy.start()
    for copy in copies:
        copy.wait()
    q = as_rows(q_in[...].astype(jnp.float32), QUERY_HEADS)
    r = as_rows(r_in[...].astype(jnp.float32), QUERY_HEADS)
    fresh = as_rows(n_in[...].astype(jnp.float32), 2 * KEY_VALUE_HEADS)
    p = p_in[...]
    shares = p / jnp.sum(p, axis=1, keepdims=True)
    lanes = iota((1, HEAD_WIDTH), 1)
    gates = jnp.zeros((1, HEAD_WIDTH), jnp.float32)
    for k in range(p.shape[1]):
        gates = gates + jnp.where(c_in[:, k : k + 1] == lanes, shares[:, k : k + 1], 0.0)
    rest = jnp.zeros((MESSAGE[0] - GATE_ROW - 1, HEAD_WIDTH), jnp.float32)
    message = jnp.concatenate([q, r, fresh, gates, rest], axis=0).astype(jnp.bfloat16)
    for k in range(NEAR):
        out[k] = message


def repeat_kernel(value, out):
    for k in range(out.shape[0]):
        out[k] = value[...]


def encode(top, total, acc):
    lanes = iota(HEADS, 1)
    stats = jnp.zeros(HEADS, jnp.float32)
    for at, value in ((0, top), (3, total)):
        for k in range(3):
            part = value.astype(jnp.bfloat16).astype(jnp.float32)
            stats = jnp.where(lanes == at + k, part, stats)
            value = value - part
    return jnp.concatenate([acc, stats], axis=0).astype(jnp.bfloat16)


def decode(message):
    value = message.astype(jnp.float32)
    acc, stats = value[:QUERY_HEADS], value[QUERY_HEADS:]
    top = stats[:, 0:1] + stats[:, 1:2] + stats[:, 2:3]
    total = stats[:, 3:4] + stats[:, 4:5] + stats[:, 5:6]
    return top, total, acc


def merged(messages, extra=None):
    parts = [decode(message) for message in messages] + ([extra] if extra else [])
    top = functools.reduce(jnp.maximum, [part[0] for part in parts])
    total, acc = 0.0, 0.0
    for peak, amount, value in parts:
        share = jnp.exp(peak - top)
        total = total + share * amount
        acc = acc + share * value
    return top, total, acc


def attend_kernel(lengths, got, cache, parts):
    me, _, _ = place()
    sequences, block, _ = cache.shape
    rows = 2 * QUERY_HEADS
    first_group = (iota((rows, HEAD_WIDTH), 0) % QUERY_HEADS) < GROUPED
    positions = me * block + iota((rows, block), 1)
    for s in range(sequences):
        z, l = 2 * s // NEAR, 2 * s % NEAR
        both = jnp.concatenate([got[z, l, :QUERY_HEADS], got[z, l + 1, :QUERY_HEADS]], axis=0)
        zero = jnp.zeros_like(both)
        wide = jnp.concatenate(
            [jnp.where(first_group, both, zero), jnp.where(first_group, zero, both)], axis=1
        )
        keys = cache[s, :, :KEY_VALUE_WIDTH]
        values = cache[s, :, KEY_VALUE_WIDTH:]
        scores = (
            lax.dot_general(
                wide, keys, (((1,), (1,)), ((), ())), preferred_element_type=jnp.float32
            )
            * INV_ROOT
        )
        valid = positions < lengths[s]
        scores = jnp.where(valid, scores, floor_score)
        top = jnp.max(scores, axis=1, keepdims=True)
        weights = jnp.where(valid, jnp.exp(scores - top), 0.0).astype(jnp.bfloat16)
        total = jnp.sum(weights.astype(jnp.float32), axis=1, keepdims=True)
        acc = jnp.dot(weights, values, preferred_element_type=jnp.float32)
        acc = jnp.where(first_group, acc[:, :HEAD_WIDTH], acc[:, HEAD_WIDTH:])
        for p in range(2):
            cut = slice(p * QUERY_HEADS, (p + 1) * QUERY_HEADS)
            parts[l + p, z] = encode(top[cut], total[cut], acc[cut])


def merge_kernel(got, out):
    for z in range(got.shape[1]):
        value = encode(*merged([got[k, z] for k in range(got.shape[0])]))
        for k in range(out.shape[0]):
            out[k, z] = value


def token_kernel(got, messages, scale, hidden_out, normed_out, hidden_all):
    _, low, high = place()
    first_group = iota(HEADS, 0) < GROUPED
    second = low % 2 == 1

    def by_head(rows, at):
        return jnp.where(first_group, rows[at : at + 1], rows[at + 1 : at + 2])

    for z in range(got.shape[1]):
        message = messages[z, low].astype(jnp.float32)
        q, resid = message[:QUERY_HEADS], message[RESID_ROW:NEW_ROW]
        mine = message[NEW_ROW:GATE_ROW]
        other = messages[z, low ^ 1, NEW_ROW:].astype(jnp.float32)[: GATE_ROW - NEW_ROW]
        own_score = jnp.sum(q * by_head(mine, 0), axis=1, keepdims=True) * INV_ROOT
        other_score = jnp.sum(q * by_head(other, 0), axis=1, keepdims=True) * INV_ROOT
        other_score = jnp.where(second, other_score, floor_score)
        new_max = jnp.maximum(own_score, other_score)
        own_weight = jnp.exp(own_score - new_max).astype(jnp.bfloat16).astype(jnp.float32)
        other_weight = jnp.where(second, jnp.exp(other_score - new_max), 0.0)
        other_weight = other_weight.astype(jnp.bfloat16).astype(jnp.float32)
        new_acc = own_weight * by_head(mine, 2) + other_weight * by_head(other, 2)
        _, total, acc = merged(
            [got[k, z] for k in range(got.shape[0])],
            (new_max, own_weight + other_weight, new_acc),
        )
        hidden = resid + acc / total
        squares = jnp.sum(jnp.sum(hidden * hidden, axis=1, keepdims=True), axis=0, keepdims=True)
        normed = hidden * lax.rsqrt(squares / WIDTH + epsilon) * scale[...]
        hidden_all[z] = hidden
        for k in range(NEAR):
            normed_out[k, z] = normed.astype(jnp.bfloat16)
    hidden_out[...] = hidden_all[high]


def dot_pair(value, factor, contract):
    high = value.astype(jnp.bfloat16)
    low = (value - high.astype(jnp.float32)).astype(jnp.bfloat16)
    both = lax.dot_general(
        jnp.concatenate([high, low], axis=0),
        factor,
        (((1,), (contract,)), ((), ())),
        preferred_element_type=jnp.float32,
    )
    return both[: value.shape[0]] + both[value.shape[0] :]


def expert_kernel(got, messages, gate_w, up_w, down_w, model, inner, parts):
    me, _, _ = place()
    near, far = got.shape[:2]
    tokens = near * far
    x = got[...].astype(jnp.float32).reshape(tokens, WIDTH).astype(jnp.bfloat16)
    r = ADAPTER_RANK
    mixed = lax.dot_general(
        x, model[: 2 * r], (((1,), (1,)), ((), ())), preferred_element_type=jnp.float32
    )
    gate = jnp.dot(x, gate_w[...], preferred_element_type=jnp.float32)
    gate = gate + dot_pair(mixed[:, :r], inner[:, :r], 1)
    up = jnp.dot(x, up_w[...], preferred_element_type=jnp.float32)
    up = up + dot_pair(mixed[:, r:], inner[:, r : 2 * r], 1)
    act = (gate / (1.0 + jnp.exp(-gate)) * up).astype(jnp.bfloat16)
    lowered = jnp.dot(act, inner[:, 2 * r : 3 * r], preferred_element_type=jnp.float32)
    result = jnp.dot(act, down_w[...], preferred_element_type=jnp.float32)
    result = result + dot_pair(lowered, model[2 * r :], 0)
    lanes = iota((1, HEAD_WIDTH), 1)
    for l in range(near):
        for z in range(far):
            slot = l * far + z
            route = messages[z, l, NEW_ROW:].astype(jnp.float32)
            route = route[GATE_ROW - NEW_ROW : GATE_ROW - NEW_ROW + 1]
            share = jnp.sum(jnp.where(lanes == me, route, 0.0), axis=1, keepdims=True)
            line = as_rows(result[slot : slot + 1] * share, QUERY_HEADS)
            parts[l, z] = line.astype(jnp.bfloat16)


def add_kernel(got, out):
    for z in range(got.shape[1]):
        total = sum(got[k, z].astype(jnp.float32) for k in range(got.shape[0]))
        out[z] = total.astype(jnp.bfloat16)


def finish_kernel(hidden, got, out):
    total = hidden[...] + sum(got[k].astype(jnp.float32) for k in range(got.shape[0]))
    line = jnp.concatenate([total[j : j + 1] for j in range(QUERY_HEADS)], axis=1)
    out[...] = line.astype(jnp.bfloat16)


def swap(value, n, distance):
    return lax.ppermute(value, "exp", [(t, t ^ distance) for t in range(n)])


def lora_pack_kernel(after, model, inner, *outs):
    _, low, _ = place()
    ranks = model.shape[1]
    for k, out in enumerate(outs):
        for z in range(out.shape[0]):
            at = z * NEAR + (low ^ k)
            out[z, :ranks] = model[at]
            out[z, ranks:, :ranks] = inner[at]
            out[z, ranks:, ranks:] = jnp.zeros(
                (out.shape[1] - ranks, HEAD_WIDTH - ranks), out.dtype
            )


def lora_turn_kernel(after, *refs):
    _, low, high = place()
    got, outs = refs[:NEAR], refs[NEAR:]
    for j, out in enumerate(outs):
        for k, ref in enumerate(got):
            out[low ^ k] = ref[high ^ j]


def lora_join_kernel(*refs):
    _, _, high = place()
    got, (model, inner) = refs[:-2], refs[-2:]
    ranks = model.shape[0]
    width = inner.shape[0] // (len(got) * NEAR)
    for j, ref in enumerate(got):
        for l in range(NEAR):
            at = (high ^ j) * NEAR + l
            columns = pl.ds(pl.multiple_of(at * HEAD_WIDTH, HEAD_WIDTH), HEAD_WIDTH)
            model[:, columns] = ref[l, :ranks]
            inner[pl.ds(pl.multiple_of(at * width, width), width)] = ref[l, ranks:]


def lora(adapter_model, adapter_hidden, n, after_first, after_second):
    total, ranks, model_width = adapter_model.shape
    inner_width = adapter_hidden.shape[2]
    inner = jnp.transpose(adapter_hidden, (0, 2, 1))
    if model_width != HEAD_WIDTH or inner_width % 16:
        model = lax.all_to_all(adapter_model, "exp", split_axis=0, concat_axis=2, tiled=True)
        inner = lax.all_to_all(inner, "exp", split_axis=0, concat_axis=1, tiled=True)
        return model[0], inner[0]
    far = n // NEAR
    packed = call(
        lora_pack_kernel,
        (shape((far, ranks + inner_width, HEAD_WIDTH), jnp.bfloat16),) * NEAR,
        [ANY, VMEM, VMEM],
        after_first,
        adapter_model,
        inner,
    )
    got = [packed[0]] + [swap(packed[k], n, k) for k in range(1, NEAR)]
    turned = call(
        lora_turn_kernel,
        (shape((NEAR, ranks + inner_width, HEAD_WIDTH), jnp.bfloat16),) * far,
        [ANY] + [VMEM] * NEAR,
        after_second,
        *got,
    )
    got = [turned[0]] + [swap(turned[j], n, j * NEAR) for j in range(1, far)]
    return call(
        lora_join_kernel,
        (
            shape((ranks, n * model_width), jnp.bfloat16),
            shape((n * inner_width, HEAD_WIDTH), jnp.bfloat16),
        ),
        [VMEM] * far,
        *got,
    )


def body(
    resid,
    queries,
    incoming_key_value,
    key_value_cache,
    lengths,
    norm_scale_vector,
    expert_choice,
    router_probability,
    gate_weight,
    up_weight,
    down_weight,
    adapter_model,
    adapter_hidden,
):
    n = lax.axis_size("exp")
    far = n // NEAR
    bf16, f32 = jnp.bfloat16, jnp.float32

    message = call(
        pack_kernel,
        shape((NEAR,) + MESSAGE, bf16),
        [HBM] * 5,
        queries,
        resid,
        incoming_key_value,
        expert_choice,
        router_probability,
        scratch=[
            pltpu.VMEM(queries.shape, bf16),
            pltpu.VMEM(resid.shape, bf16),
            pltpu.VMEM(incoming_key_value.shape, bf16),
            pltpu.VMEM(expert_choice.shape, jnp.int32),
            pltpu.VMEM(router_probability.shape, f32),
            pltpu.SemaphoreType.DMA((5,)),
        ],
    )
    close = exchange(message, n, True)
    close_copies = call(repeat_kernel, shape((far,) + close.shape, bf16), [VMEM], close)
    messages = exchange(close_copies, n, False)
    parts = call(
        attend_kernel,
        shape((NEAR, far) + PARTIAL, bf16),
        [SMEM, VMEM, VMEM],
        lengths,
        messages,
        key_value_cache,
    )
    partial_sums = exchange(parts, n, True)
    merged_copies = call(
        merge_kernel, shape((far, far) + PARTIAL, bf16), [VMEM], partial_sums
    )
    columns = exchange(merged_copies, n, False)
    hidden, normed = call(
        token_kernel,
        (shape(HEADS, f32), shape((NEAR, far) + HEADS, bf16)),
        [VMEM] * 3,
        columns,
        messages,
        norm_scale_vector.reshape(HEADS),
        scratch=[pltpu.VMEM((far,) + HEADS, f32)],
    )
    rows = exchange(normed, n, True)
    model, inner = lora(adapter_model, adapter_hidden, n, close, partial_sums)
    outs = call(
        expert_kernel,
        shape((NEAR, far) + HEADS, bf16),
        [VMEM] * 7,
        rows,
        messages,
        gate_weight[0],
        up_weight[0],
        down_weight[0],
        model,
        inner,
        limit=32,
    )
    sums = call(add_kernel, shape((far,) + HEADS, bf16), [VMEM], exchange(outs, n, True))
    return call(
        finish_kernel,
        shape((1, WIDTH), bf16),
        [VMEM] * 2,
        hidden,
        exchange(sums, n, False),
    )


def solution(mesh):
    return jax.shard_map(
        body,
        mesh=mesh,
        in_specs=(
            P(("grp", "exp"), None),
            P(("grp", "exp"), None),
            P(("grp", "exp"), None),
            P("grp", "exp", None),
            P("grp"),
            P(),
            P(("grp", "exp"), None),
            P(("grp", "exp"), None),
            P("exp", None, None),
            P("exp", None, None),
            P("exp", None, None),
            P(None, None, "exp"),
            P(None, None, "exp"),
        ),
        out_specs=P(("grp", "exp"), None),
        check_vma=False,
    )
```

```python
import functools

import jax
import jax.numpy as jnp
from jax import lax
from jax.experimental import pallas as pl
from jax.experimental.pallas import tpu as pltpu
from jax.sharding import PartitionSpec as P

QUERY_HEADS = 16
KEY_VALUE_HEADS = 2
HEAD_WIDTH = 128
ADAPTER_RANK = 32
GROUPED = QUERY_HEADS // KEY_VALUE_HEADS
KEY_VALUE_WIDTH = KEY_VALUE_HEADS * HEAD_WIDTH
WIDTH = QUERY_HEADS * HEAD_WIDTH
INV_ROOT = HEAD_WIDTH ** (-0.5)
NEAR = 4
NEW_ROWS = 2 * KEY_VALUE_HEADS
HEADS = (QUERY_HEADS, HEAD_WIDTH)
PARTIAL = (2 * QUERY_HEADS, HEAD_WIDTH)
RESID_ROW = QUERY_HEADS
NEW_ROW = 2 * QUERY_HEADS
GATE_ROW = NEW_ROW + NEW_ROWS
MESSAGE = (3 * QUERY_HEADS, HEAD_WIDTH)

floor_score = -1e30
epsilon = 1e-06

VMEM = pl.BlockSpec(memory_space=pltpu.VMEM)
SMEM = pl.BlockSpec(memory_space=pltpu.SMEM)
HBM = pl.BlockSpec(memory_space=pltpu.HBM)
ANY = pl.BlockSpec(memory_space=pl.ANY)
shape = jax.ShapeDtypeStruct
bf16, f32 = jnp.bfloat16, jnp.float32


def call(kernel, shapes, specs, *args, limit=8, scratch=()):
    return pl.pallas_call(
        kernel,
        out_shape=shapes,
        in_specs=specs,
        out_specs=jax.tree.map(lambda _: VMEM, shapes),
        scratch_shapes=scratch,
        compiler_params=pltpu.CompilerParams(vmem_limit_bytes=limit * 1024 * 1024),
    )(*args)


def iota(dims, dim):
    return lax.broadcasted_iota(jnp.int32, dims, dim)


def as_rows(line, rows):
    return jnp.concatenate(
        [line[:, j * HEAD_WIDTH : (j + 1) * HEAD_WIDTH] for j in range(rows)], axis=0
    )


def swap(value, n, distance):
    return lax.ppermute(value, "exp", [(t, t ^ distance) for t in range(n)])


def distance_of(column, far):
    bits = far.bit_length() - 1
    return sum(NEAR << i for i in range(bits) if column >> (bits - 1 - i) & 1)


def pad16(rows):
    return -(-rows // 16) * 16


def pack_kernel(query, resid, new, choice, probability, out, q_in, r_in, n_in, c_in, p_in, sems):
    copies = [
        pltpu.make_async_copy(source, target, sems.at[k])
        for k, (source, target) in enumerate(
            ((query, q_in), (resid, r_in), (new, n_in), (choice, c_in), (probability, p_in))
        )
    ]
    for copy in copies:
        copy.start()
    for copy in copies:
        copy.wait()
    q = as_rows(q_in[...].astype(f32), QUERY_HEADS)
    r = as_rows(r_in[...].astype(f32), QUERY_HEADS)
    fresh = as_rows(n_in[...].astype(f32), NEW_ROWS)
    p = p_in[...]
    shares = p / jnp.sum(p, axis=1, keepdims=True)
    lanes = iota((1, HEAD_WIDTH), 1)
    gates = jnp.zeros((1, HEAD_WIDTH), f32)
    for k in range(p.shape[1]):
        gates = gates + jnp.where(c_in[:, k : k + 1] == lanes, shares[:, k : k + 1], 0.0)
    rest = jnp.zeros((MESSAGE[0] - GATE_ROW - 1, HEAD_WIDTH), f32)
    out[0] = jnp.concatenate([q, r, fresh, gates, rest], axis=0).astype(bf16)


def join_kernel(mine, theirs, out):
    half = mine.shape[0]
    out[:half] = mine[...]
    out[half:] = theirs[...]


def narrow_kernel(mine, theirs, column, out):
    half = mine.shape[0]
    far = 2 * half
    column[:half] = mine[...]
    column[half:] = theirs[...]
    tails = []
    for w in range(far):
        source, at = (mine, w) if w < half else (theirs, w - half)
        out[w * QUERY_HEADS : (w + 1) * QUERY_HEADS] = source[at, :QUERY_HEADS]
        tails.append(source[at, NEW_ROW:].astype(f32))
    fresh = jnp.concatenate([tail[:NEW_ROWS] for tail in tails], axis=0)
    gates = jnp.concatenate([tail[NEW_ROWS : NEW_ROWS + 1] for tail in tails], axis=0)
    for rows, at in ((gates, far * QUERY_HEADS), (fresh, far * QUERY_HEADS + pad16(far))):
        extra = pad16(rows.shape[0]) - rows.shape[0]
        if extra:
            rows = jnp.concatenate([rows, jnp.zeros((extra, HEAD_WIDTH), f32)], axis=0)
        out[at : at + rows.shape[0]] = rows.astype(bf16)


def encode(top, total, acc):
    lanes = iota(HEADS, 1)
    stats = jnp.zeros(HEADS, f32)
    for at, value in ((0, top), (3, total)):
        for k in range(3):
            part = value.astype(bf16).astype(f32)
            stats = jnp.where(lanes == at + k, part, stats)
            value = value - part
    return jnp.concatenate([acc, stats], axis=0).astype(bf16)


def decode(message):
    value = message.astype(f32)
    acc, stats = value[:QUERY_HEADS], value[QUERY_HEADS:]
    top = stats[:, 0:1] + stats[:, 1:2] + stats[:, 2:3]
    total = stats[:, 3:4] + stats[:, 4:5] + stats[:, 5:6]
    return top, total, acc


def merged(parts):
    top = functools.reduce(jnp.maximum, [part[0] for part in parts])
    total, acc = 0.0, 0.0
    for peak, amount, value in parts:
        share = jnp.exp(peak - top)
        total = total + share * amount
        acc = acc + share * value
    return top, total, acc


def attend_kernel(lengths, mine, theirs, cache, keep, send, *, far):
    me = lax.axis_index("exp")
    sequences, block, _ = cache.shape
    rows = 2 * QUERY_HEADS
    first_group = (iota((rows, HEAD_WIDTH), 0) % QUERY_HEADS) < GROUPED
    positions = me * block + iota((rows, block), 1)
    for y in range(2):
        for w in range(far):
            s = lax.shift_right_logical(me, 1) ^ ((distance_of(w, far) >> 1) | y)
            cut = slice(w * QUERY_HEADS, (w + 1) * QUERY_HEADS)
            both = jnp.concatenate([mine[y, cut], theirs[y, cut]], axis=0)
            zero = jnp.zeros_like(both)
            wide = jnp.concatenate(
                [jnp.where(first_group, both, zero), jnp.where(first_group, zero, both)], axis=1
            )
            keys = cache[s, :, :KEY_VALUE_WIDTH]
            values = cache[s, :, KEY_VALUE_WIDTH:]
            scores = (
                lax.dot_general(
                    wide, keys, (((1,), (1,)), ((), ())), preferred_element_type=f32
                )
                * INV_ROOT
            )
            valid = positions < lengths[s]
            scores = jnp.where(valid, scores, floor_score)
            top = jnp.max(scores, axis=1, keepdims=True)
            weights = jnp.where(valid, jnp.exp(scores - top), 0.0).astype(bf16)
            total = jnp.sum(weights.astype(f32), axis=1, keepdims=True)
            acc = jnp.dot(weights, values, preferred_element_type=f32)
            acc = jnp.where(first_group, acc[:, :HEAD_WIDTH], acc[:, HEAD_WIDTH:])
            for part, cut in (
                (keep, slice(0, QUERY_HEADS)),
                (send, slice(QUERY_HEADS, 2 * QUERY_HEADS)),
            ):
                part[y * far + w] = encode(top[cut], total[cut], acc[cut])


def merge_kernel(mine, theirs, *outs, flip):
    count = mine.shape[0] // len(outs)
    for slot in range(mine.shape[0]):
        parts = [decode(mine[slot]), decode(theirs[slot ^ flip])]
        outs[slot // count][slot % count] = encode(*merged(parts))


def token_kernel(mine, theirs, column, near, scale, hidden_out, normed_out):
    second = lax.axis_index("exp") % 2 == 1
    first_group = iota(HEADS, 0) < GROUPED
    far = column.shape[0]
    near_at = far * QUERY_HEADS + pad16(far)
    others = near[0, near_at:].astype(f32)

    def by_head(rows, at):
        return jnp.where(first_group, rows[at : at + 1], rows[at + 1 : at + 2])

    for w in range(far):
        message = column[w].astype(f32)
        q, resid, new = message[:QUERY_HEADS], message[RESID_ROW:NEW_ROW], message[NEW_ROW:GATE_ROW]
        other = others[w * NEW_ROWS : (w + 1) * NEW_ROWS]
        own_score = jnp.sum(q * by_head(new, 0), axis=1, keepdims=True) * INV_ROOT
        other_score = jnp.sum(q * by_head(other, 0), axis=1, keepdims=True) * INV_ROOT
        other_score = jnp.where(second, other_score, floor_score)
        new_max = jnp.maximum(own_score, other_score)
        own_weight = jnp.exp(own_score - new_max).astype(bf16).astype(f32)
        other_weight = jnp.where(second, jnp.exp(other_score - new_max), 0.0)
        other_weight = other_weight.astype(bf16).astype(f32)
        fresh = own_weight * by_head(new, 2) + other_weight * by_head(other, 2)
        _, total, acc = merged(
            [
                decode(mine[w]),
                decode(theirs[w ^ 1]),
                (new_max, own_weight + other_weight, fresh),
            ]
        )
        hidden = resid + acc / total
        squares = jnp.sum(jnp.sum(hidden * hidden, axis=1, keepdims=True), axis=0, keepdims=True)
        normed = hidden * lax.rsqrt(squares / WIDTH + epsilon) * scale[...]
        if w == 0:
            hidden_out[...] = hidden
        normed_out[w] = normed.astype(bf16)


def dot_pair(value, factor, contract):
    high = value.astype(bf16)
    low = (value - high.astype(f32)).astype(bf16)
    both = lax.dot_general(
        jnp.concatenate([high, low], axis=0),
        factor,
        (((1,), (contract,)), ((), ())),
        preferred_element_type=f32,
    )
    return both[: value.shape[0]] + both[value.shape[0] :]


def expert_kernel(
    mine, theirs, near, next_near, gate_w, up_w, down_w, model, inner, keep, send, *, far
):
    me = lax.axis_index("exp")
    half = mine.shape[0]
    x = jnp.concatenate([mine[...].astype(f32), theirs[...].astype(f32)], axis=0)
    x = x.reshape(2 * half, WIDTH).astype(bf16)
    r = ADAPTER_RANK
    mixed = lax.dot_general(
        x, model[: 2 * r], (((1,), (1,)), ((), ())), preferred_element_type=f32
    )
    gate = jnp.dot(x, gate_w[...], preferred_element_type=f32)
    gate = gate + dot_pair(mixed[:, :r], inner[:, :r], 1)
    up = jnp.dot(x, up_w[...], preferred_element_type=f32)
    up = up + dot_pair(mixed[:, r:], inner[:, r : 2 * r], 1)
    act = (gate / (1.0 + jnp.exp(-gate)) * up).astype(bf16)
    lowered = jnp.dot(act, inner[:, 2 * r : 3 * r], preferred_element_type=f32)
    result = jnp.dot(act, down_w[...], preferred_element_type=f32)
    result = result + dot_pair(lowered, model[2 * r :], 0)
    lanes = iota((pad16(far), HEAD_WIDTH), 1)
    gate_at = far * QUERY_HEADS
    for c, (routes, part) in enumerate(((near, keep), (next_near, send))):
        for y in range(2):
            route = routes[y, gate_at : gate_at + pad16(far)].astype(f32)
            share = jnp.sum(jnp.where(lanes == me, route, 0.0), axis=1, keepdims=True)
            for w in range(far):
                slot = y * far + w
                line = result[c * half + slot : c * half + slot + 1] * share[w : w + 1]
                part[slot] = as_rows(line, QUERY_HEADS).astype(bf16)


def add_kernel(mine, theirs, keep, send):
    half = keep.shape[0]
    for out, at in ((keep, 0), (send, half)):
        total = mine[at : at + half].astype(f32) + theirs[at : at + half].astype(f32)
        out[...] = total.astype(bf16)


def finish_kernel(hidden, mine, theirs, out):
    total = hidden[...] + mine[0].astype(f32) + theirs[0].astype(f32)
    line = jnp.concatenate([total[j : j + 1] for j in range(QUERY_HEADS)], axis=1)
    out[...] = line.astype(bf16)


def lora_pack_kernel(after, model, inner, *outs):
    low = lax.axis_index("exp") % NEAR
    ranks = model.shape[1]
    for k, out in enumerate(outs):
        for z in range(out.shape[0]):
            at = z * NEAR + (low ^ k)
            out[z, :ranks] = model[at]
            out[z, ranks:, :ranks] = inner[at]
            out[z, ranks:, ranks:] = jnp.zeros(
                (out.shape[1] - ranks, HEAD_WIDTH - ranks), out.dtype
            )


def lora_turn_kernel(after, *refs):
    me = lax.axis_index("exp")
    low, high = me % NEAR, me // NEAR
    got, outs = refs[:NEAR], refs[NEAR:]
    for j, out in enumerate(outs):
        for k, ref in enumerate(got):
            out[low ^ k] = ref[high ^ j]


def lora_join_kernel(*refs):
    high = lax.axis_index("exp") // NEAR
    got, (model, inner) = refs[:-2], refs[-2:]
    ranks = model.shape[0]
    width = inner.shape[0] // (len(got) * NEAR)
    for j, ref in enumerate(got):
        for l in range(NEAR):
            at = (high ^ j) * NEAR + l
            columns = pl.ds(pl.multiple_of(at * HEAD_WIDTH, HEAD_WIDTH), HEAD_WIDTH)
            model[:, columns] = ref[l, :ranks]
            inner[pl.ds(pl.multiple_of(at * width, width), width)] = ref[l, ranks:]


def lora(adapter_model, adapter_hidden, n, after_first, after_second):
    total, ranks, model_width = adapter_model.shape
    inner_width = adapter_hidden.shape[2]
    inner = jnp.transpose(adapter_hidden, (0, 2, 1))
    if model_width != HEAD_WIDTH or inner_width % 16:
        model = lax.all_to_all(adapter_model, "exp", split_axis=0, concat_axis=2, tiled=True)
        inner = lax.all_to_all(inner, "exp", split_axis=0, concat_axis=1, tiled=True)
        return model[0], inner[0]
    far = n // NEAR
    packed = call(
        lora_pack_kernel,
        (shape((far, ranks + inner_width, HEAD_WIDTH), bf16),) * NEAR,
        [ANY, VMEM, VMEM],
        after_first,
        adapter_model,
        inner,
    )
    got = [packed[0]] + [swap(packed[k], n, k) for k in range(1, NEAR)]
    turned = call(
        lora_turn_kernel,
        (shape((NEAR, ranks + inner_width, HEAD_WIDTH), bf16),) * far,
        [ANY] + [VMEM] * NEAR,
        after_second,
        *got,
    )
    got = [turned[0]] + [swap(turned[j], n, j * NEAR) for j in range(1, far)]
    return call(
        lora_join_kernel,
        (
            shape((ranks, n * model_width), bf16),
            shape((n * inner_width, HEAD_WIDTH), bf16),
        ),
        [VMEM] * far,
        *got,
    )


def body(
    resid,
    queries,
    incoming_key_value,
    key_value_cache,
    lengths,
    norm_scale_vector,
    expert_choice,
    router_probability,
    gate_weight,
    up_weight,
    down_weight,
    adapter_model,
    adapter_hidden,
):
    n = lax.axis_size("exp")
    far = n // NEAR

    first_inputs = (queries, resid, incoming_key_value, expert_choice, router_probability)
    message = call(
        pack_kernel,
        shape((1,) + MESSAGE, bf16),
        [HBM] * 5,
        *[pltpu.with_memory_space_constraint(x, pltpu.HBM) for x in first_inputs],
        scratch=[pltpu.VMEM(x.shape, x.dtype) for x in first_inputs]
        + [pltpu.SemaphoreType.DMA((5,))],
    )
    distance, first_join = n // 2, message
    while distance > NEAR:
        message = call(
            join_kernel,
            shape((2 * message.shape[0],) + MESSAGE, bf16),
            [VMEM] * 2,
            message,
            swap(message, n, distance),
        )
        distance //= 2
    near_rows = far * QUERY_HEADS + pad16(far) + pad16(NEW_ROWS * far)
    column, narrow = call(
        narrow_kernel,
        (shape((far,) + MESSAGE, bf16), shape((near_rows, HEAD_WIDTH), bf16)),
        [VMEM] * 2,
        message,
        swap(message, n, NEAR),
    )
    narrow = narrow[None]
    near = call(
        join_kernel,
        shape((2, near_rows, HEAD_WIDTH), bf16),
        [VMEM] * 2,
        narrow,
        swap(narrow, n, 2),
    )
    next_near = swap(near, n, 1)
    keep, send = call(
        functools.partial(attend_kernel, far=far),
        (shape((2 * far,) + PARTIAL, bf16),) * 2,
        [SMEM] + [VMEM] * 3,
        lengths,
        near,
        next_near,
        key_value_cache,
    )
    first_part = keep
    keep, send = call(
        functools.partial(merge_kernel, flip=0),
        (shape((far,) + PARTIAL, bf16),) * 2,
        [VMEM] * 2,
        keep,
        swap(send, n, 1),
    )
    theirs, distance, flip = swap(send, n, 2), NEAR, 0
    while distance < n:
        keep = call(
            functools.partial(merge_kernel, flip=flip),
            shape((far,) + PARTIAL, bf16),
            [VMEM] * 2,
            keep,
            theirs,
        )
        theirs = swap(keep, n, distance)
        flip = far * NEAR // (2 * distance)
        distance *= 2
    hidden, normed = call(
        token_kernel,
        (shape(HEADS, f32), shape((far,) + HEADS, bf16)),
        [VMEM] * 5,
        keep,
        theirs,
        column,
        next_near,
        norm_scale_vector.reshape(HEADS),
    )
    rows = call(
        join_kernel, shape((2 * far,) + HEADS, bf16), [VMEM] * 2, normed, swap(normed, n, 2)
    )
    next_rows = swap(rows, n, 1)
    model, inner = lora(adapter_model, adapter_hidden, n, near, first_part)
    keep, send = call(
        functools.partial(expert_kernel, far=far),
        (shape((2 * far,) + HEADS, bf16),) * 2,
        [VMEM] * 9,
        rows,
        next_rows,
        near,
        next_near,
        gate_weight[0],
        up_weight[0],
        down_weight[0],
        model,
        inner,
        limit=32,
    )
    distance = 1
    while distance < n // 2:
        keep, send = call(
            add_kernel,
            (shape((keep.shape[0] // 2,) + HEADS, bf16),) * 2,
            [VMEM] * 2,
            keep,
            swap(send, n, distance),
        )
        distance *= 2
    return call(
        finish_kernel,
        shape((1, WIDTH), bf16),
        [VMEM] * 3,
        hidden,
        keep,
        swap(send, n, distance),
    )


def solution(mesh):
    return jax.shard_map(
        body,
        mesh=mesh,
        in_specs=(
            P(("grp", "exp"), None),
            P(("grp", "exp"), None),
            P(("grp", "exp"), None),
            P("grp", "exp", None),
            P("grp"),
            P(),
            P(("grp", "exp"), None),
            P(("grp", "exp"), None),
            P("exp", None, None),
            P("exp", None, None),
            P("exp", None, None),
            P(None, None, "exp"),
            P(None, None, "exp"),
        ),
        out_specs=P(("grp", "exp"), None),
        check_vma=False,
    )
```

```python
import functools

import jax
import jax.numpy as jnp
from jax import lax
from jax.experimental import pallas as pl
from jax.experimental.pallas import tpu as pltpu
from jax.sharding import PartitionSpec as P

QUERY_HEADS = 16
KEY_VALUE_HEADS = 2
HEAD_WIDTH = 128
ADAPTER_RANK = 32
GROUPED = QUERY_HEADS // KEY_VALUE_HEADS
KEY_VALUE_WIDTH = KEY_VALUE_HEADS * HEAD_WIDTH
WIDTH = QUERY_HEADS * HEAD_WIDTH
INV_ROOT = HEAD_WIDTH ** (-0.5)
NEAR = 4
NEW_ROWS = 2 * KEY_VALUE_HEADS
HEADS = (QUERY_HEADS, HEAD_WIDTH)
PARTIAL = (2 * QUERY_HEADS, HEAD_WIDTH)
RESID_ROW = QUERY_HEADS
NEW_ROW = 2 * QUERY_HEADS
GATE_ROW = NEW_ROW + NEW_ROWS
MESSAGE = (3 * QUERY_HEADS, HEAD_WIDTH)

floor_score = -1e30
epsilon = 1e-06

VMEM = pl.BlockSpec(memory_space=pltpu.VMEM)
SMEM = pl.BlockSpec(memory_space=pltpu.SMEM)
HBM = pl.BlockSpec(memory_space=pltpu.HBM)
ANY = pl.BlockSpec(memory_space=pl.ANY)
shape = jax.ShapeDtypeStruct
bf16, f32 = jnp.bfloat16, jnp.float32


def call(kernel, shapes, specs, *args, limit=8, scratch=(), nanos=50):
    return pl.pallas_call(
        kernel,
        out_shape=shapes,
        in_specs=specs,
        out_specs=jax.tree.map(lambda _: VMEM, shapes),
        scratch_shapes=scratch,
        cost_estimate=pl.CostEstimate(
            flops=nanos * 1000000, transcendentals=0, bytes_accessed=0
        ),
        compiler_params=pltpu.CompilerParams(vmem_limit_bytes=limit * 1024 * 1024),
    )(*args)


def hold_kernel(value, after, out):
    pass


def hold(value, after):
    return pl.pallas_call(
        hold_kernel,
        out_shape=shape(value.shape, value.dtype),
        in_specs=[ANY, ANY],
        out_specs=ANY,
        input_output_aliases={0: 0},
    )(value, after)


def iota(dims, dim):
    return lax.broadcasted_iota(jnp.int32, dims, dim)


def as_rows(line, rows):
    return jnp.concatenate(
        [line[:, j * HEAD_WIDTH : (j + 1) * HEAD_WIDTH] for j in range(rows)], axis=0
    )


def swap(value, n, distance):
    return lax.ppermute(value, "exp", [(t, t ^ distance) for t in range(n)])


def distance_of(column, far):
    bits = far.bit_length() - 1
    return sum(NEAR << i for i in range(bits) if column >> (bits - 1 - i) & 1)


def pad16(rows):
    return -(-rows // 16) * 16


def pack_kernel(query, resid, new, choice, probability, out, q_in, r_in, n_in, c_in, p_in, sems):
    copies = [
        pltpu.make_async_copy(source, target, sems.at[k])
        for k, (source, target) in enumerate(
            ((query, q_in), (resid, r_in), (new, n_in), (choice, c_in), (probability, p_in))
        )
    ]
    for copy in copies:
        copy.start()
    for copy in copies:
        copy.wait()
    q = as_rows(q_in[...].astype(f32), QUERY_HEADS)
    r = as_rows(r_in[...].astype(f32), QUERY_HEADS)
    fresh = as_rows(n_in[...].astype(f32), NEW_ROWS)
    p = p_in[...]
    shares = p / jnp.sum(p, axis=1, keepdims=True)
    lanes = iota((1, HEAD_WIDTH), 1)
    gates = jnp.zeros((1, HEAD_WIDTH), f32)
    for k in range(p.shape[1]):
        gates = gates + jnp.where(c_in[:, k : k + 1] == lanes, shares[:, k : k + 1], 0.0)
    rest = jnp.zeros((MESSAGE[0] - GATE_ROW - 1, HEAD_WIDTH), f32)
    out[0] = jnp.concatenate([q, r, fresh, gates, rest], axis=0).astype(bf16)


def join_kernel(mine, theirs, out):
    half = mine.shape[0]
    out[:half] = mine[...]
    out[half:] = theirs[...]


def narrow_kernel(mine, theirs, column, out):
    half = mine.shape[0]
    far = 2 * half
    column[:half] = mine[...]
    column[half:] = theirs[...]
    tails = []
    for w in range(far):
        source, at = (mine, w) if w < half else (theirs, w - half)
        out[w * QUERY_HEADS : (w + 1) * QUERY_HEADS] = source[at, :QUERY_HEADS]
        tails.append(source[at, NEW_ROW:].astype(f32))
    fresh = jnp.concatenate([tail[:NEW_ROWS] for tail in tails], axis=0)
    gates = jnp.concatenate([tail[NEW_ROWS : NEW_ROWS + 1] for tail in tails], axis=0)
    for rows, at in ((gates, far * QUERY_HEADS), (fresh, far * QUERY_HEADS + pad16(far))):
        extra = pad16(rows.shape[0]) - rows.shape[0]
        if extra:
            rows = jnp.concatenate([rows, jnp.zeros((extra, HEAD_WIDTH), f32)], axis=0)
        out[at : at + rows.shape[0]] = rows.astype(bf16)


def encode(top, total, acc):
    lanes = iota(HEADS, 1)
    stats = jnp.zeros(HEADS, f32)
    for at, value in ((0, top), (3, total)):
        for k in range(3):
            part = value.astype(bf16).astype(f32)
            stats = jnp.where(lanes == at + k, part, stats)
            value = value - part
    return jnp.concatenate([acc, stats], axis=0).astype(bf16)


def decode(message):
    value = message.astype(f32)
    acc, stats = value[:QUERY_HEADS], value[QUERY_HEADS:]
    top = stats[:, 0:1] + stats[:, 1:2] + stats[:, 2:3]
    total = stats[:, 3:4] + stats[:, 4:5] + stats[:, 5:6]
    return top, total, acc


def merged(parts):
    top = functools.reduce(jnp.maximum, [part[0] for part in parts])
    total, acc = 0.0, 0.0
    for peak, amount, value in parts:
        share = jnp.exp(peak - top)
        total = total + share * amount
        acc = acc + share * value
    return top, total, acc


def attend_kernel(after, lengths, mine, theirs, cache, keep, send, *, far):
    me = lax.axis_index("exp")
    sequences, block, _ = cache.shape
    rows = 2 * QUERY_HEADS
    first_group = (iota((rows, HEAD_WIDTH), 0) % QUERY_HEADS) < GROUPED
    positions = me * block + iota((rows, block), 1)
    for y in range(2):
        for w in range(far):
            s = lax.shift_right_logical(me, 1) ^ ((distance_of(w, far) >> 1) | y)
            cut = slice(w * QUERY_HEADS, (w + 1) * QUERY_HEADS)
            both = jnp.concatenate([mine[y, cut], theirs[y, cut]], axis=0)
            zero = jnp.zeros_like(both)
            wide = jnp.concatenate(
                [jnp.where(first_group, both, zero), jnp.where(first_group, zero, both)], axis=1
            )
            keys = cache[s, :, :KEY_VALUE_WIDTH]
            values = cache[s, :, KEY_VALUE_WIDTH:]
            scores = (
                lax.dot_general(
                    wide, keys, (((1,), (1,)), ((), ())), preferred_element_type=f32
                )
                * INV_ROOT
            )
            valid = positions < lengths[s]
            scores = jnp.where(valid, scores, floor_score)
            top = jnp.max(scores, axis=1, keepdims=True)
            weights = jnp.where(valid, jnp.exp(scores - top), 0.0).astype(bf16)
            total = jnp.sum(weights.astype(f32), axis=1, keepdims=True)
            acc = jnp.dot(weights, values, preferred_element_type=f32)
            acc = jnp.where(first_group, acc[:, :HEAD_WIDTH], acc[:, HEAD_WIDTH:])
            for part, cut in (
                (keep, slice(0, QUERY_HEADS)),
                (send, slice(QUERY_HEADS, 2 * QUERY_HEADS)),
            ):
                part[y * far + w] = encode(top[cut], total[cut], acc[cut])


def merge_kernel(mine, theirs, *outs, flip):
    count = mine.shape[0] // len(outs)
    for slot in range(mine.shape[0]):
        parts = [decode(mine[slot]), decode(theirs[slot ^ flip])]
        outs[slot // count][slot % count] = encode(*merged(parts))


def token_kernel(mine, theirs, column, near, scale, hidden_out, normed_out):
    second = lax.axis_index("exp") % 2 == 1
    first_group = iota(HEADS, 0) < GROUPED
    far = column.shape[0]
    near_at = far * QUERY_HEADS + pad16(far)
    others = near[0, near_at:].astype(f32)

    def by_head(rows, at):
        return jnp.where(first_group, rows[at : at + 1], rows[at + 1 : at + 2])

    for w in range(far):
        message = column[w].astype(f32)
        q, resid, new = message[:QUERY_HEADS], message[RESID_ROW:NEW_ROW], message[NEW_ROW:GATE_ROW]
        other = others[w * NEW_ROWS : (w + 1) * NEW_ROWS]
        own_score = jnp.sum(q * by_head(new, 0), axis=1, keepdims=True) * INV_ROOT
        other_score = jnp.sum(q * by_head(other, 0), axis=1, keepdims=True) * INV_ROOT
        other_score = jnp.where(second, other_score, floor_score)
        new_max = jnp.maximum(own_score, other_score)
        own_weight = jnp.exp(own_score - new_max).astype(bf16).astype(f32)
        other_weight = jnp.where(second, jnp.exp(other_score - new_max), 0.0)
        other_weight = other_weight.astype(bf16).astype(f32)
        fresh = own_weight * by_head(new, 2) + other_weight * by_head(other, 2)
        _, total, acc = merged(
            [
                decode(mine[w]),
                decode(theirs[w ^ 1]),
                (new_max, own_weight + other_weight, fresh),
            ]
        )
        hidden = resid + acc / total
        squares = jnp.sum(jnp.sum(hidden * hidden, axis=1, keepdims=True), axis=0, keepdims=True)
        normed = hidden * lax.rsqrt(squares / WIDTH + epsilon) * scale[...]
        if w == 0:
            hidden_out[...] = hidden
        normed_out[w] = normed.astype(bf16)


def dot_pair(value, factor, contract):
    high = value.astype(bf16)
    low = (value - high.astype(f32)).astype(bf16)
    both = lax.dot_general(
        jnp.concatenate([high, low], axis=0),
        factor,
        (((1,), (contract,)), ((), ())),
        preferred_element_type=f32,
    )
    return both[: value.shape[0]] + both[value.shape[0] :]


def expert_kernel(
    mine, theirs, near, next_near, gate_w, up_w, down_w, model, inner, keep, send, *, far
):
    me = lax.axis_index("exp")
    half = mine.shape[0]
    x = jnp.concatenate([mine[...].astype(f32), theirs[...].astype(f32)], axis=0)
    x = x.reshape(2 * half, WIDTH).astype(bf16)
    r = ADAPTER_RANK
    mixed = lax.dot_general(
        x, model[: 2 * r], (((1,), (1,)), ((), ())), preferred_element_type=f32
    )
    gate = jnp.dot(x, gate_w[...], preferred_element_type=f32)
    gate = gate + dot_pair(mixed[:, :r], inner[:, :r], 1)
    up = jnp.dot(x, up_w[...], preferred_element_type=f32)
    up = up + dot_pair(mixed[:, r:], inner[:, r : 2 * r], 1)
    act = (gate / (1.0 + jnp.exp(-gate)) * up).astype(bf16)
    lowered = jnp.dot(act, inner[:, 2 * r : 3 * r], preferred_element_type=f32)
    result = jnp.dot(act, down_w[...], preferred_element_type=f32)
    result = result + dot_pair(lowered, model[2 * r :], 0)
    lanes = iota((pad16(far), HEAD_WIDTH), 1)
    gate_at = far * QUERY_HEADS
    for c, (routes, part) in enumerate(((near, keep), (next_near, send))):
        for y in range(2):
            route = routes[y, gate_at : gate_at + pad16(far)].astype(f32)
            share = jnp.sum(jnp.where(lanes == me, route, 0.0), axis=1, keepdims=True)
            for w in range(far):
                slot = y * far + w
                line = result[c * half + slot : c * half + slot + 1] * share[w : w + 1]
                part[slot] = as_rows(line, QUERY_HEADS).astype(bf16)


def add_kernel(mine, theirs, keep, send):
    half = keep.shape[0]
    for out, at in ((keep, 0), (send, half)):
        total = mine[at : at + half].astype(f32) + theirs[at : at + half].astype(f32)
        out[...] = total.astype(bf16)


def finish_kernel(hidden, mine, theirs, out):
    total = hidden[...] + mine[0].astype(f32) + theirs[0].astype(f32)
    line = jnp.concatenate([total[j : j + 1] for j in range(QUERY_HEADS)], axis=1)
    out[...] = line.astype(bf16)


def lora_pack_kernel(after, model, inner, *outs):
    low = lax.axis_index("exp") % NEAR
    ranks = model.shape[1]
    for k, out in enumerate(outs):
        for z in range(out.shape[0]):
            at = z * NEAR + (low ^ k)
            out[z, :ranks] = model[at]
            out[z, ranks:, :ranks] = inner[at]
            out[z, ranks:, ranks:] = jnp.zeros(
                (out.shape[1] - ranks, HEAD_WIDTH - ranks), out.dtype
            )


def lora_turn_kernel(after, *refs):
    me = lax.axis_index("exp")
    low, high = me % NEAR, me // NEAR
    got, outs = refs[:NEAR], refs[NEAR:]
    for j, out in enumerate(outs):
        for k, ref in enumerate(got):
            out[low ^ k] = ref[high ^ j]


def lora_join_kernel(*refs):
    high = lax.axis_index("exp") // NEAR
    got, (model, inner) = refs[:-2], refs[-2:]
    ranks = model.shape[0]
    width = inner.shape[0] // (len(got) * NEAR)
    for j, ref in enumerate(got):
        for l in range(NEAR):
            at = (high ^ j) * NEAR + l
            columns = pl.ds(pl.multiple_of(at * HEAD_WIDTH, HEAD_WIDTH), HEAD_WIDTH)
            model[:, columns] = ref[l, :ranks]
            inner[pl.ds(pl.multiple_of(at * width, width), width)] = ref[l, ranks:]


def lora_near(adapter_model, adapter_hidden, n, marks):
    total, ranks, model_width = adapter_model.shape
    inner_width = adapter_hidden.shape[2]
    inner = jnp.transpose(adapter_hidden, (0, 2, 1))
    if model_width != HEAD_WIDTH or inner_width % 16:
        model = lax.all_to_all(adapter_model, "exp", split_axis=0, concat_axis=2, tiled=True)
        inner = lax.all_to_all(inner, "exp", split_axis=0, concat_axis=1, tiled=True)
        return [model[0], inner[0]], True
    far = n // NEAR
    packed = call(
        lora_pack_kernel,
        (shape((far, ranks + inner_width, HEAD_WIDTH), bf16),) * NEAR,
        [ANY, VMEM, VMEM],
        marks[0],
        adapter_model,
        inner,
    )
    got = [packed[0]]
    for k in range(1, NEAR):
        got.append(swap(hold(packed[k], marks[1 + k // 3]), n, k))
    turned = call(
        lora_turn_kernel,
        (shape((NEAR, ranks + inner_width, HEAD_WIDTH), bf16),) * far,
        [ANY] + [VMEM] * NEAR,
        marks[3],
        *got,
    )
    return turned, False


def lora_far(turned, n, marks):
    far = len(turned)
    rows = turned[0].shape[1]
    ranks = 3 * ADAPTER_RANK
    got = [turned[0]]
    for j in range(1, far):
        got.append(swap(hold(turned[j], marks[min(j - 1, len(marks) - 1)]), n, j * NEAR))
    return call(
        lora_join_kernel,
        (shape((ranks, n * HEAD_WIDTH), bf16), shape((n * (rows - ranks), HEAD_WIDTH), bf16)),
        [VMEM] * far,
        *got,
    )


def body(
    resid,
    queries,
    incoming_key_value,
    key_value_cache,
    lengths,
    norm_scale_vector,
    expert_choice,
    router_probability,
    gate_weight,
    up_weight,
    down_weight,
    adapter_model,
    adapter_hidden,
):
    n = lax.axis_size("exp")
    far = n // NEAR

    first_inputs = (queries, resid, incoming_key_value, expert_choice, router_probability)
    message = call(
        pack_kernel,
        shape((1,) + MESSAGE, bf16),
        [HBM] * 5,
        *[pltpu.with_memory_space_constraint(x, pltpu.HBM) for x in first_inputs],
        scratch=[pltpu.VMEM(x.shape, x.dtype) for x in first_inputs]
        + [pltpu.SemaphoreType.DMA((5,))],
        nanos=4000,
    )
    marks, distance = [message], n // 2
    while distance > NEAR:
        message = call(
            join_kernel,
            shape((2 * message.shape[0],) + MESSAGE, bf16),
            [VMEM] * 2,
            message,
            swap(message, n, distance),
        )
        distance //= 2
    near_rows = far * QUERY_HEADS + pad16(far) + pad16(NEW_ROWS * far)
    column, narrow = call(
        narrow_kernel,
        (shape((far,) + MESSAGE, bf16), shape((near_rows, HEAD_WIDTH), bf16)),
        [VMEM] * 2,
        message,
        swap(message, n, NEAR),
    )
    marks += [message, column]
    narrow = narrow[None]
    near = call(
        join_kernel,
        shape((2, near_rows, HEAD_WIDTH), bf16),
        [VMEM] * 2,
        narrow,
        swap(narrow, n, 2),
    )
    marks.append(near)
    turned, whole = lora_near(adapter_model, adapter_hidden, n, marks)
    next_near = swap(near, n, 1)
    keep, send = call(
        functools.partial(attend_kernel, far=far),
        (shape((2 * far,) + PARTIAL, bf16),) * 2,
        [ANY, SMEM] + [VMEM] * 3,
        turned[0],
        lengths,
        near,
        next_near,
        key_value_cache,
        nanos=8000,
    )
    marks = [keep]
    keep, send = call(
        functools.partial(merge_kernel, flip=0),
        (shape((far,) + PARTIAL, bf16),) * 2,
        [VMEM] * 2,
        keep,
        swap(send, n, 1),
    )
    marks.append(keep)
    theirs, distance, flip = swap(send, n, 2), NEAR, 0
    while distance < n:
        keep = call(
            functools.partial(merge_kernel, flip=flip),
            shape((far,) + PARTIAL, bf16),
            [VMEM] * 2,
            keep,
            theirs,
        )
        marks.append(keep)
        theirs = swap(keep, n, distance)
        flip = far * NEAR // (2 * distance)
        distance *= 2
    hidden, normed = call(
        token_kernel,
        (shape(HEADS, f32), shape((far,) + HEADS, bf16)),
        [VMEM] * 5,
        keep,
        theirs,
        column,
        next_near,
        norm_scale_vector.reshape(HEADS),
    )
    rows = call(
        join_kernel, shape((2 * far,) + HEADS, bf16), [VMEM] * 2, normed, swap(normed, n, 2)
    )
    next_rows = swap(rows, n, 1)
    model, inner = turned if whole else lora_far(turned, n, marks)
    keep, send = call(
        functools.partial(expert_kernel, far=far),
        (shape((2 * far,) + HEADS, bf16),) * 2,
        [VMEM] * 9,
        rows,
        next_rows,
        near,
        next_near,
        gate_weight[0],
        up_weight[0],
        down_weight[0],
        model,
        inner,
        limit=32,
    )
    distance = 1
    while distance < n // 2:
        keep, send = call(
            add_kernel,
            (shape((keep.shape[0] // 2,) + HEADS, bf16),) * 2,
            [VMEM] * 2,
            keep,
            swap(send, n, distance),
        )
        distance *= 2
    return call(
        finish_kernel,
        shape((1, WIDTH), bf16),
        [VMEM] * 3,
        hidden,
        keep,
        swap(send, n, distance),
    )


def solution(mesh):
    return jax.shard_map(
        body,
        mesh=mesh,
        in_specs=(
            P(("grp", "exp"), None),
            P(("grp", "exp"), None),
            P(("grp", "exp"), None),
            P("grp", "exp", None),
            P("grp"),
            P(),
            P(("grp", "exp"), None),
            P(("grp", "exp"), None),
            P("exp", None, None),
            P("exp", None, None),
            P("exp", None, None),
            P(None, None, "exp"),
            P(None, None, "exp"),
        ),
        out_specs=P(("grp", "exp"), None),
        check_vma=False,
    )
```

```python
import functools

import jax
import jax.numpy as jnp
from jax import lax
from jax.experimental import pallas as pl
from jax.experimental.pallas import tpu as pltpu
from jax.sharding import PartitionSpec as P

QUERY_HEADS = 16
KEY_VALUE_HEADS = 2
HEAD_WIDTH = 128
ADAPTER_RANK = 32
GROUPED = QUERY_HEADS // KEY_VALUE_HEADS
KEY_VALUE_WIDTH = KEY_VALUE_HEADS * HEAD_WIDTH
WIDTH = QUERY_HEADS * HEAD_WIDTH
INV_ROOT = HEAD_WIDTH ** (-0.5)
NEAR = 4
NEW_ROWS = 2 * KEY_VALUE_HEADS
HEADS = (QUERY_HEADS, HEAD_WIDTH)
PARTIAL = (2 * QUERY_HEADS, HEAD_WIDTH)
RESID_ROW = QUERY_HEADS
NEW_ROW = 2 * QUERY_HEADS
GATE_ROW = NEW_ROW + NEW_ROWS
MESSAGE = (3 * QUERY_HEADS, HEAD_WIDTH)

floor_score = -1e30
epsilon = 1e-06
FILL = 4000

VMEM = pl.BlockSpec(memory_space=pltpu.VMEM)
SMEM = pl.BlockSpec(memory_space=pltpu.SMEM)
HBM = pl.BlockSpec(memory_space=pltpu.HBM)
shape = jax.ShapeDtypeStruct
bf16, f32 = jnp.bfloat16, jnp.float32


def call(kernel, shapes, specs, *args, limit=8, scratch=(), nanos=400):
    return pl.pallas_call(
        kernel,
        out_shape=shapes,
        in_specs=specs,
        out_specs=jax.tree.map(lambda _: VMEM, shapes),
        scratch_shapes=scratch,
        cost_estimate=pl.CostEstimate(
            flops=nanos * 1000000, transcendentals=0, bytes_accessed=0
        ),
        compiler_params=pltpu.CompilerParams(vmem_limit_bytes=limit * 1024 * 1024),
    )(*args)


def hold_kernel(value, after, out):
    out[...] = value[...]


def hold(value, after):
    return call(
        hold_kernel, shape(value.shape, value.dtype), [VMEM] * 2, value, after, nanos=FILL
    )


def iota(dims, dim):
    return lax.broadcasted_iota(jnp.int32, dims, dim)


def as_rows(line, rows):
    return jnp.concatenate(
        [line[:, j * HEAD_WIDTH : (j + 1) * HEAD_WIDTH] for j in range(rows)], axis=0
    )


def swap(value, n, distance):
    return lax.ppermute(value, "exp", [(t, t ^ distance) for t in range(n)])


def distance_of(column, far):
    bits = far.bit_length() - 1
    return sum(NEAR << i for i in range(bits) if column >> (bits - 1 - i) & 1)


def pad16(rows):
    return -(-rows // 16) * 16


def pack_kernel(query, resid, new, choice, probability, out, q_in, r_in, n_in, c_in, p_in, sems):
    copies = [
        pltpu.make_async_copy(source, target, sems.at[k])
        for k, (source, target) in enumerate(
            ((query, q_in), (resid, r_in), (new, n_in), (choice, c_in), (probability, p_in))
        )
    ]
    for copy in copies:
        copy.start()
    for copy in copies:
        copy.wait()
    q = as_rows(q_in[...].astype(f32), QUERY_HEADS)
    r = as_rows(r_in[...].astype(f32), QUERY_HEADS)
    fresh = as_rows(n_in[...].astype(f32), NEW_ROWS)
    p = p_in[...]
    shares = p / jnp.sum(p, axis=1, keepdims=True)
    lanes = iota((1, HEAD_WIDTH), 1)
    gates = jnp.zeros((1, HEAD_WIDTH), f32)
    for k in range(p.shape[1]):
        gates = gates + jnp.where(c_in[:, k : k + 1] == lanes, shares[:, k : k + 1], 0.0)
    rest = jnp.zeros((MESSAGE[0] - GATE_ROW - 1, HEAD_WIDTH), f32)
    out[0] = jnp.concatenate([q, r, fresh, gates, rest], axis=0).astype(bf16)


def join_kernel(mine, theirs, out):
    half = mine.shape[0]
    out[:half] = mine[...]
    out[half:] = theirs[...]


def narrow_kernel(mine, theirs, column, out):
    half = mine.shape[0]
    far = 2 * half
    column[:half] = mine[...]
    column[half:] = theirs[...]
    tails = []
    for w in range(far):
        source, at = (mine, w) if w < half else (theirs, w - half)
        out[w * QUERY_HEADS : (w + 1) * QUERY_HEADS] = source[at, :QUERY_HEADS]
        tails.append(source[at, NEW_ROW:].astype(f32))
    fresh = jnp.concatenate([tail[:NEW_ROWS] for tail in tails], axis=0)
    gates = jnp.concatenate([tail[NEW_ROWS : NEW_ROWS + 1] for tail in tails], axis=0)
    for rows, at in ((gates, far * QUERY_HEADS), (fresh, far * QUERY_HEADS + pad16(far))):
        extra = pad16(rows.shape[0]) - rows.shape[0]
        if extra:
            rows = jnp.concatenate([rows, jnp.zeros((extra, HEAD_WIDTH), f32)], axis=0)
        out[at : at + rows.shape[0]] = rows.astype(bf16)


def encode(top, total, acc):
    lanes = iota(HEADS, 1)
    stats = jnp.zeros(HEADS, f32)
    for at, value in ((0, top), (3, total)):
        for k in range(3):
            part = value.astype(bf16).astype(f32)
            stats = jnp.where(lanes == at + k, part, stats)
            value = value - part
    return jnp.concatenate([acc, stats], axis=0).astype(bf16)


def decode(message):
    value = message.astype(f32)
    acc, stats = value[:QUERY_HEADS], value[QUERY_HEADS:]
    top = stats[:, 0:1] + stats[:, 1:2] + stats[:, 2:3]
    total = stats[:, 3:4] + stats[:, 4:5] + stats[:, 5:6]
    return top, total, acc


def merged(parts):
    top = functools.reduce(jnp.maximum, [part[0] for part in parts])
    total, acc = 0.0, 0.0
    for peak, amount, value in parts:
        share = jnp.exp(peak - top)
        total = total + share * amount
        acc = acc + share * value
    return top, total, acc


def attend_kernel(after, lengths, mine, theirs, cache, keep, send, *, far):
    me = lax.axis_index("exp")
    sequences, block, _ = cache.shape
    rows = 2 * QUERY_HEADS
    first_group = (iota((rows, HEAD_WIDTH), 0) % QUERY_HEADS) < GROUPED
    positions = me * block + iota((rows, block), 1)
    for y in range(2):
        for w in range(far):
            s = lax.shift_right_logical(me, 1) ^ ((distance_of(w, far) >> 1) | y)
            cut = slice(w * QUERY_HEADS, (w + 1) * QUERY_HEADS)
            both = jnp.concatenate([mine[y, cut], theirs[y, cut]], axis=0)
            zero = jnp.zeros_like(both)
            wide = jnp.concatenate(
                [jnp.where(first_group, both, zero), jnp.where(first_group, zero, both)], axis=1
            )
            keys = cache[s, :, :KEY_VALUE_WIDTH]
            values = cache[s, :, KEY_VALUE_WIDTH:]
            scores = (
                lax.dot_general(
                    wide, keys, (((1,), (1,)), ((), ())), preferred_element_type=f32
                )
                * INV_ROOT
            )
            valid = positions < lengths[s]
            scores = jnp.where(valid, scores, floor_score)
            top = jnp.max(scores, axis=1, keepdims=True)
            weights = jnp.where(valid, jnp.exp(scores - top), 0.0).astype(bf16)
            total = jnp.sum(weights.astype(f32), axis=1, keepdims=True)
            acc = jnp.dot(weights, values, preferred_element_type=f32)
            acc = jnp.where(first_group, acc[:, :HEAD_WIDTH], acc[:, HEAD_WIDTH:])
            for part, cut in (
                (keep, slice(0, QUERY_HEADS)),
                (send, slice(QUERY_HEADS, 2 * QUERY_HEADS)),
            ):
                part[y * far + w] = encode(top[cut], total[cut], acc[cut])


def merge_kernel(mine, theirs, *outs, flip):
    count = mine.shape[0] // len(outs)
    for slot in range(mine.shape[0]):
        parts = [decode(mine[slot]), decode(theirs[slot ^ flip])]
        outs[slot // count][slot % count] = encode(*merged(parts))


def token_kernel(after, mine, theirs, column, near, scale, hidden_out, normed_out):
    second = lax.axis_index("exp") % 2 == 1
    first_group = iota(HEADS, 0) < GROUPED
    far = column.shape[0]
    near_at = far * QUERY_HEADS + pad16(far)
    others = near[0, near_at:].astype(f32)

    def by_head(rows, at):
        return jnp.where(first_group, rows[at : at + 1], rows[at + 1 : at + 2])

    for w in range(far):
        message = column[w].astype(f32)
        q, resid, new = message[:QUERY_HEADS], message[RESID_ROW:NEW_ROW], message[NEW_ROW:GATE_ROW]
        other = others[w * NEW_ROWS : (w + 1) * NEW_ROWS]
        own_score = jnp.sum(q * by_head(new, 0), axis=1, keepdims=True) * INV_ROOT
        other_score = jnp.sum(q * by_head(other, 0), axis=1, keepdims=True) * INV_ROOT
        other_score = jnp.where(second, other_score, floor_score)
        new_max = jnp.maximum(own_score, other_score)
        own_weight = jnp.exp(own_score - new_max).astype(bf16).astype(f32)
        other_weight = jnp.where(second, jnp.exp(other_score - new_max), 0.0)
        other_weight = other_weight.astype(bf16).astype(f32)
        fresh = own_weight * by_head(new, 2) + other_weight * by_head(other, 2)
        _, total, acc = merged(
            [
                decode(mine[w]),
                decode(theirs[w ^ 1]),
                (new_max, own_weight + other_weight, fresh),
            ]
        )
        hidden = resid + acc / total
        squares = jnp.sum(jnp.sum(hidden * hidden, axis=1, keepdims=True), axis=0, keepdims=True)
        normed = hidden * lax.rsqrt(squares / WIDTH + epsilon) * scale[...]
        if w == 0:
            hidden_out[...] = hidden
        normed_out[w] = normed.astype(bf16)


def dot_pair(value, factor, contract):
    high = value.astype(bf16)
    low = (value - high.astype(f32)).astype(bf16)
    both = lax.dot_general(
        jnp.concatenate([high, low], axis=0),
        factor,
        (((1,), (contract,)), ((), ())),
        preferred_element_type=f32,
    )
    return both[: value.shape[0]] + both[value.shape[0] :]


def expert_kernel(
    mine, theirs, near, next_near, gate_w, up_w, down_w, model, inner, keep, send, *, far
):
    me = lax.axis_index("exp")
    half = mine.shape[0]
    x = jnp.concatenate([mine[...].astype(f32), theirs[...].astype(f32)], axis=0)
    x = x.reshape(2 * half, WIDTH).astype(bf16)
    r = ADAPTER_RANK
    mixed = lax.dot_general(
        x, model[: 2 * r], (((1,), (1,)), ((), ())), preferred_element_type=f32
    )
    gate = jnp.dot(x, gate_w[...], preferred_element_type=f32)
    gate = gate + dot_pair(mixed[:, :r], inner[:, :r], 1)
    up = jnp.dot(x, up_w[...], preferred_element_type=f32)
    up = up + dot_pair(mixed[:, r:], inner[:, r : 2 * r], 1)
    act = (gate / (1.0 + jnp.exp(-gate)) * up).astype(bf16)
    lowered = jnp.dot(act, inner[:, 2 * r : 3 * r], preferred_element_type=f32)
    result = jnp.dot(act, down_w[...], preferred_element_type=f32)
    result = result + dot_pair(lowered, model[2 * r :], 0)
    lanes = iota((pad16(far), HEAD_WIDTH), 1)
    gate_at = far * QUERY_HEADS
    for c, (routes, part) in enumerate(((near, keep), (next_near, send))):
        for y in range(2):
            route = routes[y, gate_at : gate_at + pad16(far)].astype(f32)
            share = jnp.sum(jnp.where(lanes == me, route, 0.0), axis=1, keepdims=True)
            for w in range(far):
                slot = y * far + w
                line = result[c * half + slot : c * half + slot + 1] * share[w : w + 1]
                part[slot] = as_rows(line, QUERY_HEADS).astype(bf16)


def add_kernel(mine, theirs, keep, send):
    half = keep.shape[0]
    for out, at in ((keep, 0), (send, half)):
        total = mine[at : at + half].astype(f32) + theirs[at : at + half].astype(f32)
        out[...] = total.astype(bf16)


def finish_kernel(hidden, mine, theirs, out):
    total = hidden[...] + mine[0].astype(f32) + theirs[0].astype(f32)
    line = jnp.concatenate([total[j : j + 1] for j in range(QUERY_HEADS)], axis=1)
    out[...] = line.astype(bf16)


def lora_pack_kernel(after, model, inner, *outs):
    low, first = lax.axis_index("exp") % NEAR, lax.axis_index("grp") == 0
    ranks, split, most = model.shape[1], model.shape[1] // 2, outs[0].shape[1] - model.shape[1] // 2
    rest = inner.shape[1] - most
    for k, out in enumerate(outs):
        out[:, split:, ranks:] = jnp.zeros((out.shape[0], most, HEAD_WIDTH - ranks), out.dtype)
        for z in range(out.shape[0]):
            at = z * NEAR + (low ^ k)
            out[z, :split] = jnp.where(first, model[at, :split], model[at, split:])
            lower = inner[at, most:]
            if rest < most:
                pad = jnp.zeros((most - rest, ranks), out.dtype)
                lower = jnp.concatenate([lower, pad], axis=0)
            out[z, split:, :ranks] = jnp.where(first, inner[at, :most], lower)


def lora_turn_kernel(after, *refs):
    me = lax.axis_index("exp")
    low, high = me % NEAR, me // NEAR
    got, outs = refs[:NEAR], refs[NEAR:]
    for j, out in enumerate(outs):
        for k, ref in enumerate(got):
            out[low ^ k] = ref[high ^ j]


def lora_order_kernel(after, *refs):
    high = lax.axis_index("exp") // NEAR
    got, out = refs[:-1], refs[-1]
    for j, ref in enumerate(got):
        out[pl.ds((high ^ j) * NEAR, NEAR)] = ref[...]


def lora_join_kernel(mine, theirs, model, inner):
    first = lax.axis_index("grp") == 0
    split = model.shape[0] // 2
    most, width = mine.shape[1] - split, inner.shape[0] // mine.shape[0]
    for at in range(mine.shape[0]):
        own, other = mine[at], theirs[at]
        halves = jnp.where(first, own, other), jnp.where(first, other, own)
        columns = slice(at * HEAD_WIDTH, (at + 1) * HEAD_WIDTH)
        model[:split, columns] = halves[0][:split]
        model[split:, columns] = halves[1][:split]
        inner[at * width : at * width + most] = halves[0][split:]
        inner[at * width + most : (at + 1) * width] = halves[1][split : split + width - most]


def lora_near(adapter_model, adapter_hidden, n, marks):
    total, ranks, model_width = adapter_model.shape
    inner_width = adapter_hidden.shape[2]
    inner = jnp.transpose(adapter_hidden, (0, 2, 1))
    if model_width != HEAD_WIDTH or inner_width % 16 or lax.axis_size("grp") != 2:
        model = lax.all_to_all(adapter_model, "exp", split_axis=0, concat_axis=2, tiled=True)
        inner = lax.all_to_all(inner, "exp", split_axis=0, concat_axis=1, tiled=True)
        return [model[0], inner[0]], True
    far = n // NEAR
    block = (ranks // 2 + pad16(inner_width // 2), HEAD_WIDTH)
    packed = call(
        lora_pack_kernel,
        (shape((far,) + block, bf16),) * NEAR,
        [VMEM] * 3,
        marks[0],
        adapter_model,
        inner,
        nanos=FILL,
    )
    turned = call(
        lora_turn_kernel,
        (shape((NEAR,) + block, bf16),) * far,
        [VMEM] * (1 + NEAR),
        marks[3],
        packed[0],
        swap(hold(packed[1], marks[1]), n, 1),
        swap(packed[2], n, 2),
        swap(hold(packed[3], marks[1]), n, 3),
        nanos=FILL,
    )
    return turned, False


def lora_far(turned, n, marks):
    far = len(turned)
    rows = turned[0].shape[1]
    got = [turned[0], swap(turned[1], n, NEAR)]
    for j in range(2, far):
        got.append(swap(hold(turned[j], marks[j - 2]), n, j * NEAR))
    return call(
        lora_order_kernel,
        shape((n, rows, HEAD_WIDTH), bf16),
        [VMEM] * (1 + far),
        marks[far - 2],
        *got,
        nanos=FILL,
    )


def lora_join(ordered, inner_width):
    n = ordered.shape[0]
    return call(
        lora_join_kernel,
        (
            shape((3 * ADAPTER_RANK, n * HEAD_WIDTH), bf16),
            shape((n * inner_width, HEAD_WIDTH), bf16),
        ),
        [VMEM] * 2,
        ordered,
        lax.ppermute(ordered, "grp", [(0, 1), (1, 0)]),
    )


def body(
    resid,
    queries,
    incoming_key_value,
    key_value_cache,
    lengths,
    norm_scale_vector,
    expert_choice,
    router_probability,
    gate_weight,
    up_weight,
    down_weight,
    adapter_model,
    adapter_hidden,
):
    n = lax.axis_size("exp")
    far = n // NEAR

    first_inputs = (queries, resid, incoming_key_value, expert_choice, router_probability)
    message = call(
        pack_kernel,
        shape((1,) + MESSAGE, bf16),
        [HBM] * 5,
        *[pltpu.with_memory_space_constraint(x, pltpu.HBM) for x in first_inputs],
        scratch=[pltpu.VMEM(x.shape, x.dtype) for x in first_inputs]
        + [pltpu.SemaphoreType.DMA((5,))],
        nanos=4000,
    )
    marks, distance = [message], n // 2
    while distance > NEAR:
        message = call(
            join_kernel,
            shape((2 * message.shape[0],) + MESSAGE, bf16),
            [VMEM] * 2,
            message,
            swap(message, n, distance),
        )
        distance //= 2
    near_rows = far * QUERY_HEADS + pad16(far) + pad16(NEW_ROWS * far)
    column, narrow = call(
        narrow_kernel,
        (shape((far,) + MESSAGE, bf16), shape((near_rows, HEAD_WIDTH), bf16)),
        [VMEM] * 2,
        message,
        swap(message, n, NEAR),
    )
    marks += [message, column]
    narrow = narrow[None]
    near = call(
        join_kernel,
        shape((2, near_rows, HEAD_WIDTH), bf16),
        [VMEM] * 2,
        narrow,
        swap(narrow, n, 2),
    )
    marks.append(near)
    turned, whole = lora_near(adapter_model, adapter_hidden, n, marks)
    next_near = swap(near, n, 1)
    keep, send = call(
        functools.partial(attend_kernel, far=far),
        (shape((2 * far,) + PARTIAL, bf16),) * 2,
        [VMEM, SMEM] + [VMEM] * 3,
        turned[0],
        lengths,
        near,
        next_near,
        key_value_cache,
        nanos=8000,
    )
    marks = [keep]
    keep, send = call(
        functools.partial(merge_kernel, flip=0),
        (shape((far,) + PARTIAL, bf16),) * 2,
        [VMEM] * 2,
        keep,
        swap(send, n, 1),
    )
    marks.append(keep)
    theirs, distance, flip = swap(send, n, 2), NEAR, 0
    while distance < n:
        keep = call(
            functools.partial(merge_kernel, flip=flip),
            shape((far,) + PARTIAL, bf16),
            [VMEM] * 2,
            keep,
            theirs,
        )
        if distance == NEAR:
            marks.append(keep)
            ordered = turned[0] if whole else lora_far(turned, n, marks)
        theirs = swap(keep, n, distance)
        flip = far * NEAR // (2 * distance)
        distance *= 2
    hidden, normed = call(
        token_kernel,
        (shape(HEADS, f32), shape((far,) + HEADS, bf16)),
        [VMEM] * 6,
        ordered,
        keep,
        theirs,
        column,
        next_near,
        norm_scale_vector.reshape(HEADS),
        nanos=4000,
    )
    rows = call(
        join_kernel, shape((2 * far,) + HEADS, bf16), [VMEM] * 2, normed, swap(normed, n, 2)
    )
    next_rows = swap(rows, n, 1)
    model, inner = turned if whole else lora_join(ordered, adapter_hidden.shape[2])
    keep, send = call(
        functools.partial(expert_kernel, far=far),
        (shape((2 * far,) + HEADS, bf16),) * 2,
        [VMEM] * 9,
        rows,
        next_rows,
        near,
        next_near,
        gate_weight[0],
        up_weight[0],
        down_weight[0],
        model,
        inner,
        limit=32,
    )
    distance = 1
    while distance < n // 2:
        keep, send = call(
            add_kernel,
            (shape((keep.shape[0] // 2,) + HEADS, bf16),) * 2,
            [VMEM] * 2,
            keep,
            swap(send, n, distance),
        )
        distance *= 2
    return call(
        finish_kernel,
        shape((1, WIDTH), bf16),
        [VMEM] * 3,
        hidden,
        keep,
        swap(send, n, distance),
    )


def solution(mesh):
    return jax.shard_map(
        body,
        mesh=mesh,
        in_specs=(
            P(("grp", "exp"), None),
            P(("grp", "exp"), None),
            P(("grp", "exp"), None),
            P("grp", "exp", None),
            P("grp"),
            P(),
            P(("grp", "exp"), None),
            P(("grp", "exp"), None),
            P("exp", None, None),
            P("exp", None, None),
            P("exp", None, None),
            P(None, None, "exp"),
            P(None, None, "exp"),
        ),
        out_specs=P(("grp", "exp"), None),
        check_vma=False,
    )
```

```python
import functools

import jax
import jax.numpy as jnp
from jax import lax
from jax.experimental import pallas as pl
from jax.experimental.pallas import tpu as pltpu
from jax.sharding import PartitionSpec as P

QUERY_HEADS = 16
KEY_VALUE_HEADS = 2
HEAD_WIDTH = 128
ADAPTER_RANK = 32
GROUPED = QUERY_HEADS // KEY_VALUE_HEADS
KEY_VALUE_WIDTH = KEY_VALUE_HEADS * HEAD_WIDTH
WIDTH = QUERY_HEADS * HEAD_WIDTH
INV_ROOT = HEAD_WIDTH ** (-0.5)
NEAR = 4
NEW_ROWS = 2 * KEY_VALUE_HEADS
HEADS = (QUERY_HEADS, HEAD_WIDTH)
PARTIAL = (2 * QUERY_HEADS, HEAD_WIDTH)
RESID_ROW = QUERY_HEADS
NEW_ROW = 2 * QUERY_HEADS
GATE_ROW = NEW_ROW + NEW_ROWS
MESSAGE = (3 * QUERY_HEADS, HEAD_WIDTH)

floor_score = -1e30
epsilon = 1e-06
FILL = 4000
MERGE = 1600

VMEM = pl.BlockSpec(memory_space=pltpu.VMEM)
SMEM = pl.BlockSpec(memory_space=pltpu.SMEM)
HBM = pl.BlockSpec(memory_space=pltpu.HBM)
shape = jax.ShapeDtypeStruct
bf16, f32 = jnp.bfloat16, jnp.float32


def call(kernel, shapes, specs, *args, limit=8, scratch=(), nanos=400):
    return pl.pallas_call(
        kernel,
        out_shape=shapes,
        in_specs=specs,
        out_specs=jax.tree.map(lambda _: VMEM, shapes),
        scratch_shapes=scratch,
        cost_estimate=pl.CostEstimate(
            flops=nanos * 1000000, transcendentals=0, bytes_accessed=0
        ),
        compiler_params=pltpu.CompilerParams(vmem_limit_bytes=limit * 1024 * 1024),
    )(*args)


def iota(dims, dim):
    return lax.broadcasted_iota(jnp.int32, dims, dim)


def as_rows(line, rows):
    return jnp.concatenate(
        [line[:, j * HEAD_WIDTH : (j + 1) * HEAD_WIDTH] for j in range(rows)], axis=0
    )


def swap(value, n, distance):
    return lax.ppermute(value, "exp", [(t, t ^ distance) for t in range(n)])


def distance_of(column, far):
    bits = far.bit_length() - 1
    return sum(NEAR << i for i in range(bits) if column >> (bits - 1 - i) & 1)


def pad16(rows):
    return -(-rows // 16) * 16


def pack_kernel(query, resid, new, choice, probability, out, q_in, r_in, n_in, c_in, p_in, sems):
    copies = [
        pltpu.make_async_copy(source, target, sems.at[k])
        for k, (source, target) in enumerate(
            ((query, q_in), (resid, r_in), (new, n_in), (choice, c_in), (probability, p_in))
        )
    ]
    for copy in copies:
        copy.start()
    for copy in copies:
        copy.wait()
    q = as_rows(q_in[...].astype(f32), QUERY_HEADS)
    r = as_rows(r_in[...].astype(f32), QUERY_HEADS)
    fresh = as_rows(n_in[...].astype(f32), NEW_ROWS)
    p = p_in[...]
    shares = p / jnp.sum(p, axis=1, keepdims=True)
    lanes = iota((1, HEAD_WIDTH), 1)
    gates = jnp.zeros((1, HEAD_WIDTH), f32)
    for k in range(p.shape[1]):
        gates = gates + jnp.where(c_in[:, k : k + 1] == lanes, shares[:, k : k + 1], 0.0)
    rest = jnp.zeros((MESSAGE[0] - GATE_ROW - 1, HEAD_WIDTH), f32)
    out[0] = jnp.concatenate([q, r, fresh, gates, rest], axis=0).astype(bf16)


def join_kernel(mine, theirs, out):
    half = mine.shape[0]
    out[:half] = mine[...]
    out[half:] = theirs[...]


def narrow_kernel(mine, theirs, column, out):
    half = mine.shape[0]
    far = 2 * half
    column[:half] = mine[...]
    column[half:] = theirs[...]
    tails = []
    for w in range(far):
        source, at = (mine, w) if w < half else (theirs, w - half)
        out[w * QUERY_HEADS : (w + 1) * QUERY_HEADS] = source[at, :QUERY_HEADS]
        tails.append(source[at, NEW_ROW:].astype(f32))
    fresh = jnp.concatenate([tail[:NEW_ROWS] for tail in tails], axis=0)
    gates = jnp.concatenate([tail[NEW_ROWS : NEW_ROWS + 1] for tail in tails], axis=0)
    for rows, at in ((gates, far * QUERY_HEADS), (fresh, far * QUERY_HEADS + pad16(far))):
        extra = pad16(rows.shape[0]) - rows.shape[0]
        if extra:
            rows = jnp.concatenate([rows, jnp.zeros((extra, HEAD_WIDTH), f32)], axis=0)
        out[at : at + rows.shape[0]] = rows.astype(bf16)


def encode(top, total, acc):
    lanes = iota(HEADS, 1)
    stats = jnp.zeros(HEADS, f32)
    for at, value in ((0, top), (3, total)):
        for k in range(3):
            part = value.astype(bf16).astype(f32)
            stats = jnp.where(lanes == at + k, part, stats)
            value = value - part
    return jnp.concatenate([acc, stats], axis=0).astype(bf16)


def decode(message):
    value = message.astype(f32)
    acc, stats = value[:QUERY_HEADS], value[QUERY_HEADS:]
    top = stats[:, 0:1] + stats[:, 1:2] + stats[:, 2:3]
    total = stats[:, 3:4] + stats[:, 4:5] + stats[:, 5:6]
    return top, total, acc


def merged(parts):
    top = functools.reduce(jnp.maximum, [part[0] for part in parts])
    total, acc = 0.0, 0.0
    for peak, amount, value in parts:
        share = jnp.exp(peak - top)
        total = total + share * amount
        acc = acc + share * value
    return top, total, acc


def attend_kernel(after, lengths, mine, theirs, cache, keep, send, *, far):
    me = lax.axis_index("exp")
    sequences, block, _ = cache.shape
    rows = 2 * QUERY_HEADS
    first_group = (iota((rows, HEAD_WIDTH), 0) % QUERY_HEADS) < GROUPED
    positions = me * block + iota((rows, block), 1)
    for y in range(2):
        for w in range(far):
            s = lax.shift_right_logical(me, 1) ^ ((distance_of(w, far) >> 1) | y)
            cut = slice(w * QUERY_HEADS, (w + 1) * QUERY_HEADS)
            both = jnp.concatenate([mine[y, cut], theirs[y, cut]], axis=0)
            zero = jnp.zeros_like(both)
            wide = jnp.concatenate(
                [jnp.where(first_group, both, zero), jnp.where(first_group, zero, both)], axis=1
            )
            keys = cache[s, :, :KEY_VALUE_WIDTH]
            values = cache[s, :, KEY_VALUE_WIDTH:]
            scores = (
                lax.dot_general(
                    wide, keys, (((1,), (1,)), ((), ())), preferred_element_type=f32
                )
                * INV_ROOT
            )
            valid = positions < lengths[s]
            scores = jnp.where(valid, scores, floor_score)
            top = jnp.max(scores, axis=1, keepdims=True)
            weights = jnp.where(valid, jnp.exp(scores - top), 0.0).astype(bf16)
            total = jnp.sum(weights.astype(f32), axis=1, keepdims=True)
            acc = jnp.dot(weights, values, preferred_element_type=f32)
            acc = jnp.where(first_group, acc[:, :HEAD_WIDTH], acc[:, HEAD_WIDTH:])
            for part, cut in (
                (keep, slice(0, QUERY_HEADS)),
                (send, slice(QUERY_HEADS, 2 * QUERY_HEADS)),
            ):
                part[y * far + w] = encode(top[cut], total[cut], acc[cut])


def merge_kernel(mine, theirs, *outs, flip):
    count = mine.shape[0] // len(outs)
    for slot in range(mine.shape[0]):
        parts = [decode(mine[slot]), decode(theirs[slot ^ flip])]
        outs[slot // count][slot % count] = encode(*merged(parts))


def token_kernel(after, mine, theirs, column, near, scale, hidden_out, normed_out):
    second = lax.axis_index("exp") % 2 == 1
    first_group = iota(HEADS, 0) < GROUPED
    far = column.shape[0]
    near_at = far * QUERY_HEADS + pad16(far)
    others = near[0, near_at:].astype(f32)

    def by_head(rows, at):
        return jnp.where(first_group, rows[at : at + 1], rows[at + 1 : at + 2])

    for w in range(far):
        message = column[w].astype(f32)
        q, resid, new = message[:QUERY_HEADS], message[RESID_ROW:NEW_ROW], message[NEW_ROW:GATE_ROW]
        other = others[w * NEW_ROWS : (w + 1) * NEW_ROWS]
        own_score = jnp.sum(q * by_head(new, 0), axis=1, keepdims=True) * INV_ROOT
        other_score = jnp.sum(q * by_head(other, 0), axis=1, keepdims=True) * INV_ROOT
        other_score = jnp.where(second, other_score, floor_score)
        new_max = jnp.maximum(own_score, other_score)
        own_weight = jnp.exp(own_score - new_max).astype(bf16).astype(f32)
        other_weight = jnp.where(second, jnp.exp(other_score - new_max), 0.0)
        other_weight = other_weight.astype(bf16).astype(f32)
        fresh = own_weight * by_head(new, 2) + other_weight * by_head(other, 2)
        _, total, acc = merged(
            [
                decode(mine[w]),
                decode(theirs[w ^ 1]),
                (new_max, own_weight + other_weight, fresh),
            ]
        )
        hidden = resid + acc / total
        squares = jnp.sum(jnp.sum(hidden * hidden, axis=1, keepdims=True), axis=0, keepdims=True)
        normed = hidden * lax.rsqrt(squares / WIDTH + epsilon) * scale[...]
        if w == 0:
            hidden_out[...] = hidden
        normed_out[w] = normed.astype(bf16)


def dot_pair(value, factor, contract):
    high = value.astype(bf16)
    low = (value - high.astype(f32)).astype(bf16)
    both = lax.dot_general(
        jnp.concatenate([high, low], axis=0),
        factor,
        (((1,), (contract,)), ((), ())),
        preferred_element_type=f32,
    )
    return both[: value.shape[0]] + both[value.shape[0] :]


def expert_kernel(
    mine, theirs, near, next_near, gate_w, up_w, down_w, model, inner, keep, send, *, far
):
    me = lax.axis_index("exp")
    half = mine.shape[0]
    x = jnp.concatenate([mine[...].astype(f32), theirs[...].astype(f32)], axis=0)
    x = x.reshape(2 * half, WIDTH).astype(bf16)
    r = ADAPTER_RANK
    mixed = lax.dot_general(
        x, model[: 2 * r], (((1,), (1,)), ((), ())), preferred_element_type=f32
    )
    gate = jnp.dot(x, gate_w[...], preferred_element_type=f32)
    gate = gate + dot_pair(mixed[:, :r], inner[:, :r], 1)
    up = jnp.dot(x, up_w[...], preferred_element_type=f32)
    up = up + dot_pair(mixed[:, r:], inner[:, r : 2 * r], 1)
    act = (gate / (1.0 + jnp.exp(-gate)) * up).astype(bf16)
    lowered = jnp.dot(act, inner[:, 2 * r : 3 * r], preferred_element_type=f32)
    result = jnp.dot(act, down_w[...], preferred_element_type=f32)
    result = result + dot_pair(lowered, model[2 * r :], 0)
    lanes = iota((pad16(far), HEAD_WIDTH), 1)
    gate_at = far * QUERY_HEADS
    for c, (routes, part) in enumerate(((near, keep), (next_near, send))):
        for y in range(2):
            route = routes[y, gate_at : gate_at + pad16(far)].astype(f32)
            share = jnp.sum(jnp.where(lanes == me, route, 0.0), axis=1, keepdims=True)
            for w in range(far):
                slot = y * far + w
                line = result[c * half + slot : c * half + slot + 1] * share[w : w + 1]
                part[slot] = as_rows(line, QUERY_HEADS).astype(bf16)


def add_kernel(mine, theirs, keep, send):
    half = keep.shape[0]
    for out, at in ((keep, 0), (send, half)):
        total = mine[at : at + half].astype(f32) + theirs[at : at + half].astype(f32)
        out[...] = total.astype(bf16)


def finish_kernel(hidden, mine, theirs, out):
    total = hidden[...] + mine[0].astype(f32) + theirs[0].astype(f32)
    line = jnp.concatenate([total[j : j + 1] for j in range(QUERY_HEADS)], axis=1)
    out[...] = line.astype(bf16)


def without(index, bit):
    return (index // (2 * bit)) * bit + index % bit


def lora_pack_kernel(after, model, inner, keep, send, *, bit):
    me, first = lax.axis_index("exp"), lax.axis_index("grp") == 0
    ranks, split = model.shape[1], model.shape[1] // 2
    most = keep.shape[1] - split
    rest = inner.shape[1] - most
    for out in (keep, send):
        out[:, split:, ranks:] = jnp.zeros((out.shape[0], most, HEAD_WIDTH - ranks), out.dtype)
    for d in range(model.shape[0]):
        out, at, source = (send if d & bit else keep), without(d, bit), me ^ d
        out[at, :split] = jnp.where(first, model[source, :split], model[source, split:])
        lower = inner[source, most:]
        if rest < most:
            pad = jnp.zeros((most - rest, ranks), out.dtype)
            lower = jnp.concatenate([lower, pad], axis=0)
        out[at, split:, :ranks] = jnp.where(first, inner[source, :most], lower)


def lora_turn_kernel(after, kept, got, *outs, bit, following):
    for d in range(2 * kept.shape[0]):
        value = (got if d & bit else kept)[without(d, bit)]
        outs[1 if d & following else 0][without(d, following)] = value


def lora_order_kernel(after, kept, got, out, *, bit):
    me = lax.axis_index("exp")
    for d in range(2 * kept.shape[0]):
        out[me ^ d] = (got if d & bit else kept)[without(d, bit)]


def lora_join_kernel(mine, theirs, model, inner):
    first = lax.axis_index("grp") == 0
    split = model.shape[0] // 2
    most, width = mine.shape[1] - split, inner.shape[0] // mine.shape[0]
    for at in range(mine.shape[0]):
        own, other = mine[at], theirs[at]
        halves = jnp.where(first, own, other), jnp.where(first, other, own)
        columns = slice(at * HEAD_WIDTH, (at + 1) * HEAD_WIDTH)
        model[:split, columns] = halves[0][:split]
        model[split:, columns] = halves[1][:split]
        inner[at * width : at * width + most] = halves[0][split:]
        inner[at * width + most : (at + 1) * width] = halves[1][split : split + width - most]


def lora_start(adapter_model, adapter_hidden, n, after):
    total, ranks, model_width = adapter_model.shape
    inner_width = adapter_hidden.shape[2]
    inner = jnp.transpose(adapter_hidden, (0, 2, 1))
    if model_width != HEAD_WIDTH or inner_width % 16 or lax.axis_size("grp") != 2:
        model = lax.all_to_all(adapter_model, "exp", split_axis=0, concat_axis=2, tiled=True)
        inner = lax.all_to_all(inner, "exp", split_axis=0, concat_axis=1, tiled=True)
        return [model[0], inner[0]], True
    block = (ranks // 2 + pad16(inner_width // 2), HEAD_WIDTH)
    packed = call(
        functools.partial(lora_pack_kernel, bit=n // 2),
        (shape((n // 2,) + block, bf16),) * 2,
        [VMEM] * 3,
        after,
        adapter_model,
        inner,
        nanos=FILL,
    )
    return packed, False


def lora_turn(state, n, bit, following, after):
    keep, send = state
    return call(
        functools.partial(lora_turn_kernel, bit=bit, following=following),
        (shape(keep.shape, bf16),) * 2,
        [VMEM] * 3,
        after,
        keep,
        swap(send, n, bit),
        nanos=FILL,
    )


def lora_order(state, n, bit, after):
    keep, send = state
    return call(
        functools.partial(lora_order_kernel, bit=bit),
        shape((n,) + keep.shape[1:], bf16),
        [VMEM] * 3,
        after,
        keep,
        swap(send, n, bit),
        nanos=FILL,
    )


def lora_join(ordered, inner_width):
    n = ordered.shape[0]
    return call(
        lora_join_kernel,
        (
            shape((3 * ADAPTER_RANK, n * HEAD_WIDTH), bf16),
            shape((n * inner_width, HEAD_WIDTH), bf16),
        ),
        [VMEM] * 2,
        ordered,
        lax.ppermute(ordered, "grp", [(0, 1), (1, 0)]),
    )


def body(
    resid,
    queries,
    incoming_key_value,
    key_value_cache,
    lengths,
    norm_scale_vector,
    expert_choice,
    router_probability,
    gate_weight,
    up_weight,
    down_weight,
    adapter_model,
    adapter_hidden,
):
    n = lax.axis_size("exp")
    far = n // NEAR

    first_inputs = (queries, resid, incoming_key_value, expert_choice, router_probability)
    message = call(
        pack_kernel,
        shape((1,) + MESSAGE, bf16),
        [HBM] * 5,
        *[pltpu.with_memory_space_constraint(x, pltpu.HBM) for x in first_inputs],
        scratch=[pltpu.VMEM(x.shape, x.dtype) for x in first_inputs]
        + [pltpu.SemaphoreType.DMA((5,))],
        nanos=4000,
    )
    state, whole = lora_start(adapter_model, adapter_hidden, n, message)
    distance = n // 2
    while distance > NEAR:
        message = call(
            join_kernel,
            shape((2 * message.shape[0],) + MESSAGE, bf16),
            [VMEM] * 2,
            message,
            swap(message, n, distance),
        )
        distance //= 2
    near_rows = far * QUERY_HEADS + pad16(far) + pad16(NEW_ROWS * far)
    column, narrow = call(
        narrow_kernel,
        (shape((far,) + MESSAGE, bf16), shape((near_rows, HEAD_WIDTH), bf16)),
        [VMEM] * 2,
        message,
        swap(message, n, NEAR),
    )
    if not whole:
        state = lora_turn(state, n, n // 2, NEAR, column)
    narrow = narrow[None]
    near = call(
        join_kernel,
        shape((2, near_rows, HEAD_WIDTH), bf16),
        [VMEM] * 2,
        narrow,
        swap(narrow, n, 2),
    )
    next_near = swap(near, n, 1)
    keep, send = call(
        functools.partial(attend_kernel, far=far),
        (shape((2 * far,) + PARTIAL, bf16),) * 2,
        [VMEM, SMEM] + [VMEM] * 3,
        state[0],
        lengths,
        near,
        next_near,
        key_value_cache,
        nanos=8000,
    )
    keep, send = call(
        functools.partial(merge_kernel, flip=0),
        (shape((far,) + PARTIAL, bf16),) * 2,
        [VMEM] * 2,
        keep,
        swap(send, n, 1),
        nanos=MERGE,
    )
    if not whole:
        state = lora_turn(state, n, NEAR, 2, keep)
    theirs, distance, flip = swap(send, n, 2), NEAR, 0
    while distance < n:
        keep = call(
            functools.partial(merge_kernel, flip=flip),
            shape((far,) + PARTIAL, bf16),
            [VMEM] * 2,
            keep,
            theirs,
            nanos=MERGE,
        )
        if distance == NEAR and not whole:
            state = lora_turn(state, n, 2, 1, keep)
        elif not whole:
            ordered = lora_order(state, n, 1, keep)
        theirs = swap(keep, n, distance)
        flip = far * NEAR // (2 * distance)
        distance *= 2
    ordered = state[0] if whole else ordered
    hidden, normed = call(
        token_kernel,
        (shape(HEADS, f32), shape((far,) + HEADS, bf16)),
        [VMEM] * 6,
        ordered,
        keep,
        theirs,
        column,
        next_near,
        norm_scale_vector.reshape(HEADS),
        nanos=4000,
    )
    rows = call(
        join_kernel, shape((2 * far,) + HEADS, bf16), [VMEM] * 2, normed, swap(normed, n, 2)
    )
    next_rows = swap(rows, n, 1)
    model, inner = state if whole else lora_join(ordered, adapter_hidden.shape[2])
    keep, send = call(
        functools.partial(expert_kernel, far=far),
        (shape((2 * far,) + HEADS, bf16),) * 2,
        [VMEM] * 9,
        rows,
        next_rows,
        near,
        next_near,
        gate_weight[0],
        up_weight[0],
        down_weight[0],
        model,
        inner,
        limit=32,
    )
    distance = 1
    while distance < n // 2:
        keep, send = call(
            add_kernel,
            (shape((keep.shape[0] // 2,) + HEADS, bf16),) * 2,
            [VMEM] * 2,
            keep,
            swap(send, n, distance),
        )
        distance *= 2
    return call(
        finish_kernel,
        shape((1, WIDTH), bf16),
        [VMEM] * 3,
        hidden,
        keep,
        swap(send, n, distance),
    )


def solution(mesh):
    return jax.shard_map(
        body,
        mesh=mesh,
        in_specs=(
            P(("grp", "exp"), None),
            P(("grp", "exp"), None),
            P(("grp", "exp"), None),
            P("grp", "exp", None),
            P("grp"),
            P(),
            P(("grp", "exp"), None),
            P(("grp", "exp"), None),
            P("exp", None, None),
            P("exp", None, None),
            P("exp", None, None),
            P(None, None, "exp"),
            P(None, None, "exp"),
        ),
        out_specs=P(("grp", "exp"), None),
        check_vma=False,
    )
```

```python
import functools

import jax
import jax.numpy as jnp
from jax import lax
from jax.experimental import pallas as pl
from jax.experimental.pallas import tpu as pltpu
from jax.sharding import PartitionSpec as P

QUERY_HEADS = 16
KEY_VALUE_HEADS = 2
HEAD_WIDTH = 128
ADAPTER_RANK = 32
GROUPED = QUERY_HEADS // KEY_VALUE_HEADS
KEY_VALUE_WIDTH = KEY_VALUE_HEADS * HEAD_WIDTH
WIDTH = QUERY_HEADS * HEAD_WIDTH
INV_ROOT = HEAD_WIDTH ** (-0.5)
NEAR = 4
NEW_ROWS = 2 * KEY_VALUE_HEADS
HEADS = (QUERY_HEADS, HEAD_WIDTH)
MESSAGE = (2 * QUERY_HEADS, HEAD_WIDTH)

floor_score = -1e30
epsilon = 1e-06
FILL = 4000

VMEM = pl.BlockSpec(memory_space=pltpu.VMEM)
SMEM = pl.BlockSpec(memory_space=pltpu.SMEM)
HBM = pl.BlockSpec(memory_space=pltpu.HBM)
shape = jax.ShapeDtypeStruct
bf16, f32 = jnp.bfloat16, jnp.float32


def call(kernel, shapes, specs, *args, limit=8, scratch=(), nanos=400):
    return pl.pallas_call(
        kernel,
        out_shape=shapes,
        in_specs=specs,
        out_specs=jax.tree.map(lambda _: VMEM, shapes),
        scratch_shapes=scratch,
        cost_estimate=pl.CostEstimate(
            flops=nanos * 1000000, transcendentals=0, bytes_accessed=0
        ),
        compiler_params=pltpu.CompilerParams(vmem_limit_bytes=limit * 1024 * 1024),
    )(*args)


def hold_kernel(value, after, out):
    out[...] = value[...]


def hold(value, after):
    return call(
        hold_kernel, shape(value.shape, value.dtype), [VMEM] * 2, value, after, nanos=FILL
    )


def iota(dims, dim):
    return lax.broadcasted_iota(jnp.int32, dims, dim)


def as_rows(line, rows):
    return jnp.concatenate(
        [line[:, j * HEAD_WIDTH : (j + 1) * HEAD_WIDTH] for j in range(rows)], axis=0
    )


def swap(value, n, distance):
    return lax.ppermute(value, "exp", [(t, t ^ distance) for t in range(n)])


def distance_of(column, far):
    bits = far.bit_length() - 1
    return sum(NEAR << i for i in range(bits) if column >> (bits - 1 - i) & 1)


def pad16(rows):
    return -(-rows // 16) * 16


def stat_tiles(slots):
    return 1 if 6 * slots <= HEAD_WIDTH else 3


def pack_kernel(query, resid, out, q_in, r_in, sems):
    copies = [
        pltpu.make_async_copy(source, target, sems.at[k])
        for k, (source, target) in enumerate(((query, q_in), (resid, r_in)))
    ]
    for copy in copies:
        copy.start()
    for copy in copies:
        copy.wait()
    q = as_rows(q_in[...].astype(f32), QUERY_HEADS)
    r = as_rows(r_in[...].astype(f32), QUERY_HEADS)
    out[0] = jnp.concatenate([q, r], axis=0).astype(bf16)


def join_kernel(mine, theirs, out):
    half = mine.shape[0]
    out[:half] = mine[...]
    out[half:] = theirs[...]


def narrow_kernel(mine, theirs, new, residuals, out):
    half = mine.shape[0]
    for k, source in enumerate((mine, theirs)):
        for w in range(half):
            slot = k * half + w
            out[slot] = source[w, :QUERY_HEADS]
            residuals[slot] = source[w, QUERY_HEADS:]
    fresh = as_rows(new[...].astype(f32), NEW_ROWS)
    rest = jnp.zeros((QUERY_HEADS - NEW_ROWS, HEAD_WIDTH), f32)
    out[2 * half] = jnp.concatenate([fresh, rest], axis=0).astype(bf16)


def write_stats(stats, out, slots):
    parts = []
    for _ in range(3):
        part = stats.astype(bf16).astype(f32)
        parts.append(part)
        stats = stats - part
    if stat_tiles(slots) == 1:
        tile = parts[0]
        for k in (1, 2):
            tile = tile + pltpu.roll(parts[k], 2 * slots * k, 1)
        out[slots] = tile.astype(bf16)
    else:
        for k in range(3):
            out[slots + k] = parts[k].astype(bf16)


def read_stats(message, slots):
    if stat_tiles(slots) == 1:
        tile = message[slots].astype(f32)
        lanes = iota(HEADS, 1)
        stats = tile
        for k in (1, 2):
            stats = stats + pltpu.roll(tile, HEAD_WIDTH - 2 * slots * k, 1)
        stats = jnp.where(lanes < 2 * slots, stats, 0.0)
    else:
        stats = sum(message[slots + k].astype(f32) for k in range(3))
    return stats, pltpu.roll(stats, HEAD_WIDTH - slots, 1)


def flipped(value, flip):
    if not flip:
        return value
    ahead = pltpu.roll(value, HEAD_WIDTH - flip, 1)
    behind = pltpu.roll(value, flip, 1)
    return jnp.where((iota(HEADS, 1) & flip) == 0, ahead, behind)


def merged(mine, theirs, slots, flip):
    top, total = read_stats(mine, slots)
    other_top, other_total = (flipped(x, flip) for x in read_stats(theirs, slots))
    peak = jnp.maximum(top, other_top)
    share, other_share = jnp.exp(top - peak), jnp.exp(other_top - peak)
    total = share * total + other_share * other_total

    def acc(slot):
        return share[:, slot : slot + 1] * mine[slot].astype(f32) + other_share[
            :, slot : slot + 1
        ] * theirs[slot ^ flip].astype(f32)

    return peak, total, acc


def merge_kernel(mine, theirs, out, *, slots, flip):
    peak, total, acc = merged(mine, theirs, slots, flip)
    lanes = iota(HEADS, 1)
    stats = jnp.where(lanes < slots, peak, 0.0)
    stats = stats + pltpu.roll(jnp.where(lanes < slots, total, 0.0), slots, 1)
    write_stats(stats, out, slots)
    for slot in range(slots):
        out[slot] = acc(slot).astype(bf16)


def fresh_block(mine, theirs, me):
    slots = mine.shape[0] - 1
    second = me % 2 == 1
    first_group = iota(HEADS, 0) < GROUPED

    def by_head(rows, at):
        return jnp.where(first_group, rows[at : at + 1], rows[at + 1 : at + 2])

    q = mine[0].astype(f32)
    own, other = mine[slots].astype(f32), theirs[slots].astype(f32)
    own_score = jnp.sum(q * by_head(own, 0), axis=1, keepdims=True) * INV_ROOT
    other_score = jnp.sum(q * by_head(other, 0), axis=1, keepdims=True) * INV_ROOT
    other_score = jnp.where(second, other_score, floor_score)
    top = jnp.maximum(own_score, other_score)
    own_weight = jnp.exp(own_score - top).astype(bf16).astype(f32)
    other_weight = jnp.where(second, jnp.exp(other_score - top), 0.0).astype(bf16).astype(f32)
    acc = own_weight * by_head(own, 2) + other_weight * by_head(other, 2)
    return top, own_weight + other_weight, acc


def attend_kernel(after, lengths, mine, theirs, cache, keep, send, *, far):
    me = lax.axis_index("exp")
    sequences, block, _ = cache.shape
    rows = 2 * QUERY_HEADS
    first_group = (iota((rows, HEAD_WIDTH), 0) % QUERY_HEADS) < GROUPED
    positions = me * block + iota((rows, block), 1)
    lanes = iota(HEADS, 1)
    fresh = fresh_block(mine, theirs, me)
    stats = [jnp.zeros(HEADS, f32), jnp.zeros(HEADS, f32)]
    batch = 8 if sequences % 8 == 0 else 1
    for base in range(0, sequences, batch):
        slots = range(base, base + batch)
        where = [
            lax.shift_right_logical(me, 1)
            ^ ((distance_of(slot % far, far) >> 1) | (slot // far))
            for slot in slots
        ]
        scores, valid = [], []
        for slot, s in zip(slots, where):
            both = jnp.concatenate([mine[slot], theirs[slot]], axis=0)
            zero = jnp.zeros_like(both)
            wide = jnp.concatenate(
                [jnp.where(first_group, both, zero), jnp.where(first_group, zero, both)], axis=1
            )
            product = lax.dot_general(
                wide,
                cache[s, :, :KEY_VALUE_WIDTH],
                (((1,), (1,)), ((), ())),
                preferred_element_type=f32,
            )
            valid.append(positions < lengths[s])
            scores.append(jnp.where(valid[-1], product * INV_ROOT, floor_score))
        tops = [jnp.max(score, axis=1, keepdims=True) for score in scores]
        weights = [
            jnp.where(ok, jnp.exp(score - top), 0.0).astype(bf16)
            for ok, score, top in zip(valid, scores, tops)
        ]
        totals = [jnp.sum(weight.astype(f32), axis=1, keepdims=True) for weight in weights]
        accs = [
            jnp.dot(weight, cache[s, :, KEY_VALUE_WIDTH:], preferred_element_type=f32)
            for weight, s in zip(weights, where)
        ]
        for slot, top, total, acc in zip(slots, tops, totals, accs):
            acc = jnp.where(first_group, acc[:, :HEAD_WIDTH], acc[:, HEAD_WIDTH:])
            for k, part in enumerate((keep, send)):
                cut = slice(k * QUERY_HEADS, (k + 1) * QUERY_HEADS)
                t, z, a = top[cut], total[cut], acc[cut]
                if slot == 0 and k == 0:
                    peak = jnp.maximum(t, fresh[0])
                    old, young = jnp.exp(t - peak), jnp.exp(fresh[0] - peak)
                    t, z, a = peak, old * z + young * fresh[1], old * a + young * fresh[2]
                part[slot] = a.astype(bf16)
                stats[k] = jnp.where(lanes == slot, t, stats[k])
                stats[k] = jnp.where(lanes == sequences + slot, z, stats[k])
    for k, part in enumerate((keep, send)):
        write_stats(stats[k], part, sequences)


def token_kernel(after, mine, theirs, residuals, scale, hidden_out, normed_out):
    slots = residuals.shape[0]
    _, total, acc = merged(mine, theirs, slots, 1)
    inverse = 1.0 / jnp.where(iota(HEADS, 1) < slots, total, 1.0)
    for slot in range(slots):
        hidden = residuals[slot].astype(f32) + acc(slot) * inverse[:, slot : slot + 1]
        squares = jnp.sum(jnp.sum(hidden * hidden, axis=1, keepdims=True), axis=0, keepdims=True)
        normed = hidden * lax.rsqrt(squares / WIDTH + epsilon) * scale[...]
        if slot == 0:
            hidden_out[...] = hidden
        normed_out[slot] = normed.astype(bf16)


def dot_pair(value, factor, contract):
    high = value.astype(bf16)
    low = (value - high.astype(f32)).astype(bf16)
    both = lax.dot_general(
        jnp.concatenate([high, low], axis=0),
        factor,
        (((1,), (contract,)), ((), ())),
        preferred_element_type=f32,
    )
    return both[: value.shape[0]] + both[value.shape[0] :]


def expert_kernel(mine, theirs, gate_w, up_w, down_w, model, inner, out, *, far):
    me = lax.axis_index("exp")
    half = mine.shape[0]
    x = jnp.concatenate([mine[...].astype(f32), theirs[...].astype(f32)], axis=0)
    x = x.reshape(2 * half, WIDTH).astype(bf16)
    r = ADAPTER_RANK
    mixed = lax.dot_general(
        x, model[: 2 * r], (((1,), (1,)), ((), ())), preferred_element_type=f32
    )
    gate = jnp.dot(x, gate_w[...], preferred_element_type=f32)
    gate = gate + dot_pair(mixed[:, :r], inner[:, :r], 1)
    up = jnp.dot(x, up_w[...], preferred_element_type=f32)
    up = up + dot_pair(mixed[:, r:], inner[:, r : 2 * r], 1)
    act = (gate / (1.0 + jnp.exp(-gate)) * up).astype(bf16)
    lowered = jnp.dot(act, inner[:, 2 * r : 3 * r], preferred_element_type=f32)
    result = jnp.dot(act, down_w[...], preferred_element_type=f32)
    result = result + dot_pair(lowered, model[2 * r :], 0)
    for c in range(2):
        for y in range(2):
            for w in range(far):
                slot = (c * 2 + y) * far + w
                line = as_rows(result[slot : slot + 1], QUERY_HEADS)
                out[me ^ (distance_of(w, far) | 2 * y | c)] = line.astype(bf16)


def finish_kernel(hidden, got, choice, probability, out):
    p = probability[...]
    shares = p / jnp.sum(p, axis=1, keepdims=True)
    lanes = iota((1, HEAD_WIDTH), 1)
    gates = jnp.zeros((1, HEAD_WIDTH), f32)
    for k in range(p.shape[1]):
        gates = gates + jnp.where(choice[:, k : k + 1] == lanes, shares[:, k : k + 1], 0.0)
    gates = gates.astype(bf16).astype(f32)
    total = hidden[...]
    for e in range(got.shape[0]):
        total = total + gates[:, e : e + 1] * got[e].astype(f32)
    line = jnp.concatenate([total[j : j + 1] for j in range(QUERY_HEADS)], axis=1)
    out[...] = line.astype(bf16)


def lora_pack_kernel(after, model, inner, *outs):
    low, first = lax.axis_index("exp") % NEAR, lax.axis_index("grp") == 0
    ranks, split, most = model.shape[1], model.shape[1] // 2, outs[0].shape[1] - model.shape[1] // 2
    rest = inner.shape[1] - most
    for k, out in enumerate(outs):
        out[:, split:, ranks:] = jnp.zeros((out.shape[0], most, HEAD_WIDTH - ranks), out.dtype)
        for z in range(out.shape[0]):
            at = z * NEAR + (low ^ k)
            out[z, :split] = jnp.where(first, model[at, :split], model[at, split:])
            lower = inner[at, most:]
            if rest < most:
                pad = jnp.zeros((most - rest, ranks), out.dtype)
                lower = jnp.concatenate([lower, pad], axis=0)
            out[z, split:, :ranks] = jnp.where(first, inner[at, :most], lower)


def lora_turn_kernel(after, *refs):
    me = lax.axis_index("exp")
    low, high = me % NEAR, me // NEAR
    got, outs = refs[:NEAR], refs[NEAR:]
    for j, out in enumerate(outs):
        for k, ref in enumerate(got):
            out[low ^ k] = ref[high ^ j]


def lora_order_kernel(after, *refs):
    high = lax.axis_index("exp") // NEAR
    got, out = refs[:-1], refs[-1]
    for j, ref in enumerate(got):
        out[pl.ds((high ^ j) * NEAR, NEAR)] = ref[...]


def lora_join_kernel(mine, theirs, model, inner):
    first = lax.axis_index("grp") == 0
    split = model.shape[0] // 2
    most, width = mine.shape[1] - split, inner.shape[0] // mine.shape[0]
    for at in range(mine.shape[0]):
        own, other = mine[at], theirs[at]
        halves = jnp.where(first, own, other), jnp.where(first, other, own)
        columns = slice(at * HEAD_WIDTH, (at + 1) * HEAD_WIDTH)
        model[:split, columns] = halves[0][:split]
        model[split:, columns] = halves[1][:split]
        inner[at * width : at * width + most] = halves[0][split:]
        inner[at * width + most : (at + 1) * width] = halves[1][split : split + width - most]


def lora_near(adapter_model, adapter_hidden, n, marks):
    total, ranks, model_width = adapter_model.shape
    inner_width = adapter_hidden.shape[2]
    inner = jnp.transpose(adapter_hidden, (0, 2, 1))
    if model_width != HEAD_WIDTH or inner_width % 16 or lax.axis_size("grp") != 2:
        model = lax.all_to_all(adapter_model, "exp", split_axis=0, concat_axis=2, tiled=True)
        inner = lax.all_to_all(inner, "exp", split_axis=0, concat_axis=1, tiled=True)
        return [model[0], inner[0]], True
    far = n // NEAR
    block = (ranks // 2 + pad16(inner_width // 2), HEAD_WIDTH)
    packed = call(
        lora_pack_kernel,
        (shape((far,) + block, bf16),) * NEAR,
        [VMEM] * 3,
        marks[0],
        adapter_model,
        inner,
        nanos=FILL,
    )
    turned = call(
        lora_turn_kernel,
        (shape((NEAR,) + block, bf16),) * far,
        [VMEM] * (1 + NEAR),
        marks[3],
        packed[0],
        swap(hold(packed[1], marks[1]), n, 1),
        swap(packed[2], n, 2),
        swap(hold(packed[3], marks[1]), n, 3),
        nanos=FILL,
    )
    return turned, False


def lora_far(turned, n, marks):
    far = len(turned)
    rows = turned[0].shape[1]
    got = [turned[0], swap(turned[1], n, NEAR)]
    for j in range(2, far):
        got.append(swap(hold(turned[j], marks[j - 2]), n, j * NEAR))
    return call(
        lora_order_kernel,
        shape((n, rows, HEAD_WIDTH), bf16),
        [VMEM] * (1 + far),
        marks[far - 2],
        *got,
        nanos=FILL,
    )


def lora_join(ordered, inner_width):
    n = ordered.shape[0]
    return call(
        lora_join_kernel,
        (
            shape((3 * ADAPTER_RANK, n * HEAD_WIDTH), bf16),
            shape((n * inner_width, HEAD_WIDTH), bf16),
        ),
        [VMEM] * 2,
        ordered,
        lax.ppermute(ordered, "grp", [(0, 1), (1, 0)]),
    )


def body(
    resid,
    queries,
    incoming_key_value,
    key_value_cache,
    lengths,
    norm_scale_vector,
    expert_choice,
    router_probability,
    gate_weight,
    up_weight,
    down_weight,
    adapter_model,
    adapter_hidden,
):
    n = lax.axis_size("exp")
    far = n // NEAR

    slots = 2 * far
    first_inputs = (queries, resid)
    message = call(
        pack_kernel,
        shape((1,) + MESSAGE, bf16),
        [HBM] * 2,
        *[pltpu.with_memory_space_constraint(x, pltpu.HBM) for x in first_inputs],
        scratch=[pltpu.VMEM(x.shape, x.dtype) for x in first_inputs]
        + [pltpu.SemaphoreType.DMA((2,))],
        nanos=4000,
    )
    marks, distance = [message], n // 2
    while distance > 2:
        message = call(
            join_kernel,
            shape((2 * message.shape[0],) + MESSAGE, bf16),
            [VMEM] * 2,
            message,
            swap(message, n, distance),
        )
        marks.append(message)
        distance //= 2
    residuals, near = call(
        narrow_kernel,
        (shape((slots,) + HEADS, bf16), shape((slots + 1,) + HEADS, bf16)),
        [VMEM] * 3,
        message,
        swap(message, n, 2),
        incoming_key_value,
    )
    marks = marks[:3] + [near]
    turned, whole = lora_near(adapter_model, adapter_hidden, n, marks)
    next_near = swap(near, n, 1)
    partial = shape((slots + stat_tiles(slots),) + HEADS, bf16)
    keep, send = call(
        functools.partial(attend_kernel, far=far),
        (partial,) * 2,
        [VMEM, SMEM] + [VMEM] * 3,
        turned[0],
        lengths,
        near,
        next_near,
        key_value_cache,
        nanos=8000,
    )
    marks = [keep]
    theirs, flip, distance = swap(send, n, 1), 0, 2
    while distance < n:
        keep = call(
            functools.partial(merge_kernel, slots=slots, flip=flip),
            partial,
            [VMEM] * 2,
            keep,
            theirs,
        )
        marks.append(keep)
        if distance == n // 2:
            ordered = turned[0] if whole else lora_far(turned, n, marks)
        theirs = swap(keep, n, distance)
        flip = slots // distance
        distance *= 2
    hidden, normed = call(
        token_kernel,
        (shape(HEADS, f32), shape((slots,) + HEADS, bf16)),
        [VMEM] * 5,
        ordered,
        keep,
        theirs,
        residuals,
        norm_scale_vector.reshape(HEADS),
        nanos=4000,
    )
    model, inner = turned if whole else lora_join(ordered, adapter_hidden.shape[2])
    out = call(
        functools.partial(expert_kernel, far=far),
        shape((n,) + HEADS, bf16),
        [VMEM] * 7,
        normed,
        swap(normed, n, 1),
        gate_weight[0],
        up_weight[0],
        down_weight[0],
        model,
        inner,
        limit=32,
    )
    return call(
        finish_kernel,
        shape((1, WIDTH), bf16),
        [VMEM] * 4,
        hidden,
        lax.all_to_all(out, "exp", split_axis=0, concat_axis=0, tiled=True),
        expert_choice,
        router_probability,
    )


def solution(mesh):
    return jax.shard_map(
        body,
        mesh=mesh,
        in_specs=(
            P(("grp", "exp"), None),
            P(("grp", "exp"), None),
            P(("grp", "exp"), None),
            P("grp", "exp", None),
            P("grp"),
            P(),
            P(("grp", "exp"), None),
            P(("grp", "exp"), None),
            P("exp", None, None),
            P("exp", None, None),
            P("exp", None, None),
            P(None, None, "exp"),
            P(None, None, "exp"),
        ),
        out_specs=P(("grp", "exp"), None),
        check_vma=False,
    )
```

```python
import functools

import jax
import jax.numpy as jnp
from jax import lax
from jax.experimental import pallas as pl
from jax.experimental.pallas import tpu as pltpu
from jax.sharding import PartitionSpec as P

QUERY_HEADS = 16
KEY_VALUE_HEADS = 2
HEAD_WIDTH = 128
ADAPTER_RANK = 32
GROUPED = QUERY_HEADS // KEY_VALUE_HEADS
KEY_VALUE_WIDTH = KEY_VALUE_HEADS * HEAD_WIDTH
WIDTH = QUERY_HEADS * HEAD_WIDTH
INV_ROOT = HEAD_WIDTH ** (-0.5)
NEAR = 4
NEW_ROWS = 2 * KEY_VALUE_HEADS
HEADS = (QUERY_HEADS, HEAD_WIDTH)
MESSAGE = (2 * QUERY_HEADS, HEAD_WIDTH)

floor_score = -1e30
epsilon = 1e-06
FILL = 1000
TOKEN = 1500
MERGE = 1600
JOIN = 800

VMEM = pl.BlockSpec(memory_space=pltpu.VMEM)
SMEM = pl.BlockSpec(memory_space=pltpu.SMEM)
HBM = pl.BlockSpec(memory_space=pltpu.HBM)
shape = jax.ShapeDtypeStruct
bf16, f32 = jnp.bfloat16, jnp.float32


def call(kernel, shapes, specs, *args, limit=8, scratch=(), nanos=JOIN):
    return pl.pallas_call(
        kernel,
        out_shape=shapes,
        in_specs=specs,
        out_specs=jax.tree.map(lambda _: VMEM, shapes),
        scratch_shapes=scratch,
        cost_estimate=pl.CostEstimate(
            flops=nanos * 1000000, transcendentals=0, bytes_accessed=0
        ),
        compiler_params=pltpu.CompilerParams(vmem_limit_bytes=limit * 1024 * 1024),
    )(*args)


def hold_kernel(value, after, out):
    out[...] = value[...]


def hold(value, after):
    return call(
        hold_kernel, shape(value.shape, value.dtype), [VMEM] * 2, value, after, nanos=FILL
    )


def iota(dims, dim):
    return lax.broadcasted_iota(jnp.int32, dims, dim)


def as_rows(line, rows):
    return jnp.concatenate(
        [line[:, j * HEAD_WIDTH : (j + 1) * HEAD_WIDTH] for j in range(rows)], axis=0
    )


def swap(value, n, distance):
    return lax.ppermute(value, "exp", [(t, t ^ distance) for t in range(n)])


def distance_of(column, far):
    bits = far.bit_length() - 1
    return sum(NEAR << i for i in range(bits) if column >> (bits - 1 - i) & 1)


def pad16(rows):
    return -(-rows // 16) * 16


def stat_tiles(slots):
    return 1 if 6 * slots <= HEAD_WIDTH else 3


def pack_kernel(query, resid, out, q_in, r_in, sems):
    copies = [
        pltpu.make_async_copy(source, target, sems.at[k])
        for k, (source, target) in enumerate(((query, q_in), (resid, r_in)))
    ]
    for copy in copies:
        copy.start()
    for copy in copies:
        copy.wait()
    q = as_rows(q_in[...].astype(f32), QUERY_HEADS)
    r = as_rows(r_in[...].astype(f32), QUERY_HEADS)
    out[0] = jnp.concatenate([q, r], axis=0).astype(bf16)


def join_kernel(mine, theirs, out):
    half = mine.shape[0]
    out[:half] = mine[...]
    out[half:] = theirs[...]


def narrow_kernel(after, mine, theirs, new, residuals, out):
    half = mine.shape[0]
    for k, source in enumerate((mine, theirs)):
        for w in range(half):
            slot = k * half + w
            out[slot] = source[w, :QUERY_HEADS]
            residuals[slot] = source[w, QUERY_HEADS:]
    fresh = as_rows(new[...].astype(f32), NEW_ROWS)
    rest = jnp.zeros((QUERY_HEADS - NEW_ROWS, HEAD_WIDTH), f32)
    out[2 * half] = jnp.concatenate([fresh, rest], axis=0).astype(bf16)


def write_stats(stats, out, slots):
    parts = []
    for _ in range(3):
        part = stats.astype(bf16).astype(f32)
        parts.append(part)
        stats = stats - part
    if stat_tiles(slots) == 1:
        tile = parts[0]
        for k in (1, 2):
            tile = tile + pltpu.roll(parts[k], 2 * slots * k, 1)
        out[slots] = tile.astype(bf16)
    else:
        for k in range(3):
            out[slots + k] = parts[k].astype(bf16)


def read_stats(message, slots):
    if stat_tiles(slots) == 1:
        tile = message[slots].astype(f32)
        lanes = iota(HEADS, 1)
        stats = tile
        for k in (1, 2):
            stats = stats + pltpu.roll(tile, HEAD_WIDTH - 2 * slots * k, 1)
        stats = jnp.where(lanes < 2 * slots, stats, 0.0)
    else:
        stats = sum(message[slots + k].astype(f32) for k in range(3))
    return stats, pltpu.roll(stats, HEAD_WIDTH - slots, 1)


def flipped(value, flip):
    if not flip:
        return value
    ahead = pltpu.roll(value, HEAD_WIDTH - flip, 1)
    behind = pltpu.roll(value, flip, 1)
    return jnp.where((iota(HEADS, 1) & flip) == 0, ahead, behind)


def merged(mine, theirs, slots, flip):
    top, total = read_stats(mine, slots)
    other_top, other_total = (flipped(x, flip) for x in read_stats(theirs, slots))
    peak = jnp.maximum(top, other_top)
    share, other_share = jnp.exp(top - peak), jnp.exp(other_top - peak)
    total = share * total + other_share * other_total

    def acc(slot):
        return share[:, slot : slot + 1] * mine[slot].astype(f32) + other_share[
            :, slot : slot + 1
        ] * theirs[slot ^ flip].astype(f32)

    return peak, total, acc


def merge_kernel(after, mine, theirs, out, *, slots, flip):
    peak, total, acc = merged(mine, theirs, slots, flip)
    lanes = iota(HEADS, 1)
    stats = jnp.where(lanes < slots, peak, 0.0)
    stats = stats + pltpu.roll(jnp.where(lanes < slots, total, 0.0), slots, 1)
    write_stats(stats, out, slots)
    for slot in range(slots):
        out[slot] = acc(slot).astype(bf16)


def fresh_block(mine, theirs, me):
    slots = mine.shape[0] - 1
    second = me % 2 == 1
    first_group = iota(HEADS, 0) < GROUPED

    def by_head(rows, at):
        return jnp.where(first_group, rows[at : at + 1], rows[at + 1 : at + 2])

    q = mine[0].astype(f32)
    own, other = mine[slots].astype(f32), theirs[slots].astype(f32)
    own_score = jnp.sum(q * by_head(own, 0), axis=1, keepdims=True) * INV_ROOT
    other_score = jnp.sum(q * by_head(other, 0), axis=1, keepdims=True) * INV_ROOT
    other_score = jnp.where(second, other_score, floor_score)
    top = jnp.maximum(own_score, other_score)
    own_weight = jnp.exp(own_score - top).astype(bf16).astype(f32)
    other_weight = jnp.where(second, jnp.exp(other_score - top), 0.0).astype(bf16).astype(f32)
    acc = own_weight * by_head(own, 2) + other_weight * by_head(other, 2)
    return top, own_weight + other_weight, acc


def attend_kernel(lengths, mine, theirs, cache, keep, send, *, far):
    me = lax.axis_index("exp")
    sequences, block, _ = cache.shape
    rows = 2 * QUERY_HEADS
    first_group = (iota((rows, HEAD_WIDTH), 0) % QUERY_HEADS) < GROUPED
    positions = me * block + iota((rows, block), 1)
    lanes = iota(HEADS, 1)
    fresh = fresh_block(mine, theirs, me)
    stats = [jnp.zeros(HEADS, f32), jnp.zeros(HEADS, f32)]
    batch = 8 if sequences % 8 == 0 else 1
    for base in range(0, sequences, batch):
        slots = range(base, base + batch)
        where = [
            lax.shift_right_logical(me, 1)
            ^ ((distance_of(slot % far, far) >> 1) | (slot // far))
            for slot in slots
        ]
        scores, valid = [], []
        for slot, s in zip(slots, where):
            both = jnp.concatenate([mine[slot], theirs[slot]], axis=0)
            zero = jnp.zeros_like(both)
            wide = jnp.concatenate(
                [jnp.where(first_group, both, zero), jnp.where(first_group, zero, both)], axis=1
            )
            product = lax.dot_general(
                wide,
                cache[s, :, :KEY_VALUE_WIDTH],
                (((1,), (1,)), ((), ())),
                preferred_element_type=f32,
            )
            valid.append(positions < lengths[s])
            scores.append(jnp.where(valid[-1], product * INV_ROOT, floor_score))
        tops = [jnp.max(score, axis=1, keepdims=True) for score in scores]
        weights = [
            jnp.where(ok, jnp.exp(score - top), 0.0).astype(bf16)
            for ok, score, top in zip(valid, scores, tops)
        ]
        totals = [jnp.sum(weight.astype(f32), axis=1, keepdims=True) for weight in weights]
        accs = [
            jnp.dot(weight, cache[s, :, KEY_VALUE_WIDTH:], preferred_element_type=f32)
            for weight, s in zip(weights, where)
        ]
        for slot, top, total, acc in zip(slots, tops, totals, accs):
            acc = jnp.where(first_group, acc[:, :HEAD_WIDTH], acc[:, HEAD_WIDTH:])
            for k, part in enumerate((keep, send)):
                cut = slice(k * QUERY_HEADS, (k + 1) * QUERY_HEADS)
                t, z, a = top[cut], total[cut], acc[cut]
                if slot == 0 and k == 0:
                    peak = jnp.maximum(t, fresh[0])
                    old, young = jnp.exp(t - peak), jnp.exp(fresh[0] - peak)
                    t, z, a = peak, old * z + young * fresh[1], old * a + young * fresh[2]
                part[slot] = a.astype(bf16)
                stats[k] = jnp.where(lanes == slot, t, stats[k])
                stats[k] = jnp.where(lanes == sequences + slot, z, stats[k])
    for k, part in enumerate((keep, send)):
        write_stats(stats[k], part, sequences)


def token_kernel(mine, theirs, residuals, scale, hidden_out, normed_out):
    slots = residuals.shape[0]
    _, total, acc = merged(mine, theirs, slots, 1)
    inverse = 1.0 / jnp.where(iota(HEADS, 1) < slots, total, 1.0)
    for slot in range(slots):
        hidden = residuals[slot].astype(f32) + acc(slot) * inverse[:, slot : slot + 1]
        squares = jnp.sum(jnp.sum(hidden * hidden, axis=1, keepdims=True), axis=0, keepdims=True)
        normed = hidden * lax.rsqrt(squares / WIDTH + epsilon) * scale[...]
        if slot == 0:
            hidden_out[...] = hidden
        normed_out[slot] = normed.astype(bf16)


def dot_pair(value, factor, contract):
    high = value.astype(bf16)
    low = (value - high.astype(f32)).astype(bf16)
    both = lax.dot_general(
        jnp.concatenate([high, low], axis=0),
        factor,
        (((1,), (contract,)), ((), ())),
        preferred_element_type=f32,
    )
    return both[: value.shape[0]] + both[value.shape[0] :]


def expert_kernel(mine, theirs, gate_w, up_w, down_w, model, inner, out, *, far):
    me = lax.axis_index("exp")
    half = mine.shape[0]
    x = jnp.concatenate([mine[...].astype(f32), theirs[...].astype(f32)], axis=0)
    x = x.reshape(2 * half, WIDTH).astype(bf16)
    r = ADAPTER_RANK
    mixed = lax.dot_general(
        x, model[: 2 * r], (((1,), (1,)), ((), ())), preferred_element_type=f32
    )
    gate = jnp.dot(x, gate_w[...], preferred_element_type=f32)
    gate = gate + dot_pair(mixed[:, :r], inner[:, :r], 1)
    up = jnp.dot(x, up_w[...], preferred_element_type=f32)
    up = up + dot_pair(mixed[:, r:], inner[:, r : 2 * r], 1)
    act = (gate / (1.0 + jnp.exp(-gate)) * up).astype(bf16)
    lowered = jnp.dot(act, inner[:, 2 * r : 3 * r], preferred_element_type=f32)
    result = jnp.dot(act, down_w[...], preferred_element_type=f32)
    result = result + dot_pair(lowered, model[2 * r :], 0)
    for c in range(2):
        for y in range(2):
            for w in range(far):
                slot = (c * 2 + y) * far + w
                line = as_rows(result[slot : slot + 1], QUERY_HEADS)
                out[me ^ (distance_of(w, far) | 2 * y | c)] = line.astype(bf16)


def gate_kernel(after, choice, probability, out):
    p = probability[...]
    shares = p / jnp.sum(p, axis=1, keepdims=True)
    lanes = iota((1, HEAD_WIDTH), 1)
    gates = jnp.zeros((1, HEAD_WIDTH), f32)
    for k in range(p.shape[1]):
        gates = gates + jnp.where(choice[:, k : k + 1] == lanes, shares[:, k : k + 1], 0.0)
    out[...] = gates.astype(bf16).astype(f32)


def finish_kernel(hidden, got, gates, out):
    total = hidden[...]
    for e in range(got.shape[0]):
        total = total + gates[:, e : e + 1] * got[e].astype(f32)
    line = jnp.concatenate([total[j : j + 1] for j in range(QUERY_HEADS)], axis=1)
    out[...] = line.astype(bf16)


def lora_pack_kernel(after, model, inner, *outs):
    low, first = lax.axis_index("exp") % NEAR, lax.axis_index("grp") == 0
    ranks, split, most = model.shape[1], model.shape[1] // 2, outs[0].shape[1] - model.shape[1] // 2
    rest = inner.shape[1] - most
    for k, out in enumerate(outs):
        out[:, split:, ranks:] = jnp.zeros((out.shape[0], most, HEAD_WIDTH - ranks), out.dtype)
        for z in range(out.shape[0]):
            at = z * NEAR + (low ^ k)
            out[z, :split] = jnp.where(first, model[at, :split], model[at, split:])
            lower = inner[at, most:]
            if rest < most:
                pad = jnp.zeros((most - rest, ranks), out.dtype)
                lower = jnp.concatenate([lower, pad], axis=0)
            out[z, split:, :ranks] = jnp.where(first, inner[at, :most], lower)


def lora_turn_kernel(after, *refs):
    me = lax.axis_index("exp")
    low, high = me % NEAR, me // NEAR
    got, outs = refs[:NEAR], refs[NEAR:]
    for j, out in enumerate(outs):
        for k, ref in enumerate(got):
            out[low ^ k] = ref[high ^ j]


def lora_order_kernel(after, *refs):
    high = lax.axis_index("exp") // NEAR
    got, out = refs[:-1], refs[-1]
    for j, ref in enumerate(got):
        out[pl.ds((high ^ j) * NEAR, NEAR)] = ref[...]


def lora_join_kernel(mine, theirs, model, inner):
    first = lax.axis_index("grp") == 0
    split = model.shape[0] // 2
    most, width = mine.shape[1] - split, inner.shape[0] // mine.shape[0]
    for at in range(mine.shape[0]):
        own, other = mine[at], theirs[at]
        halves = jnp.where(first, own, other), jnp.where(first, other, own)
        columns = slice(at * HEAD_WIDTH, (at + 1) * HEAD_WIDTH)
        model[:split, columns] = halves[0][:split]
        model[split:, columns] = halves[1][:split]
        inner[at * width : at * width + most] = halves[0][split:]
        inner[at * width + most : (at + 1) * width] = halves[1][split : split + width - most]


def lora_near(adapter_model, adapter_hidden, n, marks):
    total, ranks, model_width = adapter_model.shape
    inner_width = adapter_hidden.shape[2]
    inner = jnp.transpose(adapter_hidden, (0, 2, 1))
    if model_width != HEAD_WIDTH or inner_width % 16 or lax.axis_size("grp") != 2:
        model = lax.all_to_all(adapter_model, "exp", split_axis=0, concat_axis=2, tiled=True)
        inner = lax.all_to_all(inner, "exp", split_axis=0, concat_axis=1, tiled=True)
        return [model[0], inner[0]], True
    far = n // NEAR
    block = (ranks // 2 + pad16(inner_width // 2), HEAD_WIDTH)
    packed = call(
        lora_pack_kernel,
        (shape((far,) + block, bf16),) * NEAR,
        [VMEM] * 3,
        marks[0],
        adapter_model,
        inner,
        nanos=FILL,
    )
    turned = call(
        lora_turn_kernel,
        (shape((NEAR,) + block, bf16),) * far,
        [VMEM] * (1 + NEAR),
        marks[2],
        packed[0],
        swap(hold(packed[1], marks[1]), n, 1),
        swap(packed[2], n, 2),
        swap(hold(packed[3], marks[1]), n, 3),
        nanos=FILL,
    )
    return turned, False


def lora_far_start(turned, n, after):
    arrived = [turned[0], swap(turned[1], n, NEAR)]
    for j in range(2, len(turned) - 1):
        arrived.append(swap(hold(turned[j], after), n, j * NEAR))
    return arrived


def lora_order(arrived, n, after):
    return call(
        lora_order_kernel,
        shape((n,) + arrived[0].shape[1:], bf16),
        [VMEM] * (1 + len(arrived)),
        after,
        *arrived,
        nanos=FILL,
    )


def lora_join(ordered, inner_width):
    n = ordered.shape[0]
    return call(
        lora_join_kernel,
        (
            shape((3 * ADAPTER_RANK, n * HEAD_WIDTH), bf16),
            shape((n * inner_width, HEAD_WIDTH), bf16),
        ),
        [VMEM] * 2,
        ordered,
        lax.ppermute(ordered, "grp", [(0, 1), (1, 0)]),
    )


def body(
    resid,
    queries,
    incoming_key_value,
    key_value_cache,
    lengths,
    norm_scale_vector,
    expert_choice,
    router_probability,
    gate_weight,
    up_weight,
    down_weight,
    adapter_model,
    adapter_hidden,
):
    n = lax.axis_size("exp")
    far = n // NEAR

    slots = 2 * far
    first_inputs = (queries, resid)
    message = call(
        pack_kernel,
        shape((1,) + MESSAGE, bf16),
        [HBM] * 2,
        *[pltpu.with_memory_space_constraint(x, pltpu.HBM) for x in first_inputs],
        scratch=[pltpu.VMEM(x.shape, x.dtype) for x in first_inputs]
        + [pltpu.SemaphoreType.DMA((2,))],
        nanos=4000,
    )
    marks, distance = [message], n // 2
    while distance > 2:
        message = call(
            join_kernel,
            shape((2 * message.shape[0],) + MESSAGE, bf16),
            [VMEM] * 2,
            message,
            swap(message, n, distance),
        )
        marks.append(message)
        distance //= 2
    turned, whole = lora_near(adapter_model, adapter_hidden, n, marks)
    residuals, near = call(
        narrow_kernel,
        (shape((slots,) + HEADS, bf16), shape((slots + 1,) + HEADS, bf16)),
        [VMEM] * 4,
        turned[0],
        message,
        swap(message, n, 2),
        incoming_key_value,
    )
    if not whole:
        arrived = lora_far_start(turned, n, near)
    next_near = swap(near, n, 1)
    partial = shape((slots + stat_tiles(slots),) + HEADS, bf16)
    keep, send = call(
        functools.partial(attend_kernel, far=far),
        (partial,) * 2,
        [SMEM] + [VMEM] * 3,
        lengths,
        near,
        next_near,
        key_value_cache,
        nanos=8000,
    )
    gates = call(
        gate_kernel,
        shape((1, HEAD_WIDTH), f32),
        [VMEM] * 3,
        keep,
        expert_choice,
        router_probability,
    )
    theirs, flip, distance, after = swap(send, n, 1), 0, 2, gates
    while distance < n:
        keep = call(
            functools.partial(merge_kernel, slots=slots, flip=flip),
            partial,
            [VMEM] * 3,
            after,
            keep,
            theirs,
            nanos=MERGE,
        )
        if distance == 2 and not whole:
            last = hold(turned[-1], keep)
            arrived.append(swap(last, n, n - NEAR))
        if distance == n // 4:
            after = turned[0] if whole else lora_order(arrived, n, keep)
        theirs = swap(keep, n, distance)
        flip = slots // distance
        distance *= 2
    ordered = after
    hidden, normed = call(
        token_kernel,
        (shape(HEADS, f32), shape((slots,) + HEADS, bf16)),
        [VMEM] * 4,
        keep,
        theirs,
        residuals,
        norm_scale_vector.reshape(HEADS),
        nanos=TOKEN,
    )
    model, inner = turned if whole else lora_join(ordered, adapter_hidden.shape[2])
    out = call(
        functools.partial(expert_kernel, far=far),
        shape((n,) + HEADS, bf16),
        [VMEM] * 7,
        normed,
        swap(normed, n, 1),
        gate_weight[0],
        up_weight[0],
        down_weight[0],
        model,
        inner,
        limit=32,
    )
    return call(
        finish_kernel,
        shape((1, WIDTH), bf16),
        [VMEM] * 3,
        hidden,
        lax.all_to_all(out, "exp", split_axis=0, concat_axis=0, tiled=True),
        gates,
    )


def solution(mesh):
    return jax.shard_map(
        body,
        mesh=mesh,
        in_specs=(
            P(("grp", "exp"), None),
            P(("grp", "exp"), None),
            P(("grp", "exp"), None),
            P("grp", "exp", None),
            P("grp"),
            P(),
            P(("grp", "exp"), None),
            P(("grp", "exp"), None),
            P("exp", None, None),
            P("exp", None, None),
            P("exp", None, None),
            P(None, None, "exp"),
            P(None, None, "exp"),
        ),
        out_specs=P(("grp", "exp"), None),
        check_vma=False,
    )
```

```python
import functools

import jax
import jax.numpy as jnp
from jax import lax
from jax.experimental import pallas as pl
from jax.experimental.pallas import tpu as pltpu
from jax.sharding import PartitionSpec as P

QUERY_HEADS = 16
KEY_VALUE_HEADS = 2
HEAD_WIDTH = 128
ADAPTER_RANK = 32
GROUPED = QUERY_HEADS // KEY_VALUE_HEADS
KEY_VALUE_WIDTH = KEY_VALUE_HEADS * HEAD_WIDTH
WIDTH = QUERY_HEADS * HEAD_WIDTH
INV_ROOT = HEAD_WIDTH ** (-0.5)
NEAR = 4
NEW_ROWS = 2 * KEY_VALUE_HEADS
HEADS = (QUERY_HEADS, HEAD_WIDTH)
MESSAGE = (2 * QUERY_HEADS, HEAD_WIDTH)

floor_score = -1e30
epsilon = 1e-06
FILL = 20
TOKEN = 1500
MERGE = 1600
JOIN = 1600

VMEM = pl.BlockSpec(memory_space=pltpu.VMEM)
SMEM = pl.BlockSpec(memory_space=pltpu.SMEM)
HBM = pl.BlockSpec(memory_space=pltpu.HBM)
shape = jax.ShapeDtypeStruct
bf16, f32 = jnp.bfloat16, jnp.float32


def call(kernel, shapes, specs, *args, limit=8, scratch=(), nanos=JOIN):
    return pl.pallas_call(
        kernel,
        out_shape=shapes,
        in_specs=specs,
        out_specs=jax.tree.map(lambda _: VMEM, shapes),
        scratch_shapes=scratch,
        cost_estimate=pl.CostEstimate(
            flops=nanos * 1000000, transcendentals=0, bytes_accessed=0
        ),
        compiler_params=pltpu.CompilerParams(vmem_limit_bytes=limit * 1024 * 1024),
    )(*args)


def hold_kernel(value, after, out):
    out[...] = value[...]


def hold(value, after):
    return call(
        hold_kernel, shape(value.shape, value.dtype), [VMEM] * 2, value, after, nanos=FILL
    )


def iota(dims, dim):
    return lax.broadcasted_iota(jnp.int32, dims, dim)


def as_rows(line, rows):
    return jnp.concatenate(
        [line[:, j * HEAD_WIDTH : (j + 1) * HEAD_WIDTH] for j in range(rows)], axis=0
    )


def swap(value, n, distance):
    return lax.ppermute(value, "exp", [(t, t ^ distance) for t in range(n)])


def distance_of(column, far):
    bits = far.bit_length() - 1
    return sum(NEAR << i for i in range(bits) if column >> (bits - 1 - i) & 1)


def pad16(rows):
    return -(-rows // 16) * 16


def stat_tiles(slots):
    return 1 if 6 * slots <= HEAD_WIDTH else 3


def pack_kernel(query, resid, out, q_in, r_in, sems):
    copies = [
        pltpu.make_async_copy(source, target, sems.at[k])
        for k, (source, target) in enumerate(((query, q_in), (resid, r_in)))
    ]
    for copy in copies:
        copy.start()
    for copy in copies:
        copy.wait()
    q = as_rows(q_in[...].astype(f32), QUERY_HEADS)
    r = as_rows(r_in[...].astype(f32), QUERY_HEADS)
    out[0] = jnp.concatenate([q, r], axis=0).astype(bf16)


def join_kernel(mine, theirs, out):
    half = mine.shape[0]
    out[:half] = mine[...]
    out[half:] = theirs[...]


def narrow_kernel(after, mine, theirs, new, residuals, out):
    half = mine.shape[0]
    for k, source in enumerate((mine, theirs)):
        for w in range(half):
            slot = k * half + w
            out[slot] = source[w, :QUERY_HEADS]
            residuals[slot] = source[w, QUERY_HEADS:]
    fresh = as_rows(new[...].astype(f32), NEW_ROWS)
    rest = jnp.zeros((QUERY_HEADS - NEW_ROWS, HEAD_WIDTH), f32)
    out[2 * half] = jnp.concatenate([fresh, rest], axis=0).astype(bf16)


def write_stats(stats, out, slots):
    parts = []
    for _ in range(3):
        part = stats.astype(bf16).astype(f32)
        parts.append(part)
        stats = stats - part
    if stat_tiles(slots) == 1:
        tile = parts[0]
        for k in (1, 2):
            tile = tile + pltpu.roll(parts[k], 2 * slots * k, 1)
        out[slots] = tile.astype(bf16)
    else:
        for k in range(3):
            out[slots + k] = parts[k].astype(bf16)


def read_stats(message, slots):
    if stat_tiles(slots) == 1:
        tile = message[slots].astype(f32)
        lanes = iota(HEADS, 1)
        stats = tile
        for k in (1, 2):
            stats = stats + pltpu.roll(tile, HEAD_WIDTH - 2 * slots * k, 1)
        stats = jnp.where(lanes < 2 * slots, stats, 0.0)
    else:
        stats = sum(message[slots + k].astype(f32) for k in range(3))
    return stats, pltpu.roll(stats, HEAD_WIDTH - slots, 1)


def flipped(value, flip):
    if not flip:
        return value
    ahead = pltpu.roll(value, HEAD_WIDTH - flip, 1)
    behind = pltpu.roll(value, flip, 1)
    return jnp.where((iota(HEADS, 1) & flip) == 0, ahead, behind)


def merged(mine, theirs, slots, flip):
    top, total = read_stats(mine, slots)
    other_top, other_total = (flipped(x, flip) for x in read_stats(theirs, slots))
    peak = jnp.maximum(top, other_top)
    share, other_share = jnp.exp(top - peak), jnp.exp(other_top - peak)
    total = share * total + other_share * other_total

    def acc(slot):
        return share[:, slot : slot + 1] * mine[slot].astype(f32) + other_share[
            :, slot : slot + 1
        ] * theirs[slot ^ flip].astype(f32)

    return peak, total, acc


def merge_kernel(after, mine, theirs, out, *, slots, flip):
    peak, total, acc = merged(mine, theirs, slots, flip)
    lanes = iota(HEADS, 1)
    stats = jnp.where(lanes < slots, peak, 0.0)
    stats = stats + pltpu.roll(jnp.where(lanes < slots, total, 0.0), slots, 1)
    write_stats(stats, out, slots)
    for slot in range(slots):
        out[slot] = acc(slot).astype(bf16)


def fresh_block(mine, theirs, me):
    slots = mine.shape[0] - 1
    second = me % 2 == 1
    first_group = iota(HEADS, 0) < GROUPED

    def by_head(rows, at):
        return jnp.where(first_group, rows[at : at + 1], rows[at + 1 : at + 2])

    q = mine[0].astype(f32)
    own, other = mine[slots].astype(f32), theirs[slots].astype(f32)
    own_score = jnp.sum(q * by_head(own, 0), axis=1, keepdims=True) * INV_ROOT
    other_score = jnp.sum(q * by_head(other, 0), axis=1, keepdims=True) * INV_ROOT
    other_score = jnp.where(second, other_score, floor_score)
    top = jnp.maximum(own_score, other_score)
    own_weight = jnp.exp(own_score - top).astype(bf16).astype(f32)
    other_weight = jnp.where(second, jnp.exp(other_score - top), 0.0).astype(bf16).astype(f32)
    acc = own_weight * by_head(own, 2) + other_weight * by_head(other, 2)
    return top, own_weight + other_weight, acc


def attend_kernel(after, lengths, mine, theirs, cache, keep, send, *, far):
    me = lax.axis_index("exp")
    sequences, block, _ = cache.shape
    rows = 2 * QUERY_HEADS
    first_group = (iota((rows, HEAD_WIDTH), 0) % QUERY_HEADS) < GROUPED
    positions = me * block + iota((rows, block), 1)
    lanes = iota(HEADS, 1)
    fresh = fresh_block(mine, theirs, me)
    stats = [jnp.zeros(HEADS, f32), jnp.zeros(HEADS, f32)]
    batch = 8 if sequences % 8 == 0 else 1
    for base in range(0, sequences, batch):
        slots = range(base, base + batch)
        where = [
            lax.shift_right_logical(me, 1)
            ^ ((distance_of(slot % far, far) >> 1) | (slot // far))
            for slot in slots
        ]
        scores, valid = [], []
        for slot, s in zip(slots, where):
            both = jnp.concatenate([mine[slot], theirs[slot]], axis=0)
            zero = jnp.zeros_like(both)
            wide = jnp.concatenate(
                [jnp.where(first_group, both, zero), jnp.where(first_group, zero, both)], axis=1
            )
            product = lax.dot_general(
                wide,
                cache[s, :, :KEY_VALUE_WIDTH],
                (((1,), (1,)), ((), ())),
                preferred_element_type=f32,
            )
            valid.append(positions < lengths[s])
            scores.append(jnp.where(valid[-1], product * INV_ROOT, floor_score))
        tops = [jnp.max(score, axis=1, keepdims=True) for score in scores]
        weights = [
            jnp.where(ok, jnp.exp(score - top), 0.0).astype(bf16)
            for ok, score, top in zip(valid, scores, tops)
        ]
        totals = [jnp.sum(weight.astype(f32), axis=1, keepdims=True) for weight in weights]
        accs = [
            jnp.dot(weight, cache[s, :, KEY_VALUE_WIDTH:], preferred_element_type=f32)
            for weight, s in zip(weights, where)
        ]
        for slot, top, total, acc in zip(slots, tops, totals, accs):
            acc = jnp.where(first_group, acc[:, :HEAD_WIDTH], acc[:, HEAD_WIDTH:])
            for k, part in enumerate((keep, send)):
                cut = slice(k * QUERY_HEADS, (k + 1) * QUERY_HEADS)
                t, z, a = top[cut], total[cut], acc[cut]
                if slot == 0 and k == 0:
                    peak = jnp.maximum(t, fresh[0])
                    old, young = jnp.exp(t - peak), jnp.exp(fresh[0] - peak)
                    t, z, a = peak, old * z + young * fresh[1], old * a + young * fresh[2]
                part[slot] = a.astype(bf16)
                stats[k] = jnp.where(lanes == slot, t, stats[k])
                stats[k] = jnp.where(lanes == sequences + slot, z, stats[k])
    for k, part in enumerate((keep, send)):
        write_stats(stats[k], part, sequences)


def token_kernel(mine, theirs, residuals, scale, hidden_out, normed_out):
    slots = residuals.shape[0]
    _, total, acc = merged(mine, theirs, slots, 1)
    inverse = 1.0 / jnp.where(iota(HEADS, 1) < slots, total, 1.0)
    for slot in range(slots):
        hidden = residuals[slot].astype(f32) + acc(slot) * inverse[:, slot : slot + 1]
        squares = jnp.sum(jnp.sum(hidden * hidden, axis=1, keepdims=True), axis=0, keepdims=True)
        normed = hidden * lax.rsqrt(squares / WIDTH + epsilon) * scale[...]
        if slot == 0:
            hidden_out[...] = hidden
        normed_out[slot] = normed.astype(bf16)


def dot_pair(value, factor, contract):
    high = value.astype(bf16)
    low = (value - high.astype(f32)).astype(bf16)
    both = lax.dot_general(
        jnp.concatenate([high, low], axis=0),
        factor,
        (((1,), (contract,)), ((), ())),
        preferred_element_type=f32,
    )
    return both[: value.shape[0]] + both[value.shape[0] :]


def expert_kernel(mine, theirs, gate_w, up_w, down_w, model, inner, out, *, far):
    me = lax.axis_index("exp")
    half = mine.shape[0]
    x = jnp.concatenate([mine[...].astype(f32), theirs[...].astype(f32)], axis=0)
    x = x.reshape(2 * half, WIDTH).astype(bf16)
    r = ADAPTER_RANK
    mixed = lax.dot_general(
        x, model[: 2 * r], (((1,), (1,)), ((), ())), preferred_element_type=f32
    )
    gate = jnp.dot(x, gate_w[...], preferred_element_type=f32)
    gate = gate + dot_pair(mixed[:, :r], inner[:, :r], 1)
    up = jnp.dot(x, up_w[...], preferred_element_type=f32)
    up = up + dot_pair(mixed[:, r:], inner[:, r : 2 * r], 1)
    act = (gate / (1.0 + jnp.exp(-gate)) * up).astype(bf16)
    lowered = jnp.dot(act, inner[:, 2 * r : 3 * r], preferred_element_type=f32)
    result = jnp.dot(act, down_w[...], preferred_element_type=f32)
    result = result + dot_pair(lowered, model[2 * r :], 0)
    for c in range(2):
        for y in range(2):
            for w in range(far):
                slot = (c * 2 + y) * far + w
                line = as_rows(result[slot : slot + 1], QUERY_HEADS)
                out[me ^ (distance_of(w, far) | 2 * y | c)] = line.astype(bf16)


def gate_kernel(after, choice, probability, out):
    p = probability[...]
    shares = p / jnp.sum(p, axis=1, keepdims=True)
    lanes = iota((1, HEAD_WIDTH), 1)
    gates = jnp.zeros((1, HEAD_WIDTH), f32)
    for k in range(p.shape[1]):
        gates = gates + jnp.where(choice[:, k : k + 1] == lanes, shares[:, k : k + 1], 0.0)
    out[...] = gates.astype(bf16).astype(f32)


def finish_kernel(hidden, got, gates, out):
    total = hidden[...]
    for e in range(got.shape[0]):
        total = total + gates[:, e : e + 1] * got[e].astype(f32)
    line = jnp.concatenate([total[j : j + 1] for j in range(QUERY_HEADS)], axis=1)
    out[...] = line.astype(bf16)


def without(index, bit):
    return (index // (2 * bit)) * bit + index % bit


def lora_pack_kernel(after, model, inner, keep, send, *, bit):
    me, first = lax.axis_index("exp"), lax.axis_index("grp") == 0
    ranks, split = model.shape[1], model.shape[1] // 2
    most = keep.shape[1] - split
    rest = inner.shape[1] - most
    for out in (keep, send):
        out[:, split:, ranks:] = jnp.zeros((out.shape[0], most, HEAD_WIDTH - ranks), out.dtype)
    for d in range(model.shape[0]):
        out, at, source = (send if d & bit else keep), without(d, bit), me ^ d
        out[at, :split] = jnp.where(first, model[source, :split], model[source, split:])
        lower = inner[source, most:]
        if rest < most:
            pad = jnp.zeros((most - rest, ranks), out.dtype)
            lower = jnp.concatenate([lower, pad], axis=0)
        out[at, split:, :ranks] = jnp.where(first, inner[source, :most], lower)


def lora_turn_kernel(after, kept, got, keep, send, *, bit, following):
    for d in range(2 * kept.shape[0]):
        value = (got if d & bit else kept)[without(d, bit)]
        (send if d & following else keep)[without(d, following)] = value


def lora_spread_kernel(after, kept, got, *outs, bit):
    for d in range(2 * kept.shape[0]):
        outs[d // NEAR][d % NEAR] = (got if d & bit else kept)[without(d, bit)]


def lora_order_kernel(after, *refs):
    me = lax.axis_index("exp")
    got, out = refs[:-1], refs[-1]
    for j, ref in enumerate(got):
        for l in range(NEAR):
            out[me ^ (j * NEAR + l)] = ref[l]


def lora_join_kernel(mine, theirs, model, inner):
    first = lax.axis_index("grp") == 0
    split = model.shape[0] // 2
    most, width = mine.shape[1] - split, inner.shape[0] // mine.shape[0]
    for at in range(mine.shape[0]):
        own, other = mine[at], theirs[at]
        halves = jnp.where(first, own, other), jnp.where(first, other, own)
        columns = slice(at * HEAD_WIDTH, (at + 1) * HEAD_WIDTH)
        model[:split, columns] = halves[0][:split]
        model[split:, columns] = halves[1][:split]
        inner[at * width : at * width + most] = halves[0][split:]
        inner[at * width + most : (at + 1) * width] = halves[1][split : split + width - most]


def lora_near(adapter_model, adapter_hidden, n, marks):
    total, ranks, model_width = adapter_model.shape
    inner_width = adapter_hidden.shape[2]
    inner = jnp.transpose(adapter_hidden, (0, 2, 1))
    if model_width != HEAD_WIDTH or inner_width % 16 or lax.axis_size("grp") != 2:
        model = lax.all_to_all(adapter_model, "exp", split_axis=0, concat_axis=2, tiled=True)
        inner = lax.all_to_all(inner, "exp", split_axis=0, concat_axis=1, tiled=True)
        return [model[0], inner[0]], True
    far = n // NEAR
    block = (ranks // 2 + pad16(inner_width // 2), HEAD_WIDTH)
    halves = (shape((n // 2,) + block, bf16),) * 2
    keep, send = call(
        functools.partial(lora_pack_kernel, bit=2),
        halves,
        [VMEM] * 3,
        marks[0],
        adapter_model,
        inner,
        nanos=FILL,
    )
    keep, send = call(
        functools.partial(lora_turn_kernel, bit=2, following=1),
        halves,
        [VMEM] * 3,
        marks[1],
        keep,
        swap(send, n, 2),
        nanos=FILL,
    )
    spread = call(
        functools.partial(lora_spread_kernel, bit=1),
        (shape((NEAR,) + block, bf16),) * (n // NEAR),
        [VMEM] * 3,
        marks[2],
        keep,
        swap(send, n, 1),
        nanos=FILL,
    )
    return spread, False


def lora_far_start(turned, n, after):
    arrived = [turned[0], swap(turned[1], n, NEAR)]
    for j in range(2, len(turned) - 1):
        arrived.append(swap(hold(turned[j], after), n, j * NEAR))
    return arrived


def lora_order(arrived, n, after):
    return call(
        lora_order_kernel,
        shape((n,) + arrived[0].shape[1:], bf16),
        [VMEM] * (1 + len(arrived)),
        after,
        *arrived,
        nanos=FILL,
    )


def lora_join(ordered, inner_width):
    n = ordered.shape[0]
    return call(
        lora_join_kernel,
        (
            shape((3 * ADAPTER_RANK, n * HEAD_WIDTH), bf16),
            shape((n * inner_width, HEAD_WIDTH), bf16),
        ),
        [VMEM] * 2,
        ordered,
        lax.ppermute(ordered, "grp", [(0, 1), (1, 0)]),
    )


def body(
    resid,
    queries,
    incoming_key_value,
    key_value_cache,
    lengths,
    norm_scale_vector,
    expert_choice,
    router_probability,
    gate_weight,
    up_weight,
    down_weight,
    adapter_model,
    adapter_hidden,
):
    n = lax.axis_size("exp")
    far = n // NEAR

    slots = 2 * far
    first_inputs = (queries, resid)
    message = call(
        pack_kernel,
        shape((1,) + MESSAGE, bf16),
        [HBM] * 2,
        *[pltpu.with_memory_space_constraint(x, pltpu.HBM) for x in first_inputs],
        scratch=[pltpu.VMEM(x.shape, x.dtype) for x in first_inputs]
        + [pltpu.SemaphoreType.DMA((2,))],
        nanos=4000,
    )
    marks, distance = [message], n // 2
    while distance > 2:
        message = call(
            join_kernel,
            shape((2 * message.shape[0],) + MESSAGE, bf16),
            [VMEM] * 2,
            message,
            swap(message, n, distance),
        )
        marks.append(message)
        distance //= 2
    turned, whole = lora_near(adapter_model, adapter_hidden, n, marks)
    residuals, near = call(
        narrow_kernel,
        (shape((slots,) + HEADS, bf16), shape((slots + 1,) + HEADS, bf16)),
        [VMEM] * 4,
        turned[0],
        message,
        swap(message, n, 2),
        incoming_key_value,
    )
    if not whole:
        arrived = lora_far_start(turned, n, near)
    next_near = swap(near, n, 1)
    partial = shape((slots + stat_tiles(slots),) + HEADS, bf16)
    keep, send = call(
        functools.partial(attend_kernel, far=far),
        (partial,) * 2,
        [VMEM, SMEM] + [VMEM] * 3,
        turned[0] if whole else arrived[1],
        lengths,
        near,
        next_near,
        key_value_cache,
        nanos=8000,
    )
    gates = call(
        gate_kernel,
        shape((1, HEAD_WIDTH), f32),
        [VMEM] * 3,
        keep,
        expert_choice,
        router_probability,
    )
    theirs, flip, distance = swap(send, n, 1), 0, 2
    after = gates if whole else arrived[-1]
    while distance < n:
        keep = call(
            functools.partial(merge_kernel, slots=slots, flip=flip),
            partial,
            [VMEM] * 3,
            after,
            keep,
            theirs,
            nanos=MERGE,
        )
        if distance == 2 and not whole:
            last = hold(turned[-1], keep)
            arrived.append(swap(last, n, n - NEAR))
        if distance == n // 4:
            after = turned[0] if whole else lora_order(arrived, n, keep)
        theirs = swap(keep, n, distance)
        flip = slots // distance
        distance *= 2
    ordered = after
    hidden, normed = call(
        token_kernel,
        (shape(HEADS, f32), shape((slots,) + HEADS, bf16)),
        [VMEM] * 4,
        keep,
        theirs,
        residuals,
        norm_scale_vector.reshape(HEADS),
        nanos=TOKEN,
    )
    model, inner = turned if whole else lora_join(ordered, adapter_hidden.shape[2])
    out = call(
        functools.partial(expert_kernel, far=far),
        shape((n,) + HEADS, bf16),
        [VMEM] * 7,
        normed,
        swap(normed, n, 1),
        gate_weight[0],
        up_weight[0],
        down_weight[0],
        model,
        inner,
        limit=32,
    )
    return call(
        finish_kernel,
        shape((1, WIDTH), bf16),
        [VMEM] * 3,
        hidden,
        lax.all_to_all(out, "exp", split_axis=0, concat_axis=0, tiled=True),
        gates,
    )


def solution(mesh):
    return jax.shard_map(
        body,
        mesh=mesh,
        in_specs=(
            P(("grp", "exp"), None),
            P(("grp", "exp"), None),
            P(("grp", "exp"), None),
            P("grp", "exp", None),
            P("grp"),
            P(),
            P(("grp", "exp"), None),
            P(("grp", "exp"), None),
            P("exp", None, None),
            P("exp", None, None),
            P("exp", None, None),
            P(None, None, "exp"),
            P(None, None, "exp"),
        ),
        out_specs=P(("grp", "exp"), None),
        check_vma=False,
    )
```

```python
import functools

import jax
import jax.numpy as jnp
from jax import lax
from jax.experimental import pallas as pl
from jax.experimental.pallas import tpu as pltpu
from jax.sharding import PartitionSpec as P

QUERY_HEADS = 16
KEY_VALUE_HEADS = 2
HEAD_WIDTH = 128
ADAPTER_RANK = 32
GROUPED = QUERY_HEADS // KEY_VALUE_HEADS
KEY_VALUE_WIDTH = KEY_VALUE_HEADS * HEAD_WIDTH
WIDTH = QUERY_HEADS * HEAD_WIDTH
INV_ROOT = HEAD_WIDTH ** (-0.5)
NEAR = 4
NEW_ROWS = 2 * KEY_VALUE_HEADS
HEADS = (QUERY_HEADS, HEAD_WIDTH)
MESSAGE = (2 * QUERY_HEADS, HEAD_WIDTH)

floor_score = -1e30
epsilon = 1e-06
FILL = 20
TOKEN = 800
MERGE = 2500
JOIN = 1600

VMEM = pl.BlockSpec(memory_space=pltpu.VMEM)
SMEM = pl.BlockSpec(memory_space=pltpu.SMEM)
HBM = pl.BlockSpec(memory_space=pltpu.HBM)
shape = jax.ShapeDtypeStruct
bf16, f32 = jnp.bfloat16, jnp.float32


def call(kernel, shapes, specs, *args, limit=8, scratch=(), nanos=JOIN):
    return pl.pallas_call(
        kernel,
        out_shape=shapes,
        in_specs=specs,
        out_specs=jax.tree.map(lambda _: VMEM, shapes),
        scratch_shapes=scratch,
        cost_estimate=pl.CostEstimate(
            flops=nanos * 1000000, transcendentals=0, bytes_accessed=0
        ),
        compiler_params=pltpu.CompilerParams(vmem_limit_bytes=limit * 1024 * 1024),
    )(*args)


def hold_kernel(value, after, out):
    out[...] = value[...]


def hold(value, after):
    return call(
        hold_kernel, shape(value.shape, value.dtype), [VMEM] * 2, value, after, nanos=FILL
    )


def iota(dims, dim):
    return lax.broadcasted_iota(jnp.int32, dims, dim)


def as_rows(line, rows):
    return jnp.concatenate(
        [line[:, j * HEAD_WIDTH : (j + 1) * HEAD_WIDTH] for j in range(rows)], axis=0
    )


def swap(value, n, distance):
    return lax.ppermute(value, "exp", [(t, t ^ distance) for t in range(n)])


def distance_of(column, far):
    bits = far.bit_length() - 1
    return sum(NEAR << i for i in range(bits) if column >> (bits - 1 - i) & 1)


def pad16(rows):
    return -(-rows // 16) * 16


def stat_tiles(slots):
    return 1 if 6 * slots <= HEAD_WIDTH else 3


def pack_kernel(query, resid, out, q_in, r_in, sems):
    copies = [
        pltpu.make_async_copy(source, target, sems.at[k])
        for k, (source, target) in enumerate(((query, q_in), (resid, r_in)))
    ]
    for copy in copies:
        copy.start()
    for copy in copies:
        copy.wait()
    q = as_rows(q_in[...].astype(f32), QUERY_HEADS)
    r = as_rows(r_in[...].astype(f32), QUERY_HEADS)
    out[0] = jnp.concatenate([q, r], axis=0).astype(bf16)


def join_kernel(mine, theirs, out):
    half = mine.shape[0]
    out[:half] = mine[...]
    out[half:] = theirs[...]


def narrow_kernel(after, mine, theirs, new, residuals, out):
    half = mine.shape[0]
    for k, source in enumerate((mine, theirs)):
        for w in range(half):
            slot = k * half + w
            out[slot] = source[w, :QUERY_HEADS]
            residuals[slot] = source[w, QUERY_HEADS:]
    fresh = as_rows(new[...].astype(f32), NEW_ROWS)
    rest = jnp.zeros((QUERY_HEADS - NEW_ROWS, HEAD_WIDTH), f32)
    out[2 * half] = jnp.concatenate([fresh, rest], axis=0).astype(bf16)


def write_stats(stats, out, slots):
    parts = []
    for _ in range(3):
        part = stats.astype(bf16).astype(f32)
        parts.append(part)
        stats = stats - part
    if stat_tiles(slots) == 1:
        tile = parts[0]
        for k in (1, 2):
            tile = tile + pltpu.roll(parts[k], 2 * slots * k, 1)
        out[slots] = tile.astype(bf16)
    else:
        for k in range(3):
            out[slots + k] = parts[k].astype(bf16)


def read_stats(message, slots):
    if stat_tiles(slots) == 1:
        tile = message[slots].astype(f32)
        lanes = iota(HEADS, 1)
        stats = tile
        for k in (1, 2):
            stats = stats + pltpu.roll(tile, HEAD_WIDTH - 2 * slots * k, 1)
        stats = jnp.where(lanes < 2 * slots, stats, 0.0)
    else:
        stats = sum(message[slots + k].astype(f32) for k in range(3))
    return stats, pltpu.roll(stats, HEAD_WIDTH - slots, 1)


def flipped(value, flip):
    if not flip:
        return value
    ahead = pltpu.roll(value, HEAD_WIDTH - flip, 1)
    behind = pltpu.roll(value, flip, 1)
    return jnp.where((iota(HEADS, 1) & flip) == 0, ahead, behind)


def merged(mine, theirs, slots, flip):
    top, total = read_stats(mine, slots)
    other_top, other_total = (flipped(x, flip) for x in read_stats(theirs, slots))
    peak = jnp.maximum(top, other_top)
    share, other_share = jnp.exp(top - peak), jnp.exp(other_top - peak)
    total = share * total + other_share * other_total

    def acc(slot):
        return share[:, slot : slot + 1] * mine[slot].astype(f32) + other_share[
            :, slot : slot + 1
        ] * theirs[slot ^ flip].astype(f32)

    return peak, total, acc


def merge_kernel(after, mine, theirs, out, *, slots, flip):
    peak, total, acc = merged(mine, theirs, slots, flip)
    lanes = iota(HEADS, 1)
    stats = jnp.where(lanes < slots, peak, 0.0)
    stats = stats + pltpu.roll(jnp.where(lanes < slots, total, 0.0), slots, 1)
    write_stats(stats, out, slots)
    for slot in range(slots):
        out[slot] = acc(slot).astype(bf16)


def fresh_block(mine, theirs, me):
    slots = mine.shape[0] - 1
    second = me % 2 == 1
    first_group = iota(HEADS, 0) < GROUPED

    def by_head(rows, at):
        return jnp.where(first_group, rows[at : at + 1], rows[at + 1 : at + 2])

    q = mine[0].astype(f32)
    own, other = mine[slots].astype(f32), theirs[slots].astype(f32)
    own_score = jnp.sum(q * by_head(own, 0), axis=1, keepdims=True) * INV_ROOT
    other_score = jnp.sum(q * by_head(other, 0), axis=1, keepdims=True) * INV_ROOT
    other_score = jnp.where(second, other_score, floor_score)
    top = jnp.maximum(own_score, other_score)
    own_weight = jnp.exp(own_score - top).astype(bf16).astype(f32)
    other_weight = jnp.where(second, jnp.exp(other_score - top), 0.0).astype(bf16).astype(f32)
    acc = own_weight * by_head(own, 2) + other_weight * by_head(other, 2)
    return top, own_weight + other_weight, acc


def attend_kernel(after, lengths, mine, theirs, cache, keep, send, *, far):
    me = lax.axis_index("exp")
    sequences, block, _ = cache.shape
    rows = 2 * QUERY_HEADS
    first_group = (iota((rows, HEAD_WIDTH), 0) % QUERY_HEADS) < GROUPED
    positions = me * block + iota((rows, block), 1)
    lanes = iota(HEADS, 1)
    fresh = fresh_block(mine, theirs, me)
    stats = [jnp.zeros(HEADS, f32), jnp.zeros(HEADS, f32)]
    batch = 8 if sequences % 8 == 0 else 1
    for base in range(0, sequences, batch):
        slots = range(base, base + batch)
        where = [
            lax.shift_right_logical(me, 1)
            ^ ((distance_of(slot % far, far) >> 1) | (slot // far))
            for slot in slots
        ]
        scores, valid = [], []
        for slot, s in zip(slots, where):
            both = jnp.concatenate([mine[slot], theirs[slot]], axis=0)
            zero = jnp.zeros_like(both)
            wide = jnp.concatenate(
                [jnp.where(first_group, both, zero), jnp.where(first_group, zero, both)], axis=1
            )
            product = lax.dot_general(
                wide,
                cache[s, :, :KEY_VALUE_WIDTH],
                (((1,), (1,)), ((), ())),
                preferred_element_type=f32,
            )
            valid.append(positions < lengths[s])
            scores.append(jnp.where(valid[-1], product * INV_ROOT, floor_score))
        tops = [jnp.max(score, axis=1, keepdims=True) for score in scores]
        weights = [
            jnp.where(ok, jnp.exp(score - top), 0.0).astype(bf16)
            for ok, score, top in zip(valid, scores, tops)
        ]
        totals = [jnp.sum(weight.astype(f32), axis=1, keepdims=True) for weight in weights]
        accs = [
            jnp.dot(weight, cache[s, :, KEY_VALUE_WIDTH:], preferred_element_type=f32)
            for weight, s in zip(weights, where)
        ]
        for slot, top, total, acc in zip(slots, tops, totals, accs):
            acc = jnp.where(first_group, acc[:, :HEAD_WIDTH], acc[:, HEAD_WIDTH:])
            for k, part in enumerate((keep, send)):
                cut = slice(k * QUERY_HEADS, (k + 1) * QUERY_HEADS)
                t, z, a = top[cut], total[cut], acc[cut]
                if slot == 0 and k == 0:
                    peak = jnp.maximum(t, fresh[0])
                    old, young = jnp.exp(t - peak), jnp.exp(fresh[0] - peak)
                    t, z, a = peak, old * z + young * fresh[1], old * a + young * fresh[2]
                part[slot] = a.astype(bf16)
                stats[k] = jnp.where(lanes == slot, t, stats[k])
                stats[k] = jnp.where(lanes == sequences + slot, z, stats[k])
    for k, part in enumerate((keep, send)):
        write_stats(stats[k], part, sequences)


def token_kernel(mine, theirs, residuals, scale, hidden_out, normed_out):
    slots = residuals.shape[0]
    _, total, acc = merged(mine, theirs, slots, 1)
    inverse = 1.0 / jnp.where(iota(HEADS, 1) < slots, total, 1.0)
    for slot in range(slots):
        hidden = residuals[slot].astype(f32) + acc(slot) * inverse[:, slot : slot + 1]
        squares = jnp.sum(jnp.sum(hidden * hidden, axis=1, keepdims=True), axis=0, keepdims=True)
        normed = hidden * lax.rsqrt(squares / WIDTH + epsilon) * scale[...]
        if slot == 0:
            hidden_out[...] = hidden
        normed_out[slot] = normed.astype(bf16)


def dot_pair(value, factor, contract):
    high = value.astype(bf16)
    low = (value - high.astype(f32)).astype(bf16)
    both = lax.dot_general(
        jnp.concatenate([high, low], axis=0),
        factor,
        (((1,), (contract,)), ((), ())),
        preferred_element_type=f32,
    )
    return both[: value.shape[0]] + both[value.shape[0] :]


def expert_kernel(mine, theirs, gate_w, up_w, down_w, model, inner, out, *, far):
    me = lax.axis_index("exp")
    half = mine.shape[0]
    x = jnp.concatenate([mine[...].astype(f32), theirs[...].astype(f32)], axis=0)
    x = x.reshape(2 * half, WIDTH).astype(bf16)
    r = ADAPTER_RANK
    mixed = lax.dot_general(
        x, model[: 2 * r], (((1,), (1,)), ((), ())), preferred_element_type=f32
    )
    gate = jnp.dot(x, gate_w[...], preferred_element_type=f32)
    gate = gate + dot_pair(mixed[:, :r], inner[:, :r], 1)
    up = jnp.dot(x, up_w[...], preferred_element_type=f32)
    up = up + dot_pair(mixed[:, r:], inner[:, r : 2 * r], 1)
    act = (gate / (1.0 + jnp.exp(-gate)) * up).astype(bf16)
    lowered = jnp.dot(act, inner[:, 2 * r : 3 * r], preferred_element_type=f32)
    result = jnp.dot(act, down_w[...], preferred_element_type=f32)
    result = result + dot_pair(lowered, model[2 * r :], 0)
    for c in range(2):
        for y in range(2):
            for w in range(far):
                slot = (c * 2 + y) * far + w
                line = as_rows(result[slot : slot + 1], QUERY_HEADS)
                out[me ^ (distance_of(w, far) | 2 * y | c)] = line.astype(bf16)


def gate_kernel(after, choice, probability, out):
    p = probability[...]
    shares = p / jnp.sum(p, axis=1, keepdims=True)
    lanes = iota((1, HEAD_WIDTH), 1)
    gates = jnp.zeros((1, HEAD_WIDTH), f32)
    for k in range(p.shape[1]):
        gates = gates + jnp.where(choice[:, k : k + 1] == lanes, shares[:, k : k + 1], 0.0)
    out[...] = gates.astype(bf16).astype(f32)


def finish_kernel(hidden, got, gates, out):
    total = hidden[...]
    for e in range(got.shape[0]):
        total = total + gates[:, e : e + 1] * got[e].astype(f32)
    line = jnp.concatenate([total[j : j + 1] for j in range(QUERY_HEADS)], axis=1)
    out[...] = line.astype(bf16)


def without(index, bit):
    return (index // (2 * bit)) * bit + index % bit


def lora_pack_kernel(after, model, inner, keep, send, *, bit):
    me, first = lax.axis_index("exp"), lax.axis_index("grp") == 0
    ranks, split = model.shape[1], model.shape[1] // 2
    most = keep.shape[1] - split
    rest = inner.shape[1] - most
    for out in (keep, send):
        out[:, split:, ranks:] = jnp.zeros((out.shape[0], most, HEAD_WIDTH - ranks), out.dtype)
    for d in range(model.shape[0]):
        out, at, source = (send if d & bit else keep), without(d, bit), me ^ d
        out[at, :split] = jnp.where(first, model[source, :split], model[source, split:])
        lower = inner[source, most:]
        if rest < most:
            pad = jnp.zeros((most - rest, ranks), out.dtype)
            lower = jnp.concatenate([lower, pad], axis=0)
        out[at, split:, :ranks] = jnp.where(first, inner[source, :most], lower)


def lora_turn_kernel(after, kept, got, keep, send, *, bit, following):
    for d in range(2 * kept.shape[0]):
        value = (got if d & bit else kept)[without(d, bit)]
        (send if d & following else keep)[without(d, following)] = value


def lora_spread_kernel(after, kept, got, *outs, bit):
    for d in range(2 * kept.shape[0]):
        outs[d // NEAR][d % NEAR] = (got if d & bit else kept)[without(d, bit)]


def lora_order_kernel(after, *refs):
    me = lax.axis_index("exp")
    got, out = refs[:-1], refs[-1]
    for j, ref in enumerate(got):
        for l in range(NEAR):
            out[me ^ (j * NEAR + l)] = ref[l]


def lora_join_kernel(mine, theirs, model, inner):
    first = lax.axis_index("grp") == 0
    split = model.shape[0] // 2
    most, width = mine.shape[1] - split, inner.shape[0] // mine.shape[0]
    for at in range(mine.shape[0]):
        own, other = mine[at], theirs[at]
        halves = jnp.where(first, own, other), jnp.where(first, other, own)
        columns = slice(at * HEAD_WIDTH, (at + 1) * HEAD_WIDTH)
        model[:split, columns] = halves[0][:split]
        model[split:, columns] = halves[1][:split]
        inner[at * width : at * width + most] = halves[0][split:]
        inner[at * width + most : (at + 1) * width] = halves[1][split : split + width - most]


def lora_near(adapter_model, adapter_hidden, n, marks):
    total, ranks, model_width = adapter_model.shape
    inner_width = adapter_hidden.shape[2]
    inner = jnp.transpose(adapter_hidden, (0, 2, 1))
    if model_width != HEAD_WIDTH or inner_width % 16 or lax.axis_size("grp") != 2:
        model = lax.all_to_all(adapter_model, "exp", split_axis=0, concat_axis=2, tiled=True)
        inner = lax.all_to_all(inner, "exp", split_axis=0, concat_axis=1, tiled=True)
        return [model[0], inner[0]], True
    far = n // NEAR
    block = (ranks // 2 + pad16(inner_width // 2), HEAD_WIDTH)
    halves = (shape((n // 2,) + block, bf16),) * 2
    keep, send = call(
        functools.partial(lora_pack_kernel, bit=2),
        halves,
        [VMEM] * 3,
        marks[0],
        adapter_model,
        inner,
        nanos=FILL,
    )
    keep, send = call(
        functools.partial(lora_turn_kernel, bit=2, following=1),
        halves,
        [VMEM] * 3,
        marks[1],
        keep,
        swap(send, n, 2),
        nanos=FILL,
    )
    spread = call(
        functools.partial(lora_spread_kernel, bit=1),
        (shape((NEAR,) + block, bf16),) * (n // NEAR),
        [VMEM] * 3,
        marks[2],
        keep,
        swap(send, n, 1),
        nanos=FILL,
    )
    return spread, False


def lora_far_start(turned, n, after):
    arrived = [turned[0], swap(turned[1], n, NEAR)]
    for j in range(2, len(turned) - 1):
        arrived.append(swap(hold(turned[j], after), n, j * NEAR))
    return arrived


def lora_order(arrived, n, after):
    return call(
        lora_order_kernel,
        shape((n,) + arrived[0].shape[1:], bf16),
        [VMEM] * (1 + len(arrived)),
        after,
        *arrived,
        nanos=FILL,
    )


def lora_join(ordered, inner_width):
    n = ordered.shape[0]
    return call(
        lora_join_kernel,
        (
            shape((3 * ADAPTER_RANK, n * HEAD_WIDTH), bf16),
            shape((n * inner_width, HEAD_WIDTH), bf16),
        ),
        [VMEM] * 2,
        ordered,
        lax.ppermute(ordered, "grp", [(0, 1), (1, 0)]),
    )


def body(
    resid,
    queries,
    incoming_key_value,
    key_value_cache,
    lengths,
    norm_scale_vector,
    expert_choice,
    router_probability,
    gate_weight,
    up_weight,
    down_weight,
    adapter_model,
    adapter_hidden,
):
    n = lax.axis_size("exp")
    far = n // NEAR

    slots = 2 * far
    first_inputs = (queries, resid)
    message = call(
        pack_kernel,
        shape((1,) + MESSAGE, bf16),
        [HBM] * 2,
        *[pltpu.with_memory_space_constraint(x, pltpu.HBM) for x in first_inputs],
        scratch=[pltpu.VMEM(x.shape, x.dtype) for x in first_inputs]
        + [pltpu.SemaphoreType.DMA((2,))],
        nanos=4000,
    )
    marks, distance = [message], n // 2
    while distance > 2:
        message = call(
            join_kernel,
            shape((2 * message.shape[0],) + MESSAGE, bf16),
            [VMEM] * 2,
            message,
            swap(message, n, distance),
        )
        marks.append(message)
        distance //= 2
    turned, whole = lora_near(adapter_model, adapter_hidden, n, marks)
    residuals, near = call(
        narrow_kernel,
        (shape((slots,) + HEADS, bf16), shape((slots + 1,) + HEADS, bf16)),
        [VMEM] * 4,
        turned[0],
        message,
        swap(message, n, 2),
        incoming_key_value,
    )
    if not whole:
        arrived = lora_far_start(turned, n, near)
    next_near = swap(near, n, 1)
    partial = shape((slots + stat_tiles(slots),) + HEADS, bf16)
    keep, send = call(
        functools.partial(attend_kernel, far=far),
        (partial,) * 2,
        [VMEM, SMEM] + [VMEM] * 3,
        turned[0] if whole else arrived[1],
        lengths,
        near,
        next_near,
        key_value_cache,
        nanos=8000,
    )
    gates = call(
        gate_kernel,
        shape((1, HEAD_WIDTH), f32),
        [VMEM] * 3,
        keep,
        expert_choice,
        router_probability,
    )
    theirs, flip, distance = swap(send, n, 1), 0, 2
    after = gates
    while distance < n:
        keep = call(
            functools.partial(merge_kernel, slots=slots, flip=flip),
            partial,
            [VMEM] * 3,
            after,
            keep,
            theirs,
            nanos=MERGE,
        )
        if distance == 2 and not whole:
            after = arrived[-1]
            last = hold(turned[-1], keep)
            arrived.append(swap(last, n, n - NEAR))
        if distance == n // 4:
            after = turned[0] if whole else lora_order(arrived, n, keep)
        theirs = swap(keep, n, distance)
        flip = slots // distance
        distance *= 2
    ordered = after
    hidden, normed = call(
        token_kernel,
        (shape(HEADS, f32), shape((slots,) + HEADS, bf16)),
        [VMEM] * 4,
        keep,
        theirs,
        residuals,
        norm_scale_vector.reshape(HEADS),
        nanos=TOKEN,
    )
    model, inner = turned if whole else lora_join(ordered, adapter_hidden.shape[2])
    out = call(
        functools.partial(expert_kernel, far=far),
        shape((n,) + HEADS, bf16),
        [VMEM] * 7,
        normed,
        swap(normed, n, 1),
        gate_weight[0],
        up_weight[0],
        down_weight[0],
        model,
        inner,
        limit=32,
    )
    return call(
        finish_kernel,
        shape((1, WIDTH), bf16),
        [VMEM] * 3,
        hidden,
        lax.all_to_all(out, "exp", split_axis=0, concat_axis=0, tiled=True),
        gates,
    )


def solution(mesh):
    return jax.shard_map(
        body,
        mesh=mesh,
        in_specs=(
            P(("grp", "exp"), None),
            P(("grp", "exp"), None),
            P(("grp", "exp"), None),
            P("grp", "exp", None),
            P("grp"),
            P(),
            P(("grp", "exp"), None),
            P(("grp", "exp"), None),
            P("exp", None, None),
            P("exp", None, None),
            P("exp", None, None),
            P(None, None, "exp"),
            P(None, None, "exp"),
        ),
        out_specs=P(("grp", "exp"), None),
        check_vma=False,
    )
```

```python
import functools

import jax
import jax.numpy as jnp
from jax import lax
from jax.experimental import pallas as pl
from jax.experimental.pallas import tpu as pltpu
from jax.sharding import PartitionSpec as P

QUERY_HEADS = 16
KEY_VALUE_HEADS = 2
HEAD_WIDTH = 128
ADAPTER_RANK = 32
GROUPED = QUERY_HEADS // KEY_VALUE_HEADS
KEY_VALUE_WIDTH = KEY_VALUE_HEADS * HEAD_WIDTH
WIDTH = QUERY_HEADS * HEAD_WIDTH
INV_ROOT = HEAD_WIDTH ** (-0.5)
NEAR = 4
NEW_ROWS = 2 * KEY_VALUE_HEADS
HEADS = (QUERY_HEADS, HEAD_WIDTH)
MESSAGE = (2 * QUERY_HEADS, HEAD_WIDTH)

floor_score = -1e30
epsilon = 1e-06
FILL = 20
TOKEN = 800
MERGE = 2500
JOIN = 1600

VMEM = pl.BlockSpec(memory_space=pltpu.VMEM)
SMEM = pl.BlockSpec(memory_space=pltpu.SMEM)
HBM = pl.BlockSpec(memory_space=pltpu.HBM)
shape = jax.ShapeDtypeStruct
bf16, f32 = jnp.bfloat16, jnp.float32


def call(kernel, shapes, specs, *args, limit=8, scratch=(), nanos=JOIN):
    return pl.pallas_call(
        kernel,
        out_shape=shapes,
        in_specs=specs,
        out_specs=jax.tree.map(lambda _: VMEM, shapes),
        scratch_shapes=scratch,
        cost_estimate=pl.CostEstimate(
            flops=nanos * 1000000, transcendentals=0, bytes_accessed=0
        ),
        compiler_params=pltpu.CompilerParams(vmem_limit_bytes=limit * 1024 * 1024),
    )(*args)


def hold_kernel(value, after, out):
    out[...] = value[...]


def hold(value, after):
    return call(
        hold_kernel, shape(value.shape, value.dtype), [VMEM] * 2, value, after, nanos=FILL
    )


def iota(dims, dim):
    return lax.broadcasted_iota(jnp.int32, dims, dim)


def as_rows(line, rows):
    return jnp.concatenate(
        [line[:, j * HEAD_WIDTH : (j + 1) * HEAD_WIDTH] for j in range(rows)], axis=0
    )


def swap(value, n, distance):
    return lax.ppermute(value, "exp", [(t, t ^ distance) for t in range(n)])


def distance_of(column, far):
    bits = far.bit_length() - 1
    return sum(NEAR << i for i in range(bits) if column >> (bits - 1 - i) & 1)


def pad16(rows):
    return -(-rows // 16) * 16


def stat_tiles(slots):
    return 1 if 6 * slots <= HEAD_WIDTH else 3


def pack_kernel(query, resid, out, q_in, r_in, sems):
    copies = [
        pltpu.make_async_copy(source, target, sems.at[k])
        for k, (source, target) in enumerate(((query, q_in), (resid, r_in)))
    ]
    for copy in copies:
        copy.start()
    for copy in copies:
        copy.wait()
    q = as_rows(q_in[...].astype(f32), QUERY_HEADS)
    r = as_rows(r_in[...].astype(f32), QUERY_HEADS)
    out[0] = jnp.concatenate([q, r], axis=0).astype(bf16)


def join_kernel(mine, theirs, out):
    half = mine.shape[0]
    out[:half] = mine[...]
    out[half:] = theirs[...]


def narrow_kernel(after, mine, theirs, new, residuals, out):
    half = mine.shape[0]
    for k, source in enumerate((mine, theirs)):
        for w in range(half):
            slot = k * half + w
            out[slot] = source[w, :QUERY_HEADS]
            residuals[slot] = source[w, QUERY_HEADS:]
    fresh = as_rows(new[...].astype(f32), NEW_ROWS)
    rest = jnp.zeros((QUERY_HEADS - NEW_ROWS, HEAD_WIDTH), f32)
    out[2 * half] = jnp.concatenate([fresh, rest], axis=0).astype(bf16)


def write_stats(stats, out, slots):
    parts = []
    for _ in range(3):
        part = stats.astype(bf16).astype(f32)
        parts.append(part)
        stats = stats - part
    if stat_tiles(slots) == 1:
        tile = parts[0]
        for k in (1, 2):
            tile = tile + pltpu.roll(parts[k], 2 * slots * k, 1)
        out[slots] = tile.astype(bf16)
    else:
        for k in range(3):
            out[slots + k] = parts[k].astype(bf16)


def read_stats(message, slots):
    if stat_tiles(slots) == 1:
        tile = message[slots].astype(f32)
        lanes = iota(HEADS, 1)
        stats = tile
        for k in (1, 2):
            stats = stats + pltpu.roll(tile, HEAD_WIDTH - 2 * slots * k, 1)
        stats = jnp.where(lanes < 2 * slots, stats, 0.0)
    else:
        stats = sum(message[slots + k].astype(f32) for k in range(3))
    return stats, pltpu.roll(stats, HEAD_WIDTH - slots, 1)


def flipped(value, flip):
    if not flip:
        return value
    ahead = pltpu.roll(value, HEAD_WIDTH - flip, 1)
    behind = pltpu.roll(value, flip, 1)
    return jnp.where((iota(HEADS, 1) & flip) == 0, ahead, behind)


def merged(mine, theirs, slots, flip):
    top, total = read_stats(mine, slots)
    other_top, other_total = (flipped(x, flip) for x in read_stats(theirs, slots))
    peak = jnp.maximum(top, other_top)
    share, other_share = jnp.exp(top - peak), jnp.exp(other_top - peak)
    total = share * total + other_share * other_total

    def acc(slot):
        return share[:, slot : slot + 1] * mine[slot].astype(f32) + other_share[
            :, slot : slot + 1
        ] * theirs[slot ^ flip].astype(f32)

    return peak, total, acc


def merge_kernel(after, mine, theirs, out, *, slots, flip):
    peak, total, acc = merged(mine, theirs, slots, flip)
    lanes = iota(HEADS, 1)
    stats = jnp.where(lanes < slots, peak, 0.0)
    stats = stats + pltpu.roll(jnp.where(lanes < slots, total, 0.0), slots, 1)
    write_stats(stats, out, slots)
    for slot in range(slots):
        out[slot] = acc(slot).astype(bf16)


def fresh_block(mine, theirs, me):
    slots = mine.shape[0] - 1
    second = me % 2 == 1
    first_group = iota(HEADS, 0) < GROUPED

    def by_head(rows, at):
        return jnp.where(first_group, rows[at : at + 1], rows[at + 1 : at + 2])

    q = mine[0].astype(f32)
    own, other = mine[slots].astype(f32), theirs[slots].astype(f32)
    own_score = jnp.sum(q * by_head(own, 0), axis=1, keepdims=True) * INV_ROOT
    other_score = jnp.sum(q * by_head(other, 0), axis=1, keepdims=True) * INV_ROOT
    other_score = jnp.where(second, other_score, floor_score)
    top = jnp.maximum(own_score, other_score)
    own_weight = jnp.exp(own_score - top).astype(bf16).astype(f32)
    other_weight = jnp.where(second, jnp.exp(other_score - top), 0.0).astype(bf16).astype(f32)
    acc = own_weight * by_head(own, 2) + other_weight * by_head(other, 2)
    return top, own_weight + other_weight, acc


def attend_kernel(after, lengths, mine, theirs, cache, keep, send, *, far):
    me = lax.axis_index("exp")
    sequences, block, _ = cache.shape
    rows = 2 * QUERY_HEADS
    first_group = (iota((rows, HEAD_WIDTH), 0) % QUERY_HEADS) < GROUPED
    positions = me * block + iota((rows, block), 1)
    lanes = iota(HEADS, 1)
    fresh = fresh_block(mine, theirs, me)
    stats = [jnp.zeros(HEADS, f32), jnp.zeros(HEADS, f32)]
    batch = 8 if sequences % 8 == 0 else 1
    for base in range(0, sequences, batch):
        slots = range(base, base + batch)
        where = [
            lax.shift_right_logical(me, 1)
            ^ ((distance_of(slot % far, far) >> 1) | (slot // far))
            for slot in slots
        ]
        scores, valid = [], []
        for slot, s in zip(slots, where):
            both = jnp.concatenate([mine[slot], theirs[slot]], axis=0)
            zero = jnp.zeros_like(both)
            wide = jnp.concatenate(
                [jnp.where(first_group, both, zero), jnp.where(first_group, zero, both)], axis=1
            )
            product = lax.dot_general(
                wide,
                cache[s, :, :KEY_VALUE_WIDTH],
                (((1,), (1,)), ((), ())),
                preferred_element_type=f32,
            )
            valid.append(positions < lengths[s])
            scores.append(jnp.where(valid[-1], product * INV_ROOT, floor_score))
        tops = [jnp.max(score, axis=1, keepdims=True) for score in scores]
        weights = [
            jnp.where(ok, jnp.exp(score - top), 0.0).astype(bf16)
            for ok, score, top in zip(valid, scores, tops)
        ]
        totals = [jnp.sum(weight.astype(f32), axis=1, keepdims=True) for weight in weights]
        accs = [
            jnp.dot(weight, cache[s, :, KEY_VALUE_WIDTH:], preferred_element_type=f32)
            for weight, s in zip(weights, where)
        ]
        for slot, top, total, acc in zip(slots, tops, totals, accs):
            acc = jnp.where(first_group, acc[:, :HEAD_WIDTH], acc[:, HEAD_WIDTH:])
            for k, part in enumerate((keep, send)):
                cut = slice(k * QUERY_HEADS, (k + 1) * QUERY_HEADS)
                t, z, a = top[cut], total[cut], acc[cut]
                if slot == 0 and k == 0:
                    peak = jnp.maximum(t, fresh[0])
                    old, young = jnp.exp(t - peak), jnp.exp(fresh[0] - peak)
                    t, z, a = peak, old * z + young * fresh[1], old * a + young * fresh[2]
                part[slot] = a.astype(bf16)
                stats[k] = jnp.where(lanes == slot, t, stats[k])
                stats[k] = jnp.where(lanes == sequences + slot, z, stats[k])
    for k, part in enumerate((keep, send)):
        write_stats(stats[k], part, sequences)


def token_kernel(mine, theirs, residuals, scale, hidden_out, normed_out):
    slots = residuals.shape[0]
    _, total, acc = merged(mine, theirs, slots, 1)
    inverse = 1.0 / jnp.where(iota(HEADS, 1) < slots, total, 1.0)
    for slot in range(slots):
        hidden = residuals[slot].astype(f32) + acc(slot) * inverse[:, slot : slot + 1]
        squares = jnp.sum(jnp.sum(hidden * hidden, axis=1, keepdims=True), axis=0, keepdims=True)
        normed = hidden * lax.rsqrt(squares / WIDTH + epsilon) * scale[...]
        if slot == 0:
            hidden_out[...] = hidden
        normed_out[slot] = normed.astype(bf16)


def dot_pair(value, factor, contract):
    high = value.astype(bf16)
    low = (value - high.astype(f32)).astype(bf16)
    both = lax.dot_general(
        jnp.concatenate([high, low], axis=0),
        factor,
        (((1,), (contract,)), ((), ())),
        preferred_element_type=f32,
    )
    return both[: value.shape[0]] + both[value.shape[0] :]


def expert_kernel(mine, theirs, gate_w, up_w, down_w, model, inner, out, *, far):
    me = lax.axis_index("exp")
    half = mine.shape[0]
    x = jnp.concatenate([mine[...].astype(f32), theirs[...].astype(f32)], axis=0)
    x = x.reshape(2 * half, WIDTH).astype(bf16)
    r = ADAPTER_RANK
    mixed = lax.dot_general(
        x, model[: 2 * r], (((1,), (1,)), ((), ())), preferred_element_type=f32
    )
    gate = jnp.dot(x, gate_w[...], preferred_element_type=f32)
    gate = gate + dot_pair(mixed[:, :r], inner[:, :r], 1)
    up = jnp.dot(x, up_w[...], preferred_element_type=f32)
    up = up + dot_pair(mixed[:, r:], inner[:, r : 2 * r], 1)
    act = (gate / (1.0 + jnp.exp(-gate)) * up).astype(bf16)
    lowered = jnp.dot(act, inner[:, 2 * r : 3 * r], preferred_element_type=f32)
    result = jnp.dot(act, down_w[...], preferred_element_type=f32)
    result = result + dot_pair(lowered, model[2 * r :], 0)
    for c in range(2):
        for y in range(2):
            for w in range(far):
                slot = (c * 2 + y) * far + w
                line = as_rows(result[slot : slot + 1], QUERY_HEADS)
                out[me ^ (distance_of(w, far) | 2 * y | c)] = line.astype(bf16)


def gate_kernel(after, choice, probability, out):
    p = probability[...]
    shares = p / jnp.sum(p, axis=1, keepdims=True)
    lanes = iota((1, HEAD_WIDTH), 1)
    gates = jnp.zeros((1, HEAD_WIDTH), f32)
    for k in range(p.shape[1]):
        gates = gates + jnp.where(choice[:, k : k + 1] == lanes, shares[:, k : k + 1], 0.0)
    out[...] = gates.astype(bf16).astype(f32)


def finish_kernel(hidden, got, gates, out):
    total = hidden[...]
    for e in range(got.shape[0]):
        total = total + gates[:, e : e + 1] * got[e].astype(f32)
    line = jnp.concatenate([total[j : j + 1] for j in range(QUERY_HEADS)], axis=1)
    out[...] = line.astype(bf16)


def without(index, bit):
    return (index // (2 * bit)) * bit + index % bit


def lora_pack_kernel(after, model, inner, keep, send, *, bit):
    me, first = lax.axis_index("exp"), lax.axis_index("grp") == 0
    ranks, split = model.shape[1], model.shape[1] // 2
    most = keep.shape[1] - split
    rest = inner.shape[1] - most
    for out in (keep, send):
        out[:, split:, ranks:] = jnp.zeros((out.shape[0], most, HEAD_WIDTH - ranks), out.dtype)
    for d in range(model.shape[0]):
        out, at, source = (send if d & bit else keep), without(d, bit), me ^ d
        out[at, :split] = jnp.where(first, model[source, :split], model[source, split:])
        lower = inner[source, most:]
        if rest < most:
            pad = jnp.zeros((most - rest, ranks), out.dtype)
            lower = jnp.concatenate([lower, pad], axis=0)
        out[at, split:, :ranks] = jnp.where(first, inner[source, :most], lower)


def lora_turn_kernel(after, kept, got, keep, send, *, bit, following):
    for d in range(2 * kept.shape[0]):
        value = (got if d & bit else kept)[without(d, bit)]
        (send if d & following else keep)[without(d, following)] = value


def lora_spread_kernel(after, kept, got, *outs, bit):
    for d in range(2 * kept.shape[0]):
        outs[d // NEAR][d % NEAR] = (got if d & bit else kept)[without(d, bit)]


def lora_gather_kernel(after, *refs):
    got, out = refs[:-1], refs[-1]
    for j, ref in enumerate(got):
        out[j * NEAR : (j + 1) * NEAR] = ref[...]


def lora_join_kernel(*refs):
    me, first = lax.axis_index("exp"), lax.axis_index("grp") == 0
    pairs, (model, inner) = refs[:-2], refs[-2:]
    split, d = model.shape[0] // 2, 0
    most = pairs[0].shape[1] - split
    total = sum(mine.shape[0] for mine in pairs[::2])
    width = inner.shape[0] // total
    for mine, theirs in zip(pairs[::2], pairs[1::2]):
        for k in range(mine.shape[0]):
            own, other, at = mine[k], theirs[k], me ^ d
            halves = jnp.where(first, own, other), jnp.where(first, other, own)
            columns = pl.ds(pl.multiple_of(at * HEAD_WIDTH, HEAD_WIDTH), HEAD_WIDTH)
            model[:split, columns] = halves[0][:split]
            model[split:, columns] = halves[1][:split]
            start = pl.multiple_of(at * width, 16)
            inner[pl.ds(start, most)] = halves[0][split:]
            inner[pl.ds(start + most, width - most)] = halves[1][split : split + width - most]
            d += 1


def lora_near(adapter_model, adapter_hidden, n, marks):
    total, ranks, model_width = adapter_model.shape
    inner_width = adapter_hidden.shape[2]
    inner = jnp.transpose(adapter_hidden, (0, 2, 1))
    if model_width != HEAD_WIDTH or inner_width % 16 or lax.axis_size("grp") != 2:
        model = lax.all_to_all(adapter_model, "exp", split_axis=0, concat_axis=2, tiled=True)
        inner = lax.all_to_all(inner, "exp", split_axis=0, concat_axis=1, tiled=True)
        return [model[0], inner[0]], True
    far = n // NEAR
    block = (ranks // 2 + pad16(inner_width // 2), HEAD_WIDTH)
    halves = (shape((n // 2,) + block, bf16),) * 2
    keep, send = call(
        functools.partial(lora_pack_kernel, bit=1),
        halves,
        [VMEM] * 3,
        marks[0],
        adapter_model,
        inner,
        nanos=FILL,
    )
    keep, send = call(
        functools.partial(lora_turn_kernel, bit=1, following=2),
        halves,
        [VMEM] * 3,
        marks[1],
        keep,
        swap(send, n, 1),
        nanos=FILL,
    )
    spread = call(
        functools.partial(lora_spread_kernel, bit=2),
        (shape((NEAR,) + block, bf16),) * (n // NEAR),
        [VMEM] * 3,
        marks[2],
        keep,
        swap(send, n, 2),
        nanos=FILL,
    )
    return spread, False


def lora_far_start(turned, n, after):
    arrived = [turned[0], swap(turned[1], n, NEAR)]
    for j in range(2, len(turned) - 1):
        arrived.append(swap(hold(turned[j], after), n, j * NEAR))
    return arrived


def lora_gather(arrived, after):
    blocks = sum(part.shape[0] for part in arrived)
    return call(
        lora_gather_kernel,
        shape((blocks,) + arrived[0].shape[1:], bf16),
        [VMEM] * (1 + len(arrived)),
        after,
        *arrived,
        nanos=FILL,
    )


def lora_join(parts, inner_width):
    pairs = [x for part in parts for x in (part, lax.ppermute(part, "grp", [(0, 1), (1, 0)]))]
    n = sum(part.shape[0] for part in parts)
    return call(
        lora_join_kernel,
        (
            shape((3 * ADAPTER_RANK, n * HEAD_WIDTH), bf16),
            shape((n * inner_width, HEAD_WIDTH), bf16),
        ),
        [VMEM] * len(pairs),
        *pairs,
    )


def body(
    resid,
    queries,
    incoming_key_value,
    key_value_cache,
    lengths,
    norm_scale_vector,
    expert_choice,
    router_probability,
    gate_weight,
    up_weight,
    down_weight,
    adapter_model,
    adapter_hidden,
):
    n = lax.axis_size("exp")
    far = n // NEAR

    slots = 2 * far
    first_inputs = (queries, resid)
    message = call(
        pack_kernel,
        shape((1,) + MESSAGE, bf16),
        [HBM] * 2,
        *[pltpu.with_memory_space_constraint(x, pltpu.HBM) for x in first_inputs],
        scratch=[pltpu.VMEM(x.shape, x.dtype) for x in first_inputs]
        + [pltpu.SemaphoreType.DMA((2,))],
        nanos=4000,
    )
    marks, distance = [message], n // 2
    while distance > 2:
        message = call(
            join_kernel,
            shape((2 * message.shape[0],) + MESSAGE, bf16),
            [VMEM] * 2,
            message,
            swap(message, n, distance),
        )
        marks.append(message)
        distance //= 2
    turned, whole = lora_near(adapter_model, adapter_hidden, n, marks)
    residuals, near = call(
        narrow_kernel,
        (shape((slots,) + HEADS, bf16), shape((slots + 1,) + HEADS, bf16)),
        [VMEM] * 4,
        turned[0],
        message,
        swap(message, n, 2),
        incoming_key_value,
    )
    if not whole:
        arrived = lora_far_start(turned, n, near)
    next_near = swap(near, n, 1)
    partial = shape((slots + stat_tiles(slots),) + HEADS, bf16)
    keep, send = call(
        functools.partial(attend_kernel, far=far),
        (partial,) * 2,
        [VMEM, SMEM] + [VMEM] * 3,
        turned[0] if whole else arrived[1],
        lengths,
        near,
        next_near,
        key_value_cache,
        nanos=8000,
    )
    gates = call(
        gate_kernel,
        shape((1, HEAD_WIDTH), f32),
        [VMEM] * 3,
        keep,
        expert_choice,
        router_probability,
    )
    theirs, flip, distance = swap(send, n, 1), 0, 2
    after = gates
    while distance < n:
        keep = call(
            functools.partial(merge_kernel, slots=slots, flip=flip),
            partial,
            [VMEM] * 3,
            after,
            keep,
            theirs,
            nanos=MERGE,
        )
        if distance == 2 and not whole:
            after = arrived[-1]
            last = hold(turned[-1], keep)
            arrived.append(swap(last, n, n - NEAR))
        if distance == n // 4 and not whole:
            after = lora_gather(arrived[:-1], keep)
            parts = [after, hold(arrived[-1], after)]
            after = parts[1]
        theirs = swap(keep, n, distance)
        flip = slots // distance
        distance *= 2
    hidden, normed = call(
        token_kernel,
        (shape(HEADS, f32), shape((slots,) + HEADS, bf16)),
        [VMEM] * 4,
        keep,
        theirs,
        residuals,
        norm_scale_vector.reshape(HEADS),
        nanos=TOKEN,
    )
    model, inner = turned if whole else lora_join(parts, adapter_hidden.shape[2])
    out = call(
        functools.partial(expert_kernel, far=far),
        shape((n,) + HEADS, bf16),
        [VMEM] * 7,
        normed,
        swap(normed, n, 1),
        gate_weight[0],
        up_weight[0],
        down_weight[0],
        model,
        inner,
        limit=32,
    )
    return call(
        finish_kernel,
        shape((1, WIDTH), bf16),
        [VMEM] * 3,
        hidden,
        lax.all_to_all(out, "exp", split_axis=0, concat_axis=0, tiled=True),
        gates,
    )


def solution(mesh):
    return jax.shard_map(
        body,
        mesh=mesh,
        in_specs=(
            P(("grp", "exp"), None),
            P(("grp", "exp"), None),
            P(("grp", "exp"), None),
            P("grp", "exp", None),
            P("grp"),
            P(),
            P(("grp", "exp"), None),
            P(("grp", "exp"), None),
            P("exp", None, None),
            P("exp", None, None),
            P("exp", None, None),
            P(None, None, "exp"),
            P(None, None, "exp"),
        ),
        out_specs=P(("grp", "exp"), None),
        check_vma=False,
    )
```

```python
import functools

import jax
import jax.numpy as jnp
from jax import lax
from jax.experimental import pallas as pl
from jax.experimental.pallas import tpu as pltpu
from jax.sharding import PartitionSpec as P

QUERY_HEADS = 16
KEY_VALUE_HEADS = 2
HEAD_WIDTH = 128
ADAPTER_RANK = 32
GROUPED = QUERY_HEADS // KEY_VALUE_HEADS
KEY_VALUE_WIDTH = KEY_VALUE_HEADS * HEAD_WIDTH
WIDTH = QUERY_HEADS * HEAD_WIDTH
INV_ROOT = HEAD_WIDTH ** (-0.5)
NEAR = 4
NEW_ROWS = 2 * KEY_VALUE_HEADS
HEADS = (QUERY_HEADS, HEAD_WIDTH)
MESSAGE = (2 * QUERY_HEADS, HEAD_WIDTH)

floor_score = -1e30
epsilon = 1e-06
DOWN_PARTS = 4
FILL = 20
TOKEN = 800
MERGE = 3500
JOIN = 1600

VMEM = pl.BlockSpec(memory_space=pltpu.VMEM)
SMEM = pl.BlockSpec(memory_space=pltpu.SMEM)
HBM = pl.BlockSpec(memory_space=pltpu.HBM)
shape = jax.ShapeDtypeStruct
bf16, f32 = jnp.bfloat16, jnp.float32


def call(kernel, shapes, specs, *args, limit=8, scratch=(), nanos=JOIN):
    return pl.pallas_call(
        kernel,
        out_shape=shapes,
        in_specs=specs,
        out_specs=jax.tree.map(lambda _: VMEM, shapes),
        scratch_shapes=scratch,
        cost_estimate=pl.CostEstimate(
            flops=nanos * 1000000, transcendentals=0, bytes_accessed=0
        ),
        compiler_params=pltpu.CompilerParams(vmem_limit_bytes=limit * 1024 * 1024),
    )(*args)


def hold_kernel(value, after, out):
    out[...] = value[...]


def hold(value, after):
    return call(
        hold_kernel, shape(value.shape, value.dtype), [VMEM] * 2, value, after, nanos=FILL
    )


def iota(dims, dim):
    return lax.broadcasted_iota(jnp.int32, dims, dim)


def as_rows(line, rows):
    return jnp.concatenate(
        [line[:, j * HEAD_WIDTH : (j + 1) * HEAD_WIDTH] for j in range(rows)], axis=0
    )


def swap(value, n, distance):
    return lax.ppermute(value, "exp", [(t, t ^ distance) for t in range(n)])


def distance_of(column, far):
    bits = far.bit_length() - 1
    return sum(NEAR << i for i in range(bits) if column >> (bits - 1 - i) & 1)


def pad16(rows):
    return -(-rows // 16) * 16


def stat_tiles(slots):
    return 1 if 6 * slots <= HEAD_WIDTH else 3


def pack_kernel(query, resid, out, q_in, r_in, sems):
    copies = [
        pltpu.make_async_copy(source, target, sems.at[k])
        for k, (source, target) in enumerate(((query, q_in), (resid, r_in)))
    ]
    for copy in copies:
        copy.start()
    for copy in copies:
        copy.wait()
    q = as_rows(q_in[...].astype(f32), QUERY_HEADS)
    r = as_rows(r_in[...].astype(f32), QUERY_HEADS)
    out[0] = jnp.concatenate([q, r], axis=0).astype(bf16)


def join_kernel(mine, theirs, out):
    half = mine.shape[0]
    out[:half] = mine[...]
    out[half:] = theirs[...]


def narrow_kernel(after, mine, theirs, new, residuals, out):
    half = mine.shape[0]
    for k, source in enumerate((mine, theirs)):
        for w in range(half):
            slot = k * half + w
            out[slot] = source[w, :QUERY_HEADS]
            residuals[slot] = source[w, QUERY_HEADS:]
    fresh = as_rows(new[...].astype(f32), NEW_ROWS)
    rest = jnp.zeros((QUERY_HEADS - NEW_ROWS, HEAD_WIDTH), f32)
    out[2 * half] = jnp.concatenate([fresh, rest], axis=0).astype(bf16)


def write_stats(stats, out, slots):
    parts = []
    for _ in range(3):
        part = stats.astype(bf16).astype(f32)
        parts.append(part)
        stats = stats - part
    if stat_tiles(slots) == 1:
        tile = parts[0]
        for k in (1, 2):
            tile = tile + pltpu.roll(parts[k], 2 * slots * k, 1)
        out[slots] = tile.astype(bf16)
    else:
        for k in range(3):
            out[slots + k] = parts[k].astype(bf16)


def read_stats(message, slots):
    if stat_tiles(slots) == 1:
        tile = message[slots].astype(f32)
        lanes = iota(HEADS, 1)
        stats = tile
        for k in (1, 2):
            stats = stats + pltpu.roll(tile, HEAD_WIDTH - 2 * slots * k, 1)
        stats = jnp.where(lanes < 2 * slots, stats, 0.0)
    else:
        stats = sum(message[slots + k].astype(f32) for k in range(3))
    return stats, pltpu.roll(stats, HEAD_WIDTH - slots, 1)


def flipped(value, flip):
    if not flip:
        return value
    ahead = pltpu.roll(value, HEAD_WIDTH - flip, 1)
    behind = pltpu.roll(value, flip, 1)
    return jnp.where((iota(HEADS, 1) & flip) == 0, ahead, behind)


def merged(mine, theirs, slots, flip):
    top, total = read_stats(mine, slots)
    other_top, other_total = (flipped(x, flip) for x in read_stats(theirs, slots))
    peak = jnp.maximum(top, other_top)
    share, other_share = jnp.exp(top - peak), jnp.exp(other_top - peak)
    total = share * total + other_share * other_total

    def acc(slot):
        return share[:, slot : slot + 1] * mine[slot].astype(f32) + other_share[
            :, slot : slot + 1
        ] * theirs[slot ^ flip].astype(f32)

    return peak, total, acc


def merge_kernel(after, mine, theirs, out, *, slots, flip):
    peak, total, acc = merged(mine, theirs, slots, flip)
    lanes = iota(HEADS, 1)
    stats = jnp.where(lanes < slots, peak, 0.0)
    stats = stats + pltpu.roll(jnp.where(lanes < slots, total, 0.0), slots, 1)
    write_stats(stats, out, slots)
    for slot in range(slots):
        out[slot] = acc(slot).astype(bf16)


def fresh_block(mine, theirs, me):
    slots = mine.shape[0] - 1
    second = me % 2 == 1
    first_group = iota(HEADS, 0) < GROUPED

    def by_head(rows, at):
        return jnp.where(first_group, rows[at : at + 1], rows[at + 1 : at + 2])

    q = mine[0].astype(f32)
    own, other = mine[slots].astype(f32), theirs[slots].astype(f32)
    own_score = jnp.sum(q * by_head(own, 0), axis=1, keepdims=True) * INV_ROOT
    other_score = jnp.sum(q * by_head(other, 0), axis=1, keepdims=True) * INV_ROOT
    other_score = jnp.where(second, other_score, floor_score)
    top = jnp.maximum(own_score, other_score)
    own_weight = jnp.exp(own_score - top).astype(bf16).astype(f32)
    other_weight = jnp.where(second, jnp.exp(other_score - top), 0.0).astype(bf16).astype(f32)
    acc = own_weight * by_head(own, 2) + other_weight * by_head(other, 2)
    return top, own_weight + other_weight, acc


def attend_kernel(after, lengths, mine, theirs, cache, keep, send, *, far):
    me = lax.axis_index("exp")
    sequences, block, _ = cache.shape
    rows = 2 * QUERY_HEADS
    first_group = (iota((rows, HEAD_WIDTH), 0) % QUERY_HEADS) < GROUPED
    positions = me * block + iota((rows, block), 1)
    lanes = iota(HEADS, 1)
    fresh = fresh_block(mine, theirs, me)
    stats = [jnp.zeros(HEADS, f32), jnp.zeros(HEADS, f32)]
    batch = 8 if sequences % 8 == 0 else 1
    for base in range(0, sequences, batch):
        slots = range(base, base + batch)
        where = [
            lax.shift_right_logical(me, 1)
            ^ ((distance_of(slot % far, far) >> 1) | (slot // far))
            for slot in slots
        ]
        scores, valid = [], []
        for slot, s in zip(slots, where):
            both = jnp.concatenate([mine[slot], theirs[slot]], axis=0)
            zero = jnp.zeros_like(both)
            wide = jnp.concatenate(
                [jnp.where(first_group, both, zero), jnp.where(first_group, zero, both)], axis=1
            )
            product = lax.dot_general(
                wide,
                cache[s, :, :KEY_VALUE_WIDTH],
                (((1,), (1,)), ((), ())),
                preferred_element_type=f32,
            )
            valid.append(positions < lengths[s])
            scores.append(jnp.where(valid[-1], product * INV_ROOT, floor_score))
        tops = [jnp.max(score, axis=1, keepdims=True) for score in scores]
        weights = [
            jnp.where(ok, jnp.exp(score - top), 0.0).astype(bf16)
            for ok, score, top in zip(valid, scores, tops)
        ]
        totals = [jnp.sum(weight.astype(f32), axis=1, keepdims=True) for weight in weights]
        accs = [
            jnp.dot(weight, cache[s, :, KEY_VALUE_WIDTH:], preferred_element_type=f32)
            for weight, s in zip(weights, where)
        ]
        for slot, top, total, acc in zip(slots, tops, totals, accs):
            acc = jnp.where(first_group, acc[:, :HEAD_WIDTH], acc[:, HEAD_WIDTH:])
            for k, part in enumerate((keep, send)):
                cut = slice(k * QUERY_HEADS, (k + 1) * QUERY_HEADS)
                t, z, a = top[cut], total[cut], acc[cut]
                if slot == 0 and k == 0:
                    peak = jnp.maximum(t, fresh[0])
                    old, young = jnp.exp(t - peak), jnp.exp(fresh[0] - peak)
                    t, z, a = peak, old * z + young * fresh[1], old * a + young * fresh[2]
                part[slot] = a.astype(bf16)
                stats[k] = jnp.where(lanes == slot, t, stats[k])
                stats[k] = jnp.where(lanes == sequences + slot, z, stats[k])
    for k, part in enumerate((keep, send)):
        write_stats(stats[k], part, sequences)


def token_kernel(mine, theirs, residuals, scale, hidden_out, normed_out):
    slots = residuals.shape[0]
    _, total, acc = merged(mine, theirs, slots, 1)
    inverse = 1.0 / jnp.where(iota(HEADS, 1) < slots, total, 1.0)
    for slot in range(slots):
        hidden = residuals[slot].astype(f32) + acc(slot) * inverse[:, slot : slot + 1]
        squares = jnp.sum(jnp.sum(hidden * hidden, axis=1, keepdims=True), axis=0, keepdims=True)
        normed = hidden * lax.rsqrt(squares / WIDTH + epsilon) * scale[...]
        if slot == 0:
            hidden_out[...] = hidden
        normed_out[slot] = normed.astype(bf16)


def dot_pair(value, factor, contract):
    high = value.astype(bf16)
    low = (value - high.astype(f32)).astype(bf16)
    both = lax.dot_general(
        jnp.concatenate([high, low], axis=0),
        factor,
        (((1,), (contract,)), ((), ())),
        preferred_element_type=f32,
    )
    return both[: value.shape[0]] + both[value.shape[0] :]


def expert_kernel(mine, theirs, gate_w, up_w, down_hbm, model, inner, out, down_w, sems, *, far):
    me = lax.axis_index("exp")
    rows = down_w.shape[0] // DOWN_PARTS
    copies = [
        pltpu.make_async_copy(
            down_hbm.at[pl.ds(k * rows, rows)], down_w.at[pl.ds(k * rows, rows)], sems.at[k]
        )
        for k in range(DOWN_PARTS)
    ]
    for copy in copies:
        copy.start()
    half = mine.shape[0]
    x = jnp.concatenate([mine[...].astype(f32), theirs[...].astype(f32)], axis=0)
    x = x.reshape(2 * half, WIDTH).astype(bf16)
    r = ADAPTER_RANK
    mixed = lax.dot_general(
        x, model[: 2 * r], (((1,), (1,)), ((), ())), preferred_element_type=f32
    )
    gate = jnp.dot(x, gate_w[...], preferred_element_type=f32)
    gate = gate + dot_pair(mixed[:, :r], inner[:, :r], 1)
    up = jnp.dot(x, up_w[...], preferred_element_type=f32)
    up = up + dot_pair(mixed[:, r:], inner[:, r : 2 * r], 1)
    act = (gate / (1.0 + jnp.exp(-gate)) * up).astype(bf16)
    for copy in copies:
        copy.wait()
    lowered = jnp.dot(act, inner[:, 2 * r : 3 * r], preferred_element_type=f32)
    result = jnp.dot(act, down_w[...], preferred_element_type=f32)
    result = result + dot_pair(lowered, model[2 * r :], 0)
    for c in range(2):
        for y in range(2):
            for w in range(far):
                slot = (c * 2 + y) * far + w
                line = as_rows(result[slot : slot + 1], QUERY_HEADS)
                out[me ^ (distance_of(w, far) | 2 * y | c)] = line.astype(bf16)


def gate_kernel(after, choice, probability, out):
    p = probability[...]
    shares = p / jnp.sum(p, axis=1, keepdims=True)
    lanes = iota((1, HEAD_WIDTH), 1)
    gates = jnp.zeros((1, HEAD_WIDTH), f32)
    for k in range(p.shape[1]):
        gates = gates + jnp.where(choice[:, k : k + 1] == lanes, shares[:, k : k + 1], 0.0)
    out[...] = gates.astype(bf16).astype(f32)


def finish_kernel(hidden, got, gates, out):
    total = hidden[...]
    for e in range(got.shape[0]):
        total = total + gates[:, e : e + 1] * got[e].astype(f32)
    line = jnp.concatenate([total[j : j + 1] for j in range(QUERY_HEADS)], axis=1)
    out[...] = line.astype(bf16)


def without(index, bit):
    return (index // (2 * bit)) * bit + index % bit


def lora_pack_kernel(after, model, inner, keep, send, *, bit):
    me, first = lax.axis_index("exp"), lax.axis_index("grp") == 0
    ranks, split = model.shape[1], model.shape[1] // 2
    most = keep.shape[1] - split
    rest = inner.shape[1] - most
    for out in (keep, send):
        out[:, split:, ranks:] = jnp.zeros((out.shape[0], most, HEAD_WIDTH - ranks), out.dtype)
    for d in range(model.shape[0]):
        out, at, source = (send if d & bit else keep), without(d, bit), me ^ d
        out[at, :split] = jnp.where(first, model[source, :split], model[source, split:])
        lower = inner[source, most:]
        if rest < most:
            pad = jnp.zeros((most - rest, ranks), out.dtype)
            lower = jnp.concatenate([lower, pad], axis=0)
        out[at, split:, :ranks] = jnp.where(first, inner[source, :most], lower)


def lora_turn_kernel(after, kept, got, keep, send, *, bit, following):
    for d in range(2 * kept.shape[0]):
        value = (got if d & bit else kept)[without(d, bit)]
        (send if d & following else keep)[without(d, following)] = value


def lora_spread_kernel(after, kept, got, *outs, bit):
    for d in range(2 * kept.shape[0]):
        outs[d // NEAR][d % NEAR] = (got if d & bit else kept)[without(d, bit)]


def lora_order_kernel(after, *refs):
    me = lax.axis_index("exp")
    got, out = refs[:-1], refs[-1]
    for j, ref in enumerate(got):
        for l in range(NEAR):
            out[me ^ (j * NEAR + l)] = ref[l]


def lora_join_kernel(mine, theirs, model, inner):
    first = lax.axis_index("grp") == 0
    split = model.shape[0] // 2
    most, width = mine.shape[1] - split, inner.shape[0] // mine.shape[0]
    for at in range(mine.shape[0]):
        own, other = mine[at], theirs[at]
        halves = jnp.where(first, own, other), jnp.where(first, other, own)
        columns = slice(at * HEAD_WIDTH, (at + 1) * HEAD_WIDTH)
        model[:split, columns] = halves[0][:split]
        model[split:, columns] = halves[1][:split]
        inner[at * width : at * width + most] = halves[0][split:]
        inner[at * width + most : (at + 1) * width] = halves[1][split : split + width - most]


def lora_near(adapter_model, adapter_hidden, n, marks):
    total, ranks, model_width = adapter_model.shape
    inner_width = adapter_hidden.shape[2]
    inner = jnp.transpose(adapter_hidden, (0, 2, 1))
    if model_width != HEAD_WIDTH or inner_width % 16 or lax.axis_size("grp") != 2:
        model = lax.all_to_all(adapter_model, "exp", split_axis=0, concat_axis=2, tiled=True)
        inner = lax.all_to_all(inner, "exp", split_axis=0, concat_axis=1, tiled=True)
        return [model[0], inner[0]], True
    far = n // NEAR
    block = (ranks // 2 + pad16(inner_width // 2), HEAD_WIDTH)
    halves = (shape((n // 2,) + block, bf16),) * 2
    keep, send = call(
        functools.partial(lora_pack_kernel, bit=2),
        halves,
        [VMEM] * 3,
        marks[0],
        adapter_model,
        inner,
        nanos=FILL,
    )
    keep, send = call(
        functools.partial(lora_turn_kernel, bit=2, following=1),
        halves,
        [VMEM] * 3,
        marks[1],
        keep,
        swap(send, n, 2),
        nanos=FILL,
    )
    spread = call(
        functools.partial(lora_spread_kernel, bit=1),
        (shape((NEAR,) + block, bf16),) * (n // NEAR),
        [VMEM] * 3,
        marks[2],
        keep,
        swap(send, n, 1),
        nanos=FILL,
    )
    return spread, False


def lora_far_start(turned, n, after):
    arrived = [turned[0], swap(turned[1], n, NEAR)]
    for j in range(2, len(turned) - 1):
        arrived.append(swap(hold(turned[j], after), n, j * NEAR))
    return arrived


def lora_order(arrived, n, after):
    return call(
        lora_order_kernel,
        shape((n,) + arrived[0].shape[1:], bf16),
        [VMEM] * (1 + len(arrived)),
        after,
        *arrived,
        nanos=FILL,
    )


def lora_join(ordered, inner_width):
    n = ordered.shape[0]
    return call(
        lora_join_kernel,
        (
            shape((3 * ADAPTER_RANK, n * HEAD_WIDTH), bf16),
            shape((n * inner_width, HEAD_WIDTH), bf16),
        ),
        [VMEM] * 2,
        ordered,
        lax.ppermute(ordered, "grp", [(0, 1), (1, 0)]),
    )


def body(
    resid,
    queries,
    incoming_key_value,
    key_value_cache,
    lengths,
    norm_scale_vector,
    expert_choice,
    router_probability,
    gate_weight,
    up_weight,
    down_weight,
    adapter_model,
    adapter_hidden,
):
    n = lax.axis_size("exp")
    far = n // NEAR

    slots = 2 * far
    first_inputs = (queries, resid)
    message = call(
        pack_kernel,
        shape((1,) + MESSAGE, bf16),
        [HBM] * 2,
        *[pltpu.with_memory_space_constraint(x, pltpu.HBM) for x in first_inputs],
        scratch=[pltpu.VMEM(x.shape, x.dtype) for x in first_inputs]
        + [pltpu.SemaphoreType.DMA((2,))],
        nanos=4000,
    )
    marks, distance = [message], n // 2
    while distance > 2:
        message = call(
            join_kernel,
            shape((2 * message.shape[0],) + MESSAGE, bf16),
            [VMEM] * 2,
            message,
            swap(message, n, distance),
        )
        marks.append(message)
        distance //= 2
    turned, whole = lora_near(adapter_model, adapter_hidden, n, marks)
    residuals, near = call(
        narrow_kernel,
        (shape((slots,) + HEADS, bf16), shape((slots + 1,) + HEADS, bf16)),
        [VMEM] * 4,
        turned[0],
        message,
        swap(message, n, 2),
        incoming_key_value,
    )
    if not whole:
        arrived = lora_far_start(turned, n, near)
    next_near = swap(near, n, 1)
    partial = shape((slots + stat_tiles(slots),) + HEADS, bf16)
    keep, send = call(
        functools.partial(attend_kernel, far=far),
        (partial,) * 2,
        [VMEM, SMEM] + [VMEM] * 3,
        turned[0] if whole else arrived[1],
        lengths,
        near,
        next_near,
        key_value_cache,
        nanos=8000,
    )
    gates = call(
        gate_kernel,
        shape((1, HEAD_WIDTH), f32),
        [VMEM] * 3,
        keep,
        expert_choice,
        router_probability,
    )
    theirs, flip, distance = swap(send, n, 1), 0, 2
    after = gates
    while distance < n:
        keep = call(
            functools.partial(merge_kernel, slots=slots, flip=flip),
            partial,
            [VMEM] * 3,
            after,
            keep,
            theirs,
            nanos=MERGE,
        )
        if distance == 2 and not whole:
            after = arrived[-1]
            last = hold(turned[-1], keep)
            arrived.append(swap(last, n, n - NEAR))
        if distance == n // 4:
            after = turned[0] if whole else lora_order(arrived, n, keep)
        theirs = swap(keep, n, distance)
        flip = slots // distance
        distance *= 2
    ordered = after
    hidden, normed = call(
        token_kernel,
        (shape(HEADS, f32), shape((slots,) + HEADS, bf16)),
        [VMEM] * 4,
        keep,
        theirs,
        residuals,
        norm_scale_vector.reshape(HEADS),
        nanos=TOKEN,
    )
    model, inner = turned if whole else lora_join(ordered, adapter_hidden.shape[2])
    out = call(
        functools.partial(expert_kernel, far=far),
        shape((n,) + HEADS, bf16),
        [VMEM] * 4 + [HBM] + [VMEM] * 2,
        normed,
        swap(normed, n, 1),
        gate_weight[0],
        up_weight[0],
        pltpu.with_memory_space_constraint(down_weight[0], pltpu.HBM),
        model,
        inner,
        limit=32,
        scratch=[
            pltpu.VMEM(down_weight.shape[1:], bf16),
            pltpu.SemaphoreType.DMA((DOWN_PARTS,)),
        ],
    )
    return call(
        finish_kernel,
        shape((1, WIDTH), bf16),
        [VMEM] * 3,
        hidden,
        lax.all_to_all(out, "exp", split_axis=0, concat_axis=0, tiled=True),
        gates,
    )


def solution(mesh):
    return jax.shard_map(
        body,
        mesh=mesh,
        in_specs=(
            P(("grp", "exp"), None),
            P(("grp", "exp"), None),
            P(("grp", "exp"), None),
            P("grp", "exp", None),
            P("grp"),
            P(),
            P(("grp", "exp"), None),
            P(("grp", "exp"), None),
            P("exp", None, None),
            P("exp", None, None),
            P("exp", None, None),
            P(None, None, "exp"),
            P(None, None, "exp"),
        ),
        out_specs=P(("grp", "exp"), None),
        check_vma=False,
    )
```

```python
import functools

import jax
import jax.numpy as jnp
from jax import lax
from jax.experimental import pallas as pl
from jax.experimental.pallas import tpu as pltpu
from jax.sharding import PartitionSpec as P

QUERY_HEADS = 16
KEY_VALUE_HEADS = 2
HEAD_WIDTH = 128
ADAPTER_RANK = 32
GROUPED = QUERY_HEADS // KEY_VALUE_HEADS
KEY_VALUE_WIDTH = KEY_VALUE_HEADS * HEAD_WIDTH
WIDTH = QUERY_HEADS * HEAD_WIDTH
INV_ROOT = HEAD_WIDTH ** (-0.5)
NEAR = 4
NEW_ROWS = 2 * KEY_VALUE_HEADS
HEADS = (QUERY_HEADS, HEAD_WIDTH)
MESSAGE = (2 * QUERY_HEADS, HEAD_WIDTH)

floor_score = -1e30
epsilon = 1e-06
FILL = 20
LATE = 20
TOKEN = 50
MERGE = 2500
JOIN = 1600

VMEM = pl.BlockSpec(memory_space=pltpu.VMEM)
SMEM = pl.BlockSpec(memory_space=pltpu.SMEM)
HBM = pl.BlockSpec(memory_space=pltpu.HBM)
shape = jax.ShapeDtypeStruct
bf16, f32 = jnp.bfloat16, jnp.float32


def call(kernel, shapes, specs, *args, limit=8, scratch=(), nanos=JOIN):
    return pl.pallas_call(
        kernel,
        out_shape=shapes,
        in_specs=specs,
        out_specs=jax.tree.map(lambda _: VMEM, shapes),
        scratch_shapes=scratch,
        cost_estimate=pl.CostEstimate(
            flops=nanos * 1000000, transcendentals=0, bytes_accessed=0
        ),
        compiler_params=pltpu.CompilerParams(vmem_limit_bytes=limit * 1024 * 1024),
    )(*args)


def hold_kernel(value, after, out):
    out[...] = value[...]


def hold(value, after):
    return call(
        hold_kernel, shape(value.shape, value.dtype), [VMEM] * 2, value, after, nanos=FILL
    )


def iota(dims, dim):
    return lax.broadcasted_iota(jnp.int32, dims, dim)


def as_rows(line, rows):
    return jnp.concatenate(
        [line[:, j * HEAD_WIDTH : (j + 1) * HEAD_WIDTH] for j in range(rows)], axis=0
    )


def swap(value, n, distance):
    return lax.ppermute(value, "exp", [(t, t ^ distance) for t in range(n)])


def distance_of(column, far):
    bits = far.bit_length() - 1
    return sum(NEAR << i for i in range(bits) if column >> (bits - 1 - i) & 1)


def pad16(rows):
    return -(-rows // 16) * 16


def stat_tiles(slots):
    return 1 if 6 * slots <= HEAD_WIDTH else 3


def pack_kernel(query, resid, out, q_in, r_in, sems):
    copies = [
        pltpu.make_async_copy(source, target, sems.at[k])
        for k, (source, target) in enumerate(((query, q_in), (resid, r_in)))
    ]
    for copy in copies:
        copy.start()
    for copy in copies:
        copy.wait()
    q = as_rows(q_in[...].astype(f32), QUERY_HEADS)
    r = as_rows(r_in[...].astype(f32), QUERY_HEADS)
    out[0] = jnp.concatenate([q, r], axis=0).astype(bf16)


def join_kernel(mine, theirs, out):
    half = mine.shape[0]
    out[:half] = mine[...]
    out[half:] = theirs[...]


def narrow_kernel(after, mine, theirs, new, residuals, out):
    half = mine.shape[0]
    for k, source in enumerate((mine, theirs)):
        for w in range(half):
            slot = k * half + w
            out[slot] = source[w, :QUERY_HEADS]
            residuals[slot] = source[w, QUERY_HEADS:]
    fresh = as_rows(new[...].astype(f32), NEW_ROWS)
    rest = jnp.zeros((QUERY_HEADS - NEW_ROWS, HEAD_WIDTH), f32)
    out[2 * half] = jnp.concatenate([fresh, rest], axis=0).astype(bf16)


def write_stats(stats, out, slots):
    parts = []
    for _ in range(3):
        part = stats.astype(bf16).astype(f32)
        parts.append(part)
        stats = stats - part
    if stat_tiles(slots) == 1:
        tile = parts[0]
        for k in (1, 2):
            tile = tile + pltpu.roll(parts[k], 2 * slots * k, 1)
        out[slots] = tile.astype(bf16)
    else:
        for k in range(3):
            out[slots + k] = parts[k].astype(bf16)


def read_stats(message, slots):
    if stat_tiles(slots) == 1:
        tile = message[slots].astype(f32)
        lanes = iota(HEADS, 1)
        stats = tile
        for k in (1, 2):
            stats = stats + pltpu.roll(tile, HEAD_WIDTH - 2 * slots * k, 1)
        stats = jnp.where(lanes < 2 * slots, stats, 0.0)
    else:
        stats = sum(message[slots + k].astype(f32) for k in range(3))
    return stats, pltpu.roll(stats, HEAD_WIDTH - slots, 1)


def flipped(value, flip):
    if not flip:
        return value
    ahead = pltpu.roll(value, HEAD_WIDTH - flip, 1)
    behind = pltpu.roll(value, flip, 1)
    return jnp.where((iota(HEADS, 1) & flip) == 0, ahead, behind)


def merged(mine, theirs, slots, flip):
    top, total = read_stats(mine, slots)
    other_top, other_total = (flipped(x, flip) for x in read_stats(theirs, slots))
    peak = jnp.maximum(top, other_top)
    share, other_share = jnp.exp(top - peak), jnp.exp(other_top - peak)
    total = share * total + other_share * other_total

    def acc(slot):
        return share[:, slot : slot + 1] * mine[slot].astype(f32) + other_share[
            :, slot : slot + 1
        ] * theirs[slot ^ flip].astype(f32)

    return peak, total, acc


def merge_kernel(after, mine, theirs, out, *, slots, flip):
    peak, total, acc = merged(mine, theirs, slots, flip)
    lanes = iota(HEADS, 1)
    stats = jnp.where(lanes < slots, peak, 0.0)
    stats = stats + pltpu.roll(jnp.where(lanes < slots, total, 0.0), slots, 1)
    write_stats(stats, out, slots)
    for slot in range(slots):
        out[slot] = acc(slot).astype(bf16)


def fresh_block(mine, theirs, me):
    slots = mine.shape[0] - 1
    second = me % 2 == 1
    first_group = iota(HEADS, 0) < GROUPED

    def by_head(rows, at):
        return jnp.where(first_group, rows[at : at + 1], rows[at + 1 : at + 2])

    q = mine[0].astype(f32)
    own, other = mine[slots].astype(f32), theirs[slots].astype(f32)
    own_score = jnp.sum(q * by_head(own, 0), axis=1, keepdims=True) * INV_ROOT
    other_score = jnp.sum(q * by_head(other, 0), axis=1, keepdims=True) * INV_ROOT
    other_score = jnp.where(second, other_score, floor_score)
    top = jnp.maximum(own_score, other_score)
    own_weight = jnp.exp(own_score - top).astype(bf16).astype(f32)
    other_weight = jnp.where(second, jnp.exp(other_score - top), 0.0).astype(bf16).astype(f32)
    acc = own_weight * by_head(own, 2) + other_weight * by_head(other, 2)
    return top, own_weight + other_weight, acc


def attend_kernel(after, lengths, mine, theirs, cache, keep, send, *, far):
    me = lax.axis_index("exp")
    sequences, block, _ = cache.shape
    rows = 2 * QUERY_HEADS
    first_group = (iota((rows, HEAD_WIDTH), 0) % QUERY_HEADS) < GROUPED
    positions = me * block + iota((rows, block), 1)
    lanes = iota(HEADS, 1)
    fresh = fresh_block(mine, theirs, me)
    stats = [jnp.zeros(HEADS, f32), jnp.zeros(HEADS, f32)]
    batch = 8 if sequences % 8 == 0 else 1
    for base in range(0, sequences, batch):
        slots = range(base, base + batch)
        where = [
            lax.shift_right_logical(me, 1)
            ^ ((distance_of(slot % far, far) >> 1) | (slot // far))
            for slot in slots
        ]
        scores, valid = [], []
        for slot, s in zip(slots, where):
            both = jnp.concatenate([mine[slot], theirs[slot]], axis=0)
            zero = jnp.zeros_like(both)
            wide = jnp.concatenate(
                [jnp.where(first_group, both, zero), jnp.where(first_group, zero, both)], axis=1
            )
            product = lax.dot_general(
                wide,
                cache[s, :, :KEY_VALUE_WIDTH],
                (((1,), (1,)), ((), ())),
                preferred_element_type=f32,
            )
            valid.append(positions < lengths[s])
            scores.append(jnp.where(valid[-1], product * INV_ROOT, floor_score))
        tops = [jnp.max(score, axis=1, keepdims=True) for score in scores]
        weights = [
            jnp.where(ok, jnp.exp(score - top), 0.0).astype(bf16)
            for ok, score, top in zip(valid, scores, tops)
        ]
        totals = [jnp.sum(weight.astype(f32), axis=1, keepdims=True) for weight in weights]
        accs = [
            jnp.dot(weight, cache[s, :, KEY_VALUE_WIDTH:], preferred_element_type=f32)
            for weight, s in zip(weights, where)
        ]
        for slot, top, total, acc in zip(slots, tops, totals, accs):
            acc = jnp.where(first_group, acc[:, :HEAD_WIDTH], acc[:, HEAD_WIDTH:])
            for k, part in enumerate((keep, send)):
                cut = slice(k * QUERY_HEADS, (k + 1) * QUERY_HEADS)
                t, z, a = top[cut], total[cut], acc[cut]
                if slot == 0 and k == 0:
                    peak = jnp.maximum(t, fresh[0])
                    old, young = jnp.exp(t - peak), jnp.exp(fresh[0] - peak)
                    t, z, a = peak, old * z + young * fresh[1], old * a + young * fresh[2]
                part[slot] = a.astype(bf16)
                stats[k] = jnp.where(lanes == slot, t, stats[k])
                stats[k] = jnp.where(lanes == sequences + slot, z, stats[k])
    for k, part in enumerate((keep, send)):
        write_stats(stats[k], part, sequences)


def token_kernel(mine, theirs, residuals, scale, hidden_out, normed_out):
    slots = residuals.shape[0]
    _, total, acc = merged(mine, theirs, slots, 1)
    inverse = 1.0 / jnp.where(iota(HEADS, 1) < slots, total, 1.0)
    for slot in range(slots):
        hidden = residuals[slot].astype(f32) + acc(slot) * inverse[:, slot : slot + 1]
        squares = jnp.sum(jnp.sum(hidden * hidden, axis=1, keepdims=True), axis=0, keepdims=True)
        normed = hidden * lax.rsqrt(squares / WIDTH + epsilon) * scale[...]
        if slot == 0:
            hidden_out[...] = hidden
        normed_out[slot] = normed.astype(bf16)


def dot_pair(value, factor, contract):
    high = value.astype(bf16)
    low = (value - high.astype(f32)).astype(bf16)
    both = lax.dot_general(
        jnp.concatenate([high, low], axis=0),
        factor,
        (((1,), (contract,)), ((), ())),
        preferred_element_type=f32,
    )
    return both[: value.shape[0]] + both[value.shape[0] :]


def expert_kernel(mine, theirs, gate_w, up_w, down_w, model, inner, out, *, far):
    me = lax.axis_index("exp")
    half = mine.shape[0]
    x = jnp.concatenate([mine[...].astype(f32), theirs[...].astype(f32)], axis=0)
    x = x.reshape(2 * half, WIDTH).astype(bf16)
    r = ADAPTER_RANK
    mixed = lax.dot_general(
        x, model[: 2 * r], (((1,), (1,)), ((), ())), preferred_element_type=f32
    )
    gate = jnp.dot(x, gate_w[...], preferred_element_type=f32)
    gate = gate + dot_pair(mixed[:, :r], inner[:, :r], 1)
    up = jnp.dot(x, up_w[...], preferred_element_type=f32)
    up = up + dot_pair(mixed[:, r:], inner[:, r : 2 * r], 1)
    act = (gate / (1.0 + jnp.exp(-gate)) * up).astype(bf16)
    lowered = jnp.dot(act, inner[:, 2 * r : 3 * r], preferred_element_type=f32)
    result = jnp.dot(act, down_w[...], preferred_element_type=f32)
    result = result + dot_pair(lowered, model[2 * r :], 0)
    for c in range(2):
        for y in range(2):
            for w in range(far):
                slot = (c * 2 + y) * far + w
                line = as_rows(result[slot : slot + 1], QUERY_HEADS)
                out[me ^ (distance_of(w, far) | 2 * y | c)] = line.astype(bf16)


def gate_kernel(after, choice, probability, out):
    p = probability[...]
    shares = p / jnp.sum(p, axis=1, keepdims=True)
    lanes = iota((1, HEAD_WIDTH), 1)
    gates = jnp.zeros((1, HEAD_WIDTH), f32)
    for k in range(p.shape[1]):
        gates = gates + jnp.where(choice[:, k : k + 1] == lanes, shares[:, k : k + 1], 0.0)
    out[...] = gates.astype(bf16).astype(f32)


def finish_kernel(hidden, got, gates, out):
    total = hidden[...]
    for e in range(got.shape[0]):
        total = total + gates[:, e : e + 1] * got[e].astype(f32)
    line = jnp.concatenate([total[j : j + 1] for j in range(QUERY_HEADS)], axis=1)
    out[...] = line.astype(bf16)


def without(index, bit):
    return (index // (2 * bit)) * bit + index % bit


def lora_pack_kernel(after, model, inner, keep, send, *, bit):
    me, first = lax.axis_index("exp"), lax.axis_index("grp") == 0
    ranks, split = model.shape[1], model.shape[1] // 2
    most = keep.shape[1] - split
    rest = inner.shape[1] - most
    for out in (keep, send):
        out[:, split:, ranks:] = jnp.zeros((out.shape[0], most, HEAD_WIDTH - ranks), out.dtype)
    for d in range(model.shape[0]):
        out, at, source = (send if d & bit else keep), without(d, bit), me ^ d
        out[at, :split] = jnp.where(first, model[source, :split], model[source, split:])
        lower = inner[source, most:]
        if rest < most:
            pad = jnp.zeros((most - rest, ranks), out.dtype)
            lower = jnp.concatenate([lower, pad], axis=0)
        out[at, split:, :ranks] = jnp.where(first, inner[source, :most], lower)


def lora_turn_kernel(after, kept, got, keep, send, *, bit, following):
    for d in range(2 * kept.shape[0]):
        value = (got if d & bit else kept)[without(d, bit)]
        (send if d & following else keep)[without(d, following)] = value


def lora_spread_kernel(after, kept, got, *outs, bit):
    for d in range(2 * kept.shape[0]):
        outs[d // NEAR][d % NEAR] = (got if d & bit else kept)[without(d, bit)]


def lora_order_kernel(after, *refs):
    me = lax.axis_index("exp")
    got, out = refs[:-1], refs[-1]
    for j, ref in enumerate(got):
        for l in range(NEAR):
            out[me ^ (j * NEAR + l)] = ref[l]


def lora_join_kernel(mine, theirs, model, inner):
    first = lax.axis_index("grp") == 0
    split = model.shape[0] // 2
    most, width = mine.shape[1] - split, inner.shape[0] // mine.shape[0]
    for at in range(mine.shape[0]):
        own, other = mine[at], theirs[at]
        halves = jnp.where(first, own, other), jnp.where(first, other, own)
        columns = slice(at * HEAD_WIDTH, (at + 1) * HEAD_WIDTH)
        model[:split, columns] = halves[0][:split]
        model[split:, columns] = halves[1][:split]
        inner[at * width : at * width + most] = halves[0][split:]
        inner[at * width + most : (at + 1) * width] = halves[1][split : split + width - most]


def lora_near(adapter_model, adapter_hidden, n, marks):
    total, ranks, model_width = adapter_model.shape
    inner_width = adapter_hidden.shape[2]
    inner = jnp.transpose(adapter_hidden, (0, 2, 1))
    if model_width != HEAD_WIDTH or inner_width % 16 or lax.axis_size("grp") != 2:
        model = lax.all_to_all(adapter_model, "exp", split_axis=0, concat_axis=2, tiled=True)
        inner = lax.all_to_all(inner, "exp", split_axis=0, concat_axis=1, tiled=True)
        return [model[0], inner[0]], True
    far = n // NEAR
    block = (ranks // 2 + pad16(inner_width // 2), HEAD_WIDTH)
    halves = (shape((n // 2,) + block, bf16),) * 2
    keep, send = call(
        functools.partial(lora_pack_kernel, bit=2),
        halves,
        [VMEM] * 3,
        marks[0],
        adapter_model,
        inner,
        nanos=FILL,
    )
    keep, send = call(
        functools.partial(lora_turn_kernel, bit=2, following=1),
        halves,
        [VMEM] * 3,
        marks[1],
        keep,
        swap(send, n, 2),
        nanos=FILL,
    )
    spread = call(
        functools.partial(lora_spread_kernel, bit=1),
        (shape((NEAR,) + block, bf16),) * (n // NEAR),
        [VMEM] * 3,
        marks[2],
        keep,
        swap(send, n, 1),
        nanos=FILL,
    )
    return spread, False


def lora_far_start(turned, n, after):
    arrived = [turned[0], swap(turned[1], n, NEAR)]
    for j in range(2, len(turned) - 1):
        arrived.append(swap(hold(turned[j], after), n, j * NEAR))
    return arrived


def lora_order(arrived, n, after):
    return call(
        lora_order_kernel,
        shape((n,) + arrived[0].shape[1:], bf16),
        [VMEM] * (1 + len(arrived)),
        after,
        *arrived,
        nanos=FILL,
    )


def lora_join(ordered, inner_width):
    n = ordered.shape[0]
    return call(
        lora_join_kernel,
        (
            shape((3 * ADAPTER_RANK, n * HEAD_WIDTH), bf16),
            shape((n * inner_width, HEAD_WIDTH), bf16),
        ),
        [VMEM] * 2,
        ordered,
        lax.ppermute(ordered, "grp", [(0, 1), (1, 0)]),
        nanos=LATE,
    )


def body(
    resid,
    queries,
    incoming_key_value,
    key_value_cache,
    lengths,
    norm_scale_vector,
    expert_choice,
    router_probability,
    gate_weight,
    up_weight,
    down_weight,
    adapter_model,
    adapter_hidden,
):
    n = lax.axis_size("exp")
    far = n // NEAR

    slots = 2 * far
    first_inputs = (queries, resid)
    message = call(
        pack_kernel,
        shape((1,) + MESSAGE, bf16),
        [HBM] * 2,
        *[pltpu.with_memory_space_constraint(x, pltpu.HBM) for x in first_inputs],
        scratch=[pltpu.VMEM(x.shape, x.dtype) for x in first_inputs]
        + [pltpu.SemaphoreType.DMA((2,))],
        nanos=4000,
    )
    marks, distance = [message], n // 2
    while distance > 2:
        message = call(
            join_kernel,
            shape((2 * message.shape[0],) + MESSAGE, bf16),
            [VMEM] * 2,
            message,
            swap(message, n, distance),
        )
        marks.append(message)
        distance //= 2
    turned, whole = lora_near(adapter_model, adapter_hidden, n, marks)
    residuals, near = call(
        narrow_kernel,
        (shape((slots,) + HEADS, bf16), shape((slots + 1,) + HEADS, bf16)),
        [VMEM] * 4,
        turned[0],
        message,
        swap(message, n, 2),
        incoming_key_value,
    )
    if not whole:
        arrived = lora_far_start(turned, n, near)
    next_near = swap(near, n, 1)
    partial = shape((slots + stat_tiles(slots),) + HEADS, bf16)
    keep, send = call(
        functools.partial(attend_kernel, far=far),
        (partial,) * 2,
        [VMEM, SMEM] + [VMEM] * 3,
        turned[0] if whole else arrived[1],
        lengths,
        near,
        next_near,
        key_value_cache,
        nanos=8000,
    )
    gates = call(
        gate_kernel,
        shape((1, HEAD_WIDTH), f32),
        [VMEM] * 3,
        keep,
        expert_choice,
        router_probability,
    )
    theirs, flip, distance = swap(send, n, 1), 0, 2
    after = gates
    while distance < n:
        keep = call(
            functools.partial(merge_kernel, slots=slots, flip=flip),
            partial,
            [VMEM] * 3,
            after,
            keep,
            theirs,
            nanos=MERGE,
        )
        if distance == 2 and not whole:
            after = arrived[-1]
            last = hold(turned[-1], keep)
            arrived.append(swap(last, n, n - NEAR))
        if distance == n // 4:
            after = turned[0] if whole else lora_order(arrived, n, keep)
        theirs = swap(keep, n, distance)
        flip = slots // distance
        distance *= 2
    ordered = after
    hidden, normed = call(
        token_kernel,
        (shape(HEADS, f32), shape((slots,) + HEADS, bf16)),
        [VMEM] * 4,
        keep,
        theirs,
        residuals,
        norm_scale_vector.reshape(HEADS),
        nanos=TOKEN,
    )
    model, inner = turned if whole else lora_join(ordered, adapter_hidden.shape[2])
    out = call(
        functools.partial(expert_kernel, far=far),
        shape((n,) + HEADS, bf16),
        [VMEM] * 7,
        normed,
        swap(normed, n, 1),
        gate_weight[0],
        up_weight[0],
        down_weight[0],
        model,
        inner,
        limit=32,
    )
    return call(
        finish_kernel,
        shape((1, WIDTH), bf16),
        [VMEM] * 3,
        hidden,
        lax.all_to_all(out, "exp", split_axis=0, concat_axis=0, tiled=True),
        gates,
    )


def solution(mesh):
    return jax.shard_map(
        body,
        mesh=mesh,
        in_specs=(
            P(("grp", "exp"), None),
            P(("grp", "exp"), None),
            P(("grp", "exp"), None),
            P("grp", "exp", None),
            P("grp"),
            P(),
            P(("grp", "exp"), None),
            P(("grp", "exp"), None),
            P("exp", None, None),
            P("exp", None, None),
            P("exp", None, None),
            P(None, None, "exp"),
            P(None, None, "exp"),
        ),
        out_specs=P(("grp", "exp"), None),
        check_vma=False,
    )
```

```python
import functools

import jax
import jax.numpy as jnp
from jax import lax
from jax.experimental import pallas as pl
from jax.experimental.pallas import tpu as pltpu
from jax.sharding import PartitionSpec as P

QUERY_HEADS = 16
KEY_VALUE_HEADS = 2
HEAD_WIDTH = 128
ADAPTER_RANK = 32
GROUPED = QUERY_HEADS // KEY_VALUE_HEADS
KEY_VALUE_WIDTH = KEY_VALUE_HEADS * HEAD_WIDTH
WIDTH = QUERY_HEADS * HEAD_WIDTH
INV_ROOT = HEAD_WIDTH ** (-0.5)
NEAR = 4
NEW_ROWS = 2 * KEY_VALUE_HEADS
HEADS = (QUERY_HEADS, HEAD_WIDTH)
MESSAGE = (2 * QUERY_HEADS, HEAD_WIDTH)

floor_score = -1e30
epsilon = 1e-06
FILL = 20
LATE = 20
TOKEN = 50
MERGE = 2500
JOIN = 1600

VMEM = pl.BlockSpec(memory_space=pltpu.VMEM)
SMEM = pl.BlockSpec(memory_space=pltpu.SMEM)
HBM = pl.BlockSpec(memory_space=pltpu.HBM)
shape = jax.ShapeDtypeStruct
bf16, f32 = jnp.bfloat16, jnp.float32


def call(kernel, shapes, specs, *args, limit=8, scratch=(), nanos=JOIN):
    return pl.pallas_call(
        kernel,
        out_shape=shapes,
        in_specs=specs,
        out_specs=jax.tree.map(lambda _: VMEM, shapes),
        scratch_shapes=scratch,
        cost_estimate=pl.CostEstimate(
            flops=nanos * 1000000, transcendentals=0, bytes_accessed=0
        ),
        compiler_params=pltpu.CompilerParams(vmem_limit_bytes=limit * 1024 * 1024),
    )(*args)


def hold_kernel(value, after, out):
    out[...] = value[...]


def hold(value, after):
    return call(
        hold_kernel, shape(value.shape, value.dtype), [VMEM] * 2, value, after, nanos=FILL
    )


def iota(dims, dim):
    return lax.broadcasted_iota(jnp.int32, dims, dim)


def as_rows(line, rows):
    return jnp.concatenate(
        [line[:, j * HEAD_WIDTH : (j + 1) * HEAD_WIDTH] for j in range(rows)], axis=0
    )


def swap(value, n, distance):
    return lax.ppermute(value, "exp", [(t, t ^ distance) for t in range(n)])


def distance_of(column, far):
    bits = far.bit_length() - 1
    return sum(NEAR << i for i in range(bits) if column >> (bits - 1 - i) & 1)


def pad16(rows):
    return -(-rows // 16) * 16


def stat_tiles(slots):
    return 1 if 6 * slots <= HEAD_WIDTH else 3


def pack_kernel(query, resid, out, q_in, r_in, sems):
    copies = [
        pltpu.make_async_copy(source, target, sems.at[k])
        for k, (source, target) in enumerate(((query, q_in), (resid, r_in)))
    ]
    for copy in copies:
        copy.start()
    for copy in copies:
        copy.wait()
    q = as_rows(q_in[...].astype(f32), QUERY_HEADS)
    r = as_rows(r_in[...].astype(f32), QUERY_HEADS)
    out[0] = jnp.concatenate([q, r], axis=0).astype(bf16)


def join_kernel(mine, theirs, out):
    half = mine.shape[0]
    out[:half] = mine[...]
    out[half:] = theirs[...]


def narrow_kernel(after, mine, theirs, new, residuals, out):
    half = mine.shape[0]
    for k, source in enumerate((mine, theirs)):
        for w in range(half):
            slot = k * half + w
            out[slot] = source[w, :QUERY_HEADS]
            residuals[slot] = source[w, QUERY_HEADS:]
    fresh = as_rows(new[...].astype(f32), NEW_ROWS)
    rest = jnp.zeros((QUERY_HEADS - NEW_ROWS, HEAD_WIDTH), f32)
    out[2 * half] = jnp.concatenate([fresh, rest], axis=0).astype(bf16)


def split_three(value):
    parts = []
    for _ in range(3):
        part = value.astype(bf16).astype(f32)
        parts.append(part)
        value = value - part
    return parts


def turned_to(value, lane):
    return pltpu.roll(value, lane % HEAD_WIDTH, 1) if lane % HEAD_WIDTH else value


def write_stats(groups, out, slots):
    single = stat_tiles(slots) == 1
    copies = 3 if single else 1
    spread = sum(
        turned_to(value, 2 * slots * k + at) for k in range(copies) for at, value in groups
    )
    parts = split_three(spread)
    if single:
        lanes = iota(HEADS, 1)
        low = jnp.where(lanes < 4 * slots, parts[1], parts[2])
        out[slots] = jnp.where(lanes < 2 * slots, parts[0], low).astype(bf16)
    else:
        for k in range(3):
            out[slots + k] = parts[k].astype(bf16)


def read_stats(message, slots):
    if stat_tiles(slots) == 1:
        tile = message[slots].astype(f32)
        return [sum(turned_to(tile, -2 * slots * k - at) for k in range(3)) for at in (0, slots)]
    stats = sum(message[slots + k].astype(f32) for k in range(3))
    return [stats, turned_to(stats, -slots)]


def flipped(value, flip):
    if not flip:
        return value
    ahead = pltpu.roll(value, HEAD_WIDTH - flip, 1)
    behind = pltpu.roll(value, flip, 1)
    return jnp.where((iota(HEADS, 1) & flip) == 0, ahead, behind)


def merged(mine, theirs, slots, flip):
    top, total = read_stats(mine, slots)
    other_top, other_total = (flipped(x, flip) for x in read_stats(theirs, slots))
    peak = jnp.maximum(top, other_top)
    share, other_share = jnp.exp(top - peak), jnp.exp(other_top - peak)
    total = share * total + other_share * other_total

    def acc(slot):
        return share[:, slot : slot + 1] * mine[slot].astype(f32) + other_share[
            :, slot : slot + 1
        ] * theirs[slot ^ flip].astype(f32)

    return peak, total, acc


def merge_kernel(after, mine, theirs, out, *, slots, flip):
    peak, total, acc = merged(mine, theirs, slots, flip)
    lanes = iota(HEADS, 1)
    peak, total = jnp.where(lanes < slots, peak, 0.0), jnp.where(lanes < slots, total, 0.0)
    write_stats([(0, peak), (slots, total)], out, slots)
    for slot in range(slots):
        out[slot] = acc(slot).astype(bf16)


def fresh_block(mine, theirs, me):
    slots = mine.shape[0] - 1
    second = me % 2 == 1
    first_group = iota(HEADS, 0) < GROUPED

    def by_head(rows, at):
        return jnp.where(first_group, rows[at : at + 1], rows[at + 1 : at + 2])

    q = mine[0].astype(f32)
    own, other = mine[slots].astype(f32), theirs[slots].astype(f32)
    own_score = jnp.sum(q * by_head(own, 0), axis=1, keepdims=True) * INV_ROOT
    other_score = jnp.sum(q * by_head(other, 0), axis=1, keepdims=True) * INV_ROOT
    other_score = jnp.where(second, other_score, floor_score)
    top = jnp.maximum(own_score, other_score)
    own_weight = jnp.exp(own_score - top).astype(bf16).astype(f32)
    other_weight = jnp.where(second, jnp.exp(other_score - top), 0.0).astype(bf16).astype(f32)
    acc = own_weight * by_head(own, 2) + other_weight * by_head(other, 2)
    return top, own_weight + other_weight, acc


def attend_kernel(after, lengths, mine, theirs, cache, keep, send, *, far):
    me = lax.axis_index("exp")
    sequences, block, _ = cache.shape
    rows = 2 * QUERY_HEADS
    first_group = (iota((rows, HEAD_WIDTH), 0) % QUERY_HEADS) < GROUPED
    positions = me * block + iota((rows, block), 1)
    lanes = iota(HEADS, 1)
    fresh = fresh_block(mine, theirs, me)
    stats = [jnp.zeros(HEADS, f32), jnp.zeros(HEADS, f32)]
    batch = 8 if sequences % 8 == 0 else 1
    for base in range(0, sequences, batch):
        slots = range(base, base + batch)
        where = [
            lax.shift_right_logical(me, 1)
            ^ ((distance_of(slot % far, far) >> 1) | (slot // far))
            for slot in slots
        ]
        scores, valid = [], []
        for slot, s in zip(slots, where):
            both = jnp.concatenate([mine[slot], theirs[slot]], axis=0)
            zero = jnp.zeros_like(both)
            wide = jnp.concatenate(
                [jnp.where(first_group, both, zero), jnp.where(first_group, zero, both)], axis=1
            )
            product = lax.dot_general(
                wide,
                cache[s, :, :KEY_VALUE_WIDTH],
                (((1,), (1,)), ((), ())),
                preferred_element_type=f32,
            )
            valid.append(positions < lengths[s])
            scores.append(jnp.where(valid[-1], product * INV_ROOT, floor_score))
        tops = [jnp.max(score, axis=1, keepdims=True) for score in scores]
        weights = [
            jnp.where(ok, jnp.exp(score - top), 0.0).astype(bf16)
            for ok, score, top in zip(valid, scores, tops)
        ]
        totals = [jnp.sum(weight.astype(f32), axis=1, keepdims=True) for weight in weights]
        accs = [
            jnp.dot(weight, cache[s, :, KEY_VALUE_WIDTH:], preferred_element_type=f32)
            for weight, s in zip(weights, where)
        ]
        for slot, top, total, acc in zip(slots, tops, totals, accs):
            acc = jnp.where(first_group, acc[:, :HEAD_WIDTH], acc[:, HEAD_WIDTH:])
            for k, part in enumerate((keep, send)):
                cut = slice(k * QUERY_HEADS, (k + 1) * QUERY_HEADS)
                t, z, a = top[cut], total[cut], acc[cut]
                if slot == 0 and k == 0:
                    peak = jnp.maximum(t, fresh[0])
                    old, young = jnp.exp(t - peak), jnp.exp(fresh[0] - peak)
                    t, z, a = peak, old * z + young * fresh[1], old * a + young * fresh[2]
                part[slot] = a.astype(bf16)
                stats[k] = jnp.where(lanes == slot, t, stats[k])
                stats[k] = jnp.where(lanes == sequences + slot, z, stats[k])
    for k, part in enumerate((keep, send)):
        write_stats([(0, stats[k])], part, sequences)


def token_kernel(mine, theirs, residuals, scale, hidden_out, normed_out):
    slots = residuals.shape[0]
    _, total, acc = merged(mine, theirs, slots, 1)
    inverse = 1.0 / jnp.where(iota(HEADS, 1) < slots, total, 1.0)
    for slot in range(slots):
        hidden = residuals[slot].astype(f32) + acc(slot) * inverse[:, slot : slot + 1]
        squares = jnp.sum(jnp.sum(hidden * hidden, axis=1, keepdims=True), axis=0, keepdims=True)
        normed = hidden * lax.rsqrt(squares / WIDTH + epsilon) * scale[...]
        if slot == 0:
            hidden_out[...] = hidden
        normed_out[slot] = normed.astype(bf16)


def dot_pair(value, factor, contract):
    high = value.astype(bf16)
    low = (value - high.astype(f32)).astype(bf16)
    both = lax.dot_general(
        jnp.concatenate([high, low], axis=0),
        factor,
        (((1,), (contract,)), ((), ())),
        preferred_element_type=f32,
    )
    return both[: value.shape[0]] + both[value.shape[0] :]


def expert_kernel(mine, theirs, gate_w, up_w, down_w, model, inner, out, *, far):
    me = lax.axis_index("exp")
    half = mine.shape[0]
    x = jnp.concatenate([mine[...].astype(f32), theirs[...].astype(f32)], axis=0)
    x = x.reshape(2 * half, WIDTH).astype(bf16)
    r = ADAPTER_RANK
    mixed = lax.dot_general(
        x, model[: 2 * r], (((1,), (1,)), ((), ())), preferred_element_type=f32
    )
    gate = jnp.dot(x, gate_w[...], preferred_element_type=f32)
    gate = gate + dot_pair(mixed[:, :r], inner[:, :r], 1)
    up = jnp.dot(x, up_w[...], preferred_element_type=f32)
    up = up + dot_pair(mixed[:, r:], inner[:, r : 2 * r], 1)
    act = (gate / (1.0 + jnp.exp(-gate)) * up).astype(bf16)
    lowered = jnp.dot(act, inner[:, 2 * r : 3 * r], preferred_element_type=f32)
    result = jnp.dot(act, down_w[...], preferred_element_type=f32)
    result = result + dot_pair(lowered, model[2 * r :], 0)
    for c in range(2):
        for y in range(2):
            for w in range(far):
                slot = (c * 2 + y) * far + w
                line = as_rows(result[slot : slot + 1], QUERY_HEADS)
                out[me ^ (distance_of(w, far) | 2 * y | c)] = line.astype(bf16)


def gate_kernel(after, choice, probability, out):
    p = probability[...]
    shares = p / jnp.sum(p, axis=1, keepdims=True)
    lanes = iota((1, HEAD_WIDTH), 1)
    gates = jnp.zeros((1, HEAD_WIDTH), f32)
    for k in range(p.shape[1]):
        gates = gates + jnp.where(choice[:, k : k + 1] == lanes, shares[:, k : k + 1], 0.0)
    out[...] = gates.astype(bf16).astype(f32)


def finish_kernel(hidden, got, gates, out):
    total = hidden[...]
    for e in range(got.shape[0]):
        total = total + gates[:, e : e + 1] * got[e].astype(f32)
    line = jnp.concatenate([total[j : j + 1] for j in range(QUERY_HEADS)], axis=1)
    out[...] = line.astype(bf16)


def without(index, bit):
    return (index // (2 * bit)) * bit + index % bit


def lora_pack_kernel(after, model, inner, keep, send, *, bit):
    me, first = lax.axis_index("exp"), lax.axis_index("grp") == 0
    ranks, split = model.shape[1], model.shape[1] // 2
    most = keep.shape[1] - split
    rest = inner.shape[1] - most
    for out in (keep, send):
        out[:, split:, ranks:] = jnp.zeros((out.shape[0], most, HEAD_WIDTH - ranks), out.dtype)
    for d in range(model.shape[0]):
        out, at, source = (send if d & bit else keep), without(d, bit), me ^ d
        out[at, :split] = jnp.where(first, model[source, :split], model[source, split:])
        lower = inner[source, most:]
        if rest < most:
            pad = jnp.zeros((most - rest, ranks), out.dtype)
            lower = jnp.concatenate([lower, pad], axis=0)
        out[at, split:, :ranks] = jnp.where(first, inner[source, :most], lower)


def lora_turn_kernel(after, kept, got, keep, send, *, bit, following):
    for d in range(2 * kept.shape[0]):
        value = (got if d & bit else kept)[without(d, bit)]
        (send if d & following else keep)[without(d, following)] = value


def lora_spread_kernel(after, kept, got, *outs, bit):
    for d in range(2 * kept.shape[0]):
        outs[d // NEAR][d % NEAR] = (got if d & bit else kept)[without(d, bit)]


def lora_order_kernel(after, *refs):
    me = lax.axis_index("exp")
    got, out = refs[:-1], refs[-1]
    for j, ref in enumerate(got):
        for l in range(NEAR):
            out[me ^ (j * NEAR + l)] = ref[l]


def lora_join_kernel(mine, theirs, model, inner):
    first = lax.axis_index("grp") == 0
    split = model.shape[0] // 2
    most, width = mine.shape[1] - split, inner.shape[0] // mine.shape[0]
    for at in range(mine.shape[0]):
        own, other = mine[at], theirs[at]
        halves = jnp.where(first, own, other), jnp.where(first, other, own)
        columns = slice(at * HEAD_WIDTH, (at + 1) * HEAD_WIDTH)
        model[:split, columns] = halves[0][:split]
        model[split:, columns] = halves[1][:split]
        inner[at * width : at * width + most] = halves[0][split:]
        inner[at * width + most : (at + 1) * width] = halves[1][split : split + width - most]


def lora_near(adapter_model, adapter_hidden, n, marks):
    total, ranks, model_width = adapter_model.shape
    inner_width = adapter_hidden.shape[2]
    inner = jnp.transpose(adapter_hidden, (0, 2, 1))
    if model_width != HEAD_WIDTH or inner_width % 16 or lax.axis_size("grp") != 2:
        model = lax.all_to_all(adapter_model, "exp", split_axis=0, concat_axis=2, tiled=True)
        inner = lax.all_to_all(inner, "exp", split_axis=0, concat_axis=1, tiled=True)
        return [model[0], inner[0]], True
    far = n // NEAR
    block = (ranks // 2 + pad16(inner_width // 2), HEAD_WIDTH)
    halves = (shape((n // 2,) + block, bf16),) * 2
    keep, send = call(
        functools.partial(lora_pack_kernel, bit=2),
        halves,
        [VMEM] * 3,
        marks[0],
        adapter_model,
        inner,
        nanos=FILL,
    )
    keep, send = call(
        functools.partial(lora_turn_kernel, bit=2, following=1),
        halves,
        [VMEM] * 3,
        marks[1],
        keep,
        swap(send, n, 2),
        nanos=FILL,
    )
    spread = call(
        functools.partial(lora_spread_kernel, bit=1),
        (shape((NEAR,) + block, bf16),) * (n // NEAR),
        [VMEM] * 3,
        marks[2],
        keep,
        swap(send, n, 1),
        nanos=FILL,
    )
    return spread, False


def lora_far_start(turned, n, after):
    arrived = [turned[0], swap(turned[1], n, NEAR)]
    for j in range(2, len(turned) - 1):
        arrived.append(swap(hold(turned[j], after), n, j * NEAR))
    return arrived


def lora_order(arrived, n, after):
    return call(
        lora_order_kernel,
        shape((n,) + arrived[0].shape[1:], bf16),
        [VMEM] * (1 + len(arrived)),
        after,
        *arrived,
        nanos=FILL,
    )


def lora_join(ordered, inner_width):
    n = ordered.shape[0]
    return call(
        lora_join_kernel,
        (
            shape((3 * ADAPTER_RANK, n * HEAD_WIDTH), bf16),
            shape((n * inner_width, HEAD_WIDTH), bf16),
        ),
        [VMEM] * 2,
        ordered,
        lax.ppermute(ordered, "grp", [(0, 1), (1, 0)]),
        nanos=LATE,
    )


def body(
    resid,
    queries,
    incoming_key_value,
    key_value_cache,
    lengths,
    norm_scale_vector,
    expert_choice,
    router_probability,
    gate_weight,
    up_weight,
    down_weight,
    adapter_model,
    adapter_hidden,
):
    n = lax.axis_size("exp")
    far = n // NEAR

    slots = 2 * far
    first_inputs = (queries, resid)
    message = call(
        pack_kernel,
        shape((1,) + MESSAGE, bf16),
        [HBM] * 2,
        *[pltpu.with_memory_space_constraint(x, pltpu.HBM) for x in first_inputs],
        scratch=[pltpu.VMEM(x.shape, x.dtype) for x in first_inputs]
        + [pltpu.SemaphoreType.DMA((2,))],
        nanos=4000,
    )
    marks, distance = [message], n // 2
    while distance > 2:
        message = call(
            join_kernel,
            shape((2 * message.shape[0],) + MESSAGE, bf16),
            [VMEM] * 2,
            message,
            swap(message, n, distance),
        )
        marks.append(message)
        distance //= 2
    turned, whole = lora_near(adapter_model, adapter_hidden, n, marks)
    residuals, near = call(
        narrow_kernel,
        (shape((slots,) + HEADS, bf16), shape((slots + 1,) + HEADS, bf16)),
        [VMEM] * 4,
        turned[0],
        message,
        swap(message, n, 2),
        incoming_key_value,
    )
    if not whole:
        arrived = lora_far_start(turned, n, near)
    next_near = swap(near, n, 1)
    partial = shape((slots + stat_tiles(slots),) + HEADS, bf16)
    keep, send = call(
        functools.partial(attend_kernel, far=far),
        (partial,) * 2,
        [VMEM, SMEM] + [VMEM] * 3,
        turned[0] if whole else arrived[1],
        lengths,
        near,
        next_near,
        key_value_cache,
        nanos=8000,
    )
    gates = call(
        gate_kernel,
        shape((1, HEAD_WIDTH), f32),
        [VMEM] * 3,
        keep,
        expert_choice,
        router_probability,
    )
    theirs, flip, distance = swap(send, n, 1), 0, 2
    after = gates
    while distance < n:
        keep = call(
            functools.partial(merge_kernel, slots=slots, flip=flip),
            partial,
            [VMEM] * 3,
            after,
            keep,
            theirs,
            nanos=MERGE,
        )
        if distance == 2 and not whole:
            after = arrived[-1]
            last = hold(turned[-1], keep)
            arrived.append(swap(last, n, n - NEAR))
        if distance == n // 4:
            after = turned[0] if whole else lora_order(arrived, n, keep)
        theirs = swap(keep, n, distance)
        flip = slots // distance
        distance *= 2
    ordered = after
    hidden, normed = call(
        token_kernel,
        (shape(HEADS, f32), shape((slots,) + HEADS, bf16)),
        [VMEM] * 4,
        keep,
        theirs,
        residuals,
        norm_scale_vector.reshape(HEADS),
        nanos=TOKEN,
    )
    model, inner = turned if whole else lora_join(ordered, adapter_hidden.shape[2])
    out = call(
        functools.partial(expert_kernel, far=far),
        shape((n,) + HEADS, bf16),
        [VMEM] * 7,
        normed,
        swap(normed, n, 1),
        gate_weight[0],
        up_weight[0],
        down_weight[0],
        model,
        inner,
        limit=32,
    )
    return call(
        finish_kernel,
        shape((1, WIDTH), bf16),
        [VMEM] * 3,
        hidden,
        lax.all_to_all(out, "exp", split_axis=0, concat_axis=0, tiled=True),
        gates,
    )


def solution(mesh):
    return jax.shard_map(
        body,
        mesh=mesh,
        in_specs=(
            P(("grp", "exp"), None),
            P(("grp", "exp"), None),
            P(("grp", "exp"), None),
            P("grp", "exp", None),
            P("grp"),
            P(),
            P(("grp", "exp"), None),
            P(("grp", "exp"), None),
            P("exp", None, None),
            P("exp", None, None),
            P("exp", None, None),
            P(None, None, "exp"),
            P(None, None, "exp"),
        ),
        out_specs=P(("grp", "exp"), None),
        check_vma=False,
    )
```

```python
import functools

import jax
import jax.numpy as jnp
from jax import lax
from jax.experimental import pallas as pl
from jax.experimental.pallas import tpu as pltpu
from jax.sharding import PartitionSpec as P

QUERY_HEADS = 16
KEY_VALUE_HEADS = 2
HEAD_WIDTH = 128
ADAPTER_RANK = 32
GROUPED = QUERY_HEADS // KEY_VALUE_HEADS
KEY_VALUE_WIDTH = KEY_VALUE_HEADS * HEAD_WIDTH
WIDTH = QUERY_HEADS * HEAD_WIDTH
INV_ROOT = HEAD_WIDTH ** (-0.5)
NEAR = 4
NEW_ROWS = 2 * KEY_VALUE_HEADS
HEADS = (QUERY_HEADS, HEAD_WIDTH)
MESSAGE = (2 * QUERY_HEADS, HEAD_WIDTH)

floor_score = -1e30
epsilon = 1e-06
FILL = 20
LATE = 20
TOKEN = 50
MERGE = 2500
JOIN = 1600

VMEM = pl.BlockSpec(memory_space=pltpu.VMEM)
SMEM = pl.BlockSpec(memory_space=pltpu.SMEM)
HBM = pl.BlockSpec(memory_space=pltpu.HBM)
shape = jax.ShapeDtypeStruct
bf16, f32 = jnp.bfloat16, jnp.float32


def call(kernel, shapes, specs, *args, limit=8, scratch=(), nanos=JOIN):
    return pl.pallas_call(
        kernel,
        out_shape=shapes,
        in_specs=specs,
        out_specs=jax.tree.map(lambda _: VMEM, shapes),
        scratch_shapes=scratch,
        cost_estimate=pl.CostEstimate(
            flops=nanos * 1000000, transcendentals=0, bytes_accessed=0
        ),
        compiler_params=pltpu.CompilerParams(vmem_limit_bytes=limit * 1024 * 1024),
    )(*args)


def hold_kernel(value, after, out):
    out[...] = value[...]


def hold(value, after):
    return call(
        hold_kernel, shape(value.shape, value.dtype), [VMEM] * 2, value, after, nanos=FILL
    )


def iota(dims, dim):
    return lax.broadcasted_iota(jnp.int32, dims, dim)


def as_rows(line, rows):
    return jnp.concatenate(
        [line[:, j * HEAD_WIDTH : (j + 1) * HEAD_WIDTH] for j in range(rows)], axis=0
    )


def swap(value, n, distance):
    return lax.ppermute(value, "exp", [(t, t ^ distance) for t in range(n)])


def distance_of(column, far):
    bits = far.bit_length() - 1
    return sum(NEAR << i for i in range(bits) if column >> (bits - 1 - i) & 1)


def pad16(rows):
    return -(-rows // 16) * 16


def stat_tiles(slots):
    return 1 if 6 * slots <= HEAD_WIDTH else 3


def pack_kernel(query, resid, out, q_in, r_in, sems):
    copies = [
        pltpu.make_async_copy(source, target, sems.at[k])
        for k, (source, target) in enumerate(((query, q_in), (resid, r_in)))
    ]
    for copy in copies:
        copy.start()
    for copy in copies:
        copy.wait()
    q = as_rows(q_in[...].astype(f32), QUERY_HEADS)
    r = as_rows(r_in[...].astype(f32), QUERY_HEADS)
    out[0] = jnp.concatenate([q, r], axis=0).astype(bf16)


def join_kernel(mine, theirs, out):
    half = mine.shape[0]
    out[:half] = mine[...]
    out[half:] = theirs[...]


def narrow_kernel(after, mine, theirs, new, residuals, out):
    half = mine.shape[0]
    for k, source in enumerate((mine, theirs)):
        for w in range(half):
            slot = k * half + w
            out[slot] = source[w, :QUERY_HEADS]
            residuals[slot] = source[w, QUERY_HEADS:]
    fresh = as_rows(new[...].astype(f32), NEW_ROWS)
    rest = jnp.zeros((QUERY_HEADS - NEW_ROWS, HEAD_WIDTH), f32)
    out[2 * half] = jnp.concatenate([fresh, rest], axis=0).astype(bf16)


def split_three(value):
    parts = []
    for _ in range(3):
        part = value.astype(bf16).astype(f32)
        parts.append(part)
        value = value - part
    return parts


def turned_to(value, lane):
    return pltpu.roll(value, lane % HEAD_WIDTH, 1) if lane % HEAD_WIDTH else value


def write_stats(groups, out, slots):
    single = stat_tiles(slots) == 1
    copies = 3 if single else 1
    spread = sum(
        turned_to(value, 2 * slots * k + at) for k in range(copies) for at, value in groups
    )
    parts = split_three(spread)
    if single:
        lanes = iota(HEADS, 1)
        low = jnp.where(lanes < 4 * slots, parts[1], parts[2])
        out[slots] = jnp.where(lanes < 2 * slots, parts[0], low).astype(bf16)
    else:
        for k in range(3):
            out[slots + k] = parts[k].astype(bf16)


def read_stats(message, slots):
    if stat_tiles(slots) == 1:
        tile = message[slots].astype(f32)
        return [sum(turned_to(tile, -2 * slots * k - at) for k in range(3)) for at in (0, slots)]
    stats = sum(message[slots + k].astype(f32) for k in range(3))
    return [stats, turned_to(stats, -slots)]


def flipped(value, flip):
    if not flip:
        return value
    ahead = pltpu.roll(value, HEAD_WIDTH - flip, 1)
    behind = pltpu.roll(value, flip, 1)
    return jnp.where((iota(HEADS, 1) & flip) == 0, ahead, behind)


def merged(mine, theirs, slots, flip):
    top, total = read_stats(mine, slots)
    other_top, other_total = (flipped(x, flip) for x in read_stats(theirs, slots))
    peak = jnp.maximum(top, other_top)
    share, other_share = jnp.exp(top - peak), jnp.exp(other_top - peak)
    total = share * total + other_share * other_total

    def acc(slot):
        return share[:, slot : slot + 1] * mine[slot].astype(f32) + other_share[
            :, slot : slot + 1
        ] * theirs[slot ^ flip].astype(f32)

    return peak, total, acc


def merge_kernel(after, mine, theirs, out, *, slots, flip):
    peak, total, acc = merged(mine, theirs, slots, flip)
    lanes = iota(HEADS, 1)
    peak, total = jnp.where(lanes < slots, peak, 0.0), jnp.where(lanes < slots, total, 0.0)
    write_stats([(0, peak), (slots, total)], out, slots)
    for slot in range(slots):
        out[slot] = acc(slot).astype(bf16)


def fresh_block(mine, theirs, me):
    slots = mine.shape[0] - 1
    second = me % 2 == 1
    first_group = iota(HEADS, 0) < GROUPED

    def by_head(rows, at):
        return jnp.where(first_group, rows[at : at + 1], rows[at + 1 : at + 2])

    q = mine[0].astype(f32)
    own, other = mine[slots].astype(f32), theirs[slots].astype(f32)
    own_score = jnp.sum(q * by_head(own, 0), axis=1, keepdims=True) * INV_ROOT
    other_score = jnp.sum(q * by_head(other, 0), axis=1, keepdims=True) * INV_ROOT
    other_score = jnp.where(second, other_score, floor_score)
    top = jnp.maximum(own_score, other_score)
    own_weight = jnp.exp(own_score - top).astype(bf16).astype(f32)
    other_weight = jnp.where(second, jnp.exp(other_score - top), 0.0).astype(bf16).astype(f32)
    acc = own_weight * by_head(own, 2) + other_weight * by_head(other, 2)
    return top, own_weight + other_weight, acc


def attend_kernel(after, lengths, mine, theirs, cache, keep, send, *, far):
    me = lax.axis_index("exp")
    sequences, block, _ = cache.shape
    rows = 2 * QUERY_HEADS
    first_group = (iota((rows, HEAD_WIDTH), 0) % QUERY_HEADS) < GROUPED
    positions = me * block + iota((rows, block), 1)
    lanes = iota(HEADS, 1)
    fresh = fresh_block(mine, theirs, me)
    stats = [jnp.zeros(HEADS, f32), jnp.zeros(HEADS, f32)]
    batch = 8 if sequences % 8 == 0 else 1
    for base in range(0, sequences, batch):
        slots = range(base, base + batch)
        where = [
            lax.shift_right_logical(me, 1)
            ^ ((distance_of(slot % far, far) >> 1) | (slot // far))
            for slot in slots
        ]
        scores, valid = [], []
        for slot, s in zip(slots, where):
            both = jnp.concatenate([mine[slot], theirs[slot]], axis=0)
            zero = jnp.zeros_like(both)
            wide = jnp.concatenate(
                [jnp.where(first_group, both, zero), jnp.where(first_group, zero, both)], axis=1
            )
            product = lax.dot_general(
                wide,
                cache[s, :, :KEY_VALUE_WIDTH],
                (((1,), (1,)), ((), ())),
                preferred_element_type=f32,
            )
            valid.append(positions < lengths[s])
            scores.append(jnp.where(valid[-1], product * INV_ROOT, floor_score))
        tops = [jnp.max(score, axis=1, keepdims=True) for score in scores]
        weights = [
            jnp.where(ok, jnp.exp(score - top), 0.0).astype(bf16)
            for ok, score, top in zip(valid, scores, tops)
        ]
        totals = [jnp.sum(weight.astype(f32), axis=1, keepdims=True) for weight in weights]
        accs = [
            jnp.dot(weight, cache[s, :, KEY_VALUE_WIDTH:], preferred_element_type=f32)
            for weight, s in zip(weights, where)
        ]
        for slot, top, total, acc in zip(slots, tops, totals, accs):
            acc = jnp.where(first_group, acc[:, :HEAD_WIDTH], acc[:, HEAD_WIDTH:])
            for k, part in enumerate((keep, send)):
                cut = slice(k * QUERY_HEADS, (k + 1) * QUERY_HEADS)
                t, z, a = top[cut], total[cut], acc[cut]
                if slot == 0 and k == 0:
                    peak = jnp.maximum(t, fresh[0])
                    old, young = jnp.exp(t - peak), jnp.exp(fresh[0] - peak)
                    t, z, a = peak, old * z + young * fresh[1], old * a + young * fresh[2]
                part[slot] = a.astype(bf16)
                stats[k] = jnp.where(lanes == slot, t, stats[k])
                stats[k] = jnp.where(lanes == sequences + slot, z, stats[k])
    for k, part in enumerate((keep, send)):
        write_stats([(0, stats[k])], part, sequences)


def token_kernel(mine, theirs, residuals, scale, hidden_out, normed_out):
    slots = residuals.shape[0]
    _, total, acc = merged(mine, theirs, slots, 1)
    inverse = 1.0 / jnp.where(iota(HEADS, 1) < slots, total, 1.0)
    for slot in range(slots):
        hidden = residuals[slot].astype(f32) + acc(slot) * inverse[:, slot : slot + 1]
        squares = jnp.sum(jnp.sum(hidden * hidden, axis=1, keepdims=True), axis=0, keepdims=True)
        normed = hidden * lax.rsqrt(squares / WIDTH + epsilon) * scale[...]
        if slot == 0:
            hidden_out[...] = hidden
        normed_out[slot] = normed.astype(bf16)


def dot_pair(value, factor, contract):
    high = value.astype(bf16)
    low = (value - high.astype(f32)).astype(bf16)
    both = lax.dot_general(
        jnp.concatenate([high, low], axis=0),
        factor,
        (((1,), (contract,)), ((), ())),
        preferred_element_type=f32,
    )
    return both[: value.shape[0]] + both[value.shape[0] :]


def expert_kernel(mine, theirs, gate_w, up_w, down_w, model, inner, out, *, far):
    me = lax.axis_index("exp")
    half = mine.shape[0]
    x = jnp.concatenate([mine[...].astype(f32), theirs[...].astype(f32)], axis=0)
    x = x.reshape(2 * half, WIDTH).astype(bf16)
    r = ADAPTER_RANK
    mixed = lax.dot_general(
        x, model[: 2 * r], (((1,), (1,)), ((), ())), preferred_element_type=f32
    )
    gate = jnp.dot(x, gate_w[...], preferred_element_type=f32)
    gate = gate + dot_pair(mixed[:, :r], inner[:, :r], 1)
    up = jnp.dot(x, up_w[...], preferred_element_type=f32)
    up = up + dot_pair(mixed[:, r:], inner[:, r : 2 * r], 1)
    act = (gate / (1.0 + jnp.exp(-gate)) * up).astype(bf16)
    lowered = jnp.dot(act, inner[:, 2 * r : 3 * r], preferred_element_type=f32)
    result = jnp.dot(act, down_w[...], preferred_element_type=f32)
    result = result + dot_pair(lowered, model[2 * r :], 0)
    for c in range(2):
        for y in range(2):
            for w in range(far):
                slot = (c * 2 + y) * far + w
                line = as_rows(result[slot : slot + 1], QUERY_HEADS)
                out[me ^ (distance_of(w, far) | 2 * y | c)] = line.astype(bf16)


def gate_kernel(after, choice, probability, out):
    p = probability[...]
    shares = p / jnp.sum(p, axis=1, keepdims=True)
    lanes = iota((1, HEAD_WIDTH), 1)
    gates = jnp.zeros((1, HEAD_WIDTH), f32)
    for k in range(p.shape[1]):
        gates = gates + jnp.where(choice[:, k : k + 1] == lanes, shares[:, k : k + 1], 0.0)
    out[...] = gates.astype(bf16).astype(f32)


def finish_kernel(hidden, got, gates, out):
    total = hidden[...]
    for e in range(got.shape[0]):
        total = total + gates[:, e : e + 1] * got[e].astype(f32)
    line = jnp.concatenate([total[j : j + 1] for j in range(QUERY_HEADS)], axis=1)
    out[...] = line.astype(bf16)


def without(index, bit):
    return (index // (2 * bit)) * bit + index % bit


def lora_pack_kernel(after, model, inner, keep, send, *, bit):
    me, first = lax.axis_index("exp"), lax.axis_index("grp") == 0
    ranks, split = model.shape[1], model.shape[1] // 2
    most = keep.shape[1] - split
    rest = inner.shape[1] - most
    for out in (keep, send):
        out[:, split:, ranks:] = jnp.zeros((out.shape[0], most, HEAD_WIDTH - ranks), out.dtype)
    for d in range(model.shape[0]):
        out, at, source = (send if d & bit else keep), without(d, bit), me ^ d
        out[at, :split] = jnp.where(first, model[source, :split], model[source, split:])
        lower = inner[source, most:]
        if rest < most:
            pad = jnp.zeros((most - rest, ranks), out.dtype)
            lower = jnp.concatenate([lower, pad], axis=0)
        out[at, split:, :ranks] = jnp.where(first, inner[source, :most], lower)


def lora_turn_kernel(after, kept, got, keep, send, *, bit, following):
    for d in range(2 * kept.shape[0]):
        value = (got if d & bit else kept)[without(d, bit)]
        (send if d & following else keep)[without(d, following)] = value


def lora_spread_kernel(after, kept, got, *outs, bit):
    for d in range(2 * kept.shape[0]):
        outs[d // NEAR][d % NEAR] = (got if d & bit else kept)[without(d, bit)]


def lora_order_kernel(after, *refs):
    me = lax.axis_index("exp")
    got, out = refs[:-1], refs[-1]
    for j, ref in enumerate(got):
        for l in range(NEAR):
            out[me ^ (j * NEAR + l)] = ref[l]


def lora_join_kernel(mine, theirs, model, inner):
    first = lax.axis_index("grp") == 0
    split = model.shape[0] // 2
    most, width = mine.shape[1] - split, inner.shape[0] // mine.shape[0]
    for at in range(mine.shape[0]):
        own, other = mine[at], theirs[at]
        halves = jnp.where(first, own, other), jnp.where(first, other, own)
        columns = slice(at * HEAD_WIDTH, (at + 1) * HEAD_WIDTH)
        model[:split, columns] = halves[0][:split]
        model[split:, columns] = halves[1][:split]
        inner[at * width : at * width + most] = halves[0][split:]
        inner[at * width + most : (at + 1) * width] = halves[1][split : split + width - most]


def lora_near(adapter_model, adapter_hidden, n, marks):
    total, ranks, model_width = adapter_model.shape
    inner_width = adapter_hidden.shape[2]
    inner = jnp.transpose(adapter_hidden, (0, 2, 1))
    if model_width != HEAD_WIDTH or inner_width % 16 or lax.axis_size("grp") != 2:
        model = lax.all_to_all(adapter_model, "exp", split_axis=0, concat_axis=2, tiled=True)
        inner = lax.all_to_all(inner, "exp", split_axis=0, concat_axis=1, tiled=True)
        return [model[0], inner[0]], True
    far = n // NEAR
    block = (ranks // 2 + pad16(inner_width // 2), HEAD_WIDTH)
    halves = (shape((n // 2,) + block, bf16),) * 2
    keep, send = call(
        functools.partial(lora_pack_kernel, bit=2),
        halves,
        [VMEM] * 3,
        marks[0],
        adapter_model,
        inner,
        nanos=FILL,
    )
    keep, send = call(
        functools.partial(lora_turn_kernel, bit=2, following=1),
        halves,
        [VMEM] * 3,
        marks[1],
        keep,
        swap(send, n, 2),
        nanos=FILL,
    )
    spread = call(
        functools.partial(lora_spread_kernel, bit=1),
        (shape((NEAR,) + block, bf16),) * (n // NEAR),
        [VMEM] * 3,
        marks[2],
        keep,
        swap(send, n, 1),
        nanos=FILL,
    )
    return spread, False


def lora_far_start(turned, n, after):
    most = len(turned) - 1
    arrived = [turned[0], swap(turned[most], n, most * NEAR)]
    for j in range(most - 1, 1, -1):
        arrived.append(swap(hold(turned[j], after), n, j * NEAR))
    return arrived


def lora_order(arrived, n, after):
    return call(
        lora_order_kernel,
        shape((n,) + arrived[0].shape[1:], bf16),
        [VMEM] * (1 + len(arrived)),
        after,
        *arrived,
        nanos=FILL,
    )


def lora_join(ordered, inner_width):
    n = ordered.shape[0]
    return call(
        lora_join_kernel,
        (
            shape((3 * ADAPTER_RANK, n * HEAD_WIDTH), bf16),
            shape((n * inner_width, HEAD_WIDTH), bf16),
        ),
        [VMEM] * 2,
        ordered,
        lax.ppermute(ordered, "grp", [(0, 1), (1, 0)]),
        nanos=LATE,
    )


def body(
    resid,
    queries,
    incoming_key_value,
    key_value_cache,
    lengths,
    norm_scale_vector,
    expert_choice,
    router_probability,
    gate_weight,
    up_weight,
    down_weight,
    adapter_model,
    adapter_hidden,
):
    n = lax.axis_size("exp")
    far = n // NEAR

    slots = 2 * far
    first_inputs = (queries, resid)
    message = call(
        pack_kernel,
        shape((1,) + MESSAGE, bf16),
        [HBM] * 2,
        *[pltpu.with_memory_space_constraint(x, pltpu.HBM) for x in first_inputs],
        scratch=[pltpu.VMEM(x.shape, x.dtype) for x in first_inputs]
        + [pltpu.SemaphoreType.DMA((2,))],
        nanos=4000,
    )
    marks, distance = [message], n // 2
    while distance > 2:
        message = call(
            join_kernel,
            shape((2 * message.shape[0],) + MESSAGE, bf16),
            [VMEM] * 2,
            message,
            swap(message, n, distance),
        )
        marks.append(message)
        distance //= 2
    turned, whole = lora_near(adapter_model, adapter_hidden, n, marks)
    residuals, near = call(
        narrow_kernel,
        (shape((slots,) + HEADS, bf16), shape((slots + 1,) + HEADS, bf16)),
        [VMEM] * 4,
        turned[0],
        message,
        swap(message, n, 2),
        incoming_key_value,
    )
    if not whole:
        arrived = lora_far_start(turned, n, near)
    next_near = swap(near, n, 1)
    partial = shape((slots + stat_tiles(slots),) + HEADS, bf16)
    keep, send = call(
        functools.partial(attend_kernel, far=far),
        (partial,) * 2,
        [VMEM, SMEM] + [VMEM] * 3,
        turned[0] if whole else arrived[1],
        lengths,
        near,
        next_near,
        key_value_cache,
        nanos=8000,
    )
    gates = call(
        gate_kernel,
        shape((1, HEAD_WIDTH), f32),
        [VMEM] * 3,
        keep,
        expert_choice,
        router_probability,
    )
    theirs, flip, distance = swap(send, n, 1), 0, 2
    after = gates
    while distance < n:
        keep = call(
            functools.partial(merge_kernel, slots=slots, flip=flip),
            partial,
            [VMEM] * 3,
            after,
            keep,
            theirs,
            nanos=MERGE,
        )
        if distance == 2 and not whole:
            after = arrived[-1]
            arrived.append(swap(hold(turned[1], keep), n, NEAR))
        if distance == n // 4:
            after = turned[0] if whole else lora_order([arrived[0]] + arrived[:0:-1], n, keep)
        theirs = swap(keep, n, distance)
        flip = slots // distance
        distance *= 2
    ordered = after
    hidden, normed = call(
        token_kernel,
        (shape(HEADS, f32), shape((slots,) + HEADS, bf16)),
        [VMEM] * 4,
        keep,
        theirs,
        residuals,
        norm_scale_vector.reshape(HEADS),
        nanos=TOKEN,
    )
    model, inner = turned if whole else lora_join(ordered, adapter_hidden.shape[2])
    out = call(
        functools.partial(expert_kernel, far=far),
        shape((n,) + HEADS, bf16),
        [VMEM] * 7,
        normed,
        swap(normed, n, 1),
        gate_weight[0],
        up_weight[0],
        down_weight[0],
        model,
        inner,
        limit=32,
    )
    return call(
        finish_kernel,
        shape((1, WIDTH), bf16),
        [VMEM] * 3,
        hidden,
        lax.all_to_all(out, "exp", split_axis=0, concat_axis=0, tiled=True),
        gates,
    )


def solution(mesh):
    return jax.shard_map(
        body,
        mesh=mesh,
        in_specs=(
            P(("grp", "exp"), None),
            P(("grp", "exp"), None),
            P(("grp", "exp"), None),
            P("grp", "exp", None),
            P("grp"),
            P(),
            P(("grp", "exp"), None),
            P(("grp", "exp"), None),
            P("exp", None, None),
            P("exp", None, None),
            P("exp", None, None),
            P(None, None, "exp"),
            P(None, None, "exp"),
        ),
        out_specs=P(("grp", "exp"), None),
        check_vma=False,
    )
```

```python
import functools

import jax
import jax.numpy as jnp
from jax import lax
from jax.experimental import pallas as pl
from jax.experimental.pallas import tpu as pltpu
from jax.sharding import PartitionSpec as P

QUERY_HEADS = 16
KEY_VALUE_HEADS = 2
HEAD_WIDTH = 128
ADAPTER_RANK = 32
GROUPED = QUERY_HEADS // KEY_VALUE_HEADS
KEY_VALUE_WIDTH = KEY_VALUE_HEADS * HEAD_WIDTH
WIDTH = QUERY_HEADS * HEAD_WIDTH
INV_ROOT = HEAD_WIDTH ** (-0.5)
NEAR = 4
NEW_ROWS = 2 * KEY_VALUE_HEADS
HEADS = (QUERY_HEADS, HEAD_WIDTH)
MESSAGE = (2 * QUERY_HEADS, HEAD_WIDTH)

floor_score = -1e30
epsilon = 1e-06
FILL = 20
LATE = 20
TOKEN = 50
MERGE = 2500
JOIN = 1600

VMEM = pl.BlockSpec(memory_space=pltpu.VMEM)
SMEM = pl.BlockSpec(memory_space=pltpu.SMEM)
HBM = pl.BlockSpec(memory_space=pltpu.HBM)
shape = jax.ShapeDtypeStruct
bf16, f32 = jnp.bfloat16, jnp.float32


def call(kernel, shapes, specs, *args, limit=8, scratch=(), nanos=JOIN):
    return pl.pallas_call(
        kernel,
        out_shape=shapes,
        in_specs=specs,
        out_specs=jax.tree.map(lambda _: VMEM, shapes),
        scratch_shapes=scratch,
        cost_estimate=pl.CostEstimate(
            flops=nanos * 1000000, transcendentals=0, bytes_accessed=0
        ),
        compiler_params=pltpu.CompilerParams(vmem_limit_bytes=limit * 1024 * 1024),
    )(*args)


def hold_kernel(value, after, out):
    out[...] = value[...]


def hold(value, after):
    return call(
        hold_kernel, shape(value.shape, value.dtype), [VMEM] * 2, value, after, nanos=FILL
    )


def iota(dims, dim):
    return lax.broadcasted_iota(jnp.int32, dims, dim)


def as_rows(line, rows):
    return jnp.concatenate(
        [line[:, j * HEAD_WIDTH : (j + 1) * HEAD_WIDTH] for j in range(rows)], axis=0
    )


def swap(value, n, distance):
    return lax.ppermute(value, "exp", [(t, t ^ distance) for t in range(n)])


def distance_of(column, far):
    bits = far.bit_length() - 1
    return sum(NEAR << i for i in range(bits) if column >> (bits - 1 - i) & 1)


def pad16(rows):
    return -(-rows // 16) * 16


def stat_tiles(slots):
    return 1 if 6 * slots <= HEAD_WIDTH else 3


def pack_kernel(query, resid, out, q_in, r_in, sems):
    copies = [
        pltpu.make_async_copy(source, target, sems.at[k])
        for k, (source, target) in enumerate(((query, q_in), (resid, r_in)))
    ]
    for copy in copies:
        copy.start()
    for copy in copies:
        copy.wait()
    q = as_rows(q_in[...].astype(f32), QUERY_HEADS)
    r = as_rows(r_in[...].astype(f32), QUERY_HEADS)
    out[0] = jnp.concatenate([q, r], axis=0).astype(bf16)


def join_kernel(mine, theirs, out):
    half = mine.shape[0]
    out[:half] = mine[...]
    out[half:] = theirs[...]


def narrow_kernel(after, mine, theirs, new, residuals, out):
    half = mine.shape[0]
    for k, source in enumerate((mine, theirs)):
        for w in range(half):
            slot = k * half + w
            out[slot] = source[w, :QUERY_HEADS]
            residuals[slot] = source[w, QUERY_HEADS:]
    fresh = as_rows(new[...].astype(f32), NEW_ROWS)
    rest = jnp.zeros((QUERY_HEADS - NEW_ROWS, HEAD_WIDTH), f32)
    out[2 * half] = jnp.concatenate([fresh, rest], axis=0).astype(bf16)


def split_three(value):
    parts = []
    for _ in range(3):
        part = value.astype(bf16).astype(f32)
        parts.append(part)
        value = value - part
    return parts


def turned_to(value, lane):
    return pltpu.roll(value, lane % HEAD_WIDTH, 1) if lane % HEAD_WIDTH else value


def write_stats(groups, out, slots):
    single = stat_tiles(slots) == 1
    copies = 3 if single else 1
    spread = sum(
        turned_to(value, 2 * slots * k + at) for k in range(copies) for at, value in groups
    )
    parts = split_three(spread)
    if single:
        lanes = iota(HEADS, 1)
        low = jnp.where(lanes < 4 * slots, parts[1], parts[2])
        out[slots] = jnp.where(lanes < 2 * slots, parts[0], low).astype(bf16)
    else:
        for k in range(3):
            out[slots + k] = parts[k].astype(bf16)


def read_stats(message, slots):
    if stat_tiles(slots) == 1:
        tile = message[slots].astype(f32)
        return [sum(turned_to(tile, -2 * slots * k - at) for k in range(3)) for at in (0, slots)]
    stats = sum(message[slots + k].astype(f32) for k in range(3))
    return [stats, turned_to(stats, -slots)]


def flipped(value, flip):
    if not flip:
        return value
    ahead = pltpu.roll(value, HEAD_WIDTH - flip, 1)
    behind = pltpu.roll(value, flip, 1)
    return jnp.where((iota(HEADS, 1) & flip) == 0, ahead, behind)


def merged(mine, theirs, slots, flip):
    top, total = read_stats(mine, slots)
    other_top, other_total = (flipped(x, flip) for x in read_stats(theirs, slots))
    peak = jnp.maximum(top, other_top)
    share, other_share = jnp.exp(top - peak), jnp.exp(other_top - peak)
    total = share * total + other_share * other_total

    def acc(slot):
        return share[:, slot : slot + 1] * mine[slot].astype(f32) + other_share[
            :, slot : slot + 1
        ] * theirs[slot ^ flip].astype(f32)

    return peak, total, acc


def merge_kernel(after, mine, theirs, out, *, slots, flip):
    peak, total, acc = merged(mine, theirs, slots, flip)
    lanes = iota(HEADS, 1)
    peak, total = jnp.where(lanes < slots, peak, 0.0), jnp.where(lanes < slots, total, 0.0)
    write_stats([(0, peak), (slots, total)], out, slots)
    for slot in range(slots):
        out[slot] = acc(slot).astype(bf16)


def fresh_block(mine, theirs, me):
    slots = mine.shape[0] - 1
    second = me % 2 == 1
    first_group = iota(HEADS, 0) < GROUPED

    def by_head(rows, at):
        return jnp.where(first_group, rows[at : at + 1], rows[at + 1 : at + 2])

    q = mine[0].astype(f32)
    own, other = mine[slots].astype(f32), theirs[slots].astype(f32)
    own_score = jnp.sum(q * by_head(own, 0), axis=1, keepdims=True) * INV_ROOT
    other_score = jnp.sum(q * by_head(other, 0), axis=1, keepdims=True) * INV_ROOT
    other_score = jnp.where(second, other_score, floor_score)
    top = jnp.maximum(own_score, other_score)
    own_weight = jnp.exp(own_score - top).astype(bf16).astype(f32)
    other_weight = jnp.where(second, jnp.exp(other_score - top), 0.0).astype(bf16).astype(f32)
    acc = own_weight * by_head(own, 2) + other_weight * by_head(other, 2)
    return top, own_weight + other_weight, acc


def attend_kernel(after, lengths, mine, theirs, cache, keep, send, *, far):
    me = lax.axis_index("exp")
    sequences, block, _ = cache.shape
    rows = 2 * QUERY_HEADS
    first_group = (iota((rows, HEAD_WIDTH), 0) % QUERY_HEADS) < GROUPED
    positions = me * block + iota((rows, block), 1)
    lanes = iota(HEADS, 1)
    fresh = fresh_block(mine, theirs, me)
    stats = [jnp.zeros(HEADS, f32), jnp.zeros(HEADS, f32)]
    batch = 8 if sequences % 8 == 0 else 1
    for base in range(0, sequences, batch):
        slots = range(base, base + batch)
        where = [
            lax.shift_right_logical(me, 1)
            ^ ((distance_of(slot % far, far) >> 1) | (slot // far))
            for slot in slots
        ]
        scores, valid = [], []
        for slot, s in zip(slots, where):
            both = jnp.concatenate([mine[slot], theirs[slot]], axis=0)
            zero = jnp.zeros_like(both)
            wide = jnp.concatenate(
                [jnp.where(first_group, both, zero), jnp.where(first_group, zero, both)], axis=1
            )
            product = lax.dot_general(
                wide,
                cache[s, :, :KEY_VALUE_WIDTH],
                (((1,), (1,)), ((), ())),
                preferred_element_type=f32,
            )
            valid.append(positions < lengths[s])
            scores.append(jnp.where(valid[-1], product * INV_ROOT, floor_score))
        tops = [jnp.max(score, axis=1, keepdims=True) for score in scores]
        weights = [
            jnp.where(ok, jnp.exp(score - top), 0.0).astype(bf16)
            for ok, score, top in zip(valid, scores, tops)
        ]
        totals = [jnp.sum(weight.astype(f32), axis=1, keepdims=True) for weight in weights]
        accs = [
            jnp.dot(weight, cache[s, :, KEY_VALUE_WIDTH:], preferred_element_type=f32)
            for weight, s in zip(weights, where)
        ]
        for slot, top, total, acc in zip(slots, tops, totals, accs):
            acc = jnp.where(first_group, acc[:, :HEAD_WIDTH], acc[:, HEAD_WIDTH:])
            for k, part in enumerate((keep, send)):
                cut = slice(k * QUERY_HEADS, (k + 1) * QUERY_HEADS)
                t, z, a = top[cut], total[cut], acc[cut]
                if slot == 0 and k == 0:
                    peak = jnp.maximum(t, fresh[0])
                    old, young = jnp.exp(t - peak), jnp.exp(fresh[0] - peak)
                    t, z, a = peak, old * z + young * fresh[1], old * a + young * fresh[2]
                part[slot] = a.astype(bf16)
                stats[k] = jnp.where(lanes == slot, t, stats[k])
                stats[k] = jnp.where(lanes == sequences + slot, z, stats[k])
    for k, part in enumerate((keep, send)):
        write_stats([(0, stats[k])], part, sequences)


def token_kernel(mine, theirs, residuals, scale, hidden_out, normed_out):
    slots = residuals.shape[0]
    _, total, acc = merged(mine, theirs, slots, 1)
    inverse = 1.0 / jnp.where(iota(HEADS, 1) < slots, total, 1.0)
    for slot in range(slots):
        hidden = residuals[slot].astype(f32) + acc(slot) * inverse[:, slot : slot + 1]
        squares = jnp.sum(jnp.sum(hidden * hidden, axis=1, keepdims=True), axis=0, keepdims=True)
        normed = hidden * lax.rsqrt(squares / WIDTH + epsilon) * scale[...]
        if slot == 0:
            hidden_out[...] = hidden
        normed_out[slot] = normed.astype(bf16)


def dot_pair(value, factor, contract):
    return lax.dot_general(
        value.astype(bf16),
        factor,
        (((1,), (contract,)), ((), ())),
        preferred_element_type=f32,
    )


def expert_kernel(mine, theirs, gate_w, up_w, down_w, model, inner, out, *, far):
    me = lax.axis_index("exp")
    half = mine.shape[0]
    x = jnp.concatenate([mine[...].astype(f32), theirs[...].astype(f32)], axis=0)
    x = x.reshape(2 * half, WIDTH).astype(bf16)
    r = ADAPTER_RANK
    mixed = lax.dot_general(
        x, model[: 2 * r], (((1,), (1,)), ((), ())), preferred_element_type=f32
    )
    gate = jnp.dot(x, gate_w[...], preferred_element_type=f32)
    gate = gate + dot_pair(mixed[:, :r], inner[:, :r], 1)
    up = jnp.dot(x, up_w[...], preferred_element_type=f32)
    up = up + dot_pair(mixed[:, r:], inner[:, r : 2 * r], 1)
    act = (gate / (1.0 + jnp.exp(-gate)) * up).astype(bf16)
    lowered = jnp.dot(act, inner[:, 2 * r : 3 * r], preferred_element_type=f32)
    result = jnp.dot(act, down_w[...], preferred_element_type=f32)
    result = result + dot_pair(lowered, model[2 * r :], 0)
    for c in range(2):
        for y in range(2):
            for w in range(far):
                slot = (c * 2 + y) * far + w
                line = as_rows(result[slot : slot + 1], QUERY_HEADS)
                out[me ^ (distance_of(w, far) | 2 * y | c)] = line.astype(bf16)


def gate_kernel(after, choice, probability, out):
    p = probability[...]
    shares = p / jnp.sum(p, axis=1, keepdims=True)
    lanes = iota((1, HEAD_WIDTH), 1)
    gates = jnp.zeros((1, HEAD_WIDTH), f32)
    for k in range(p.shape[1]):
        gates = gates + jnp.where(choice[:, k : k + 1] == lanes, shares[:, k : k + 1], 0.0)
    out[...] = gates.astype(bf16).astype(f32)


def finish_kernel(hidden, got, gates, out):
    total = hidden[...]
    for e in range(got.shape[0]):
        total = total + gates[:, e : e + 1] * got[e].astype(f32)
    line = jnp.concatenate([total[j : j + 1] for j in range(QUERY_HEADS)], axis=1)
    out[...] = line.astype(bf16)


def without(index, bit):
    return (index // (2 * bit)) * bit + index % bit


def lora_pack_kernel(after, model, inner, keep, send, *, bit):
    me, first = lax.axis_index("exp"), lax.axis_index("grp") == 0
    ranks, split = model.shape[1], model.shape[1] // 2
    most = keep.shape[1] - split
    rest = inner.shape[1] - most
    for out in (keep, send):
        out[:, split:, ranks:] = jnp.zeros((out.shape[0], most, HEAD_WIDTH - ranks), out.dtype)
    for d in range(model.shape[0]):
        out, at, source = (send if d & bit else keep), without(d, bit), me ^ d
        out[at, :split] = jnp.where(first, model[source, :split], model[source, split:])
        lower = inner[source, most:]
        if rest < most:
            pad = jnp.zeros((most - rest, ranks), out.dtype)
            lower = jnp.concatenate([lower, pad], axis=0)
        out[at, split:, :ranks] = jnp.where(first, inner[source, :most], lower)


def lora_turn_kernel(after, kept, got, keep, send, *, bit, following):
    for d in range(2 * kept.shape[0]):
        value = (got if d & bit else kept)[without(d, bit)]
        (send if d & following else keep)[without(d, following)] = value


def lora_spread_kernel(after, kept, got, *outs, bit):
    for d in range(2 * kept.shape[0]):
        outs[d // NEAR][d % NEAR] = (got if d & bit else kept)[without(d, bit)]


def lora_order_kernel(after, *refs):
    me = lax.axis_index("exp")
    got, out = refs[:-1], refs[-1]
    for j, ref in enumerate(got):
        for l in range(NEAR):
            out[me ^ (j * NEAR + l)] = ref[l]


def lora_join_kernel(mine, theirs, model, inner):
    first = lax.axis_index("grp") == 0
    split = model.shape[0] // 2
    most, width = mine.shape[1] - split, inner.shape[0] // mine.shape[0]
    for at in range(mine.shape[0]):
        own, other = mine[at], theirs[at]
        halves = jnp.where(first, own, other), jnp.where(first, other, own)
        columns = slice(at * HEAD_WIDTH, (at + 1) * HEAD_WIDTH)
        model[:split, columns] = halves[0][:split]
        model[split:, columns] = halves[1][:split]
        inner[at * width : at * width + most] = halves[0][split:]
        inner[at * width + most : (at + 1) * width] = halves[1][split : split + width - most]


def lora_near(adapter_model, adapter_hidden, n, marks):
    total, ranks, model_width = adapter_model.shape
    inner_width = adapter_hidden.shape[2]
    inner = jnp.transpose(adapter_hidden, (0, 2, 1))
    if model_width != HEAD_WIDTH or inner_width % 16 or lax.axis_size("grp") != 2:
        model = lax.all_to_all(adapter_model, "exp", split_axis=0, concat_axis=2, tiled=True)
        inner = lax.all_to_all(inner, "exp", split_axis=0, concat_axis=1, tiled=True)
        return [model[0], inner[0]], True
    far = n // NEAR
    block = (ranks // 2 + pad16(inner_width // 2), HEAD_WIDTH)
    halves = (shape((n // 2,) + block, bf16),) * 2
    keep, send = call(
        functools.partial(lora_pack_kernel, bit=2),
        halves,
        [VMEM] * 3,
        marks[0],
        adapter_model,
        inner,
        nanos=FILL,
    )
    keep, send = call(
        functools.partial(lora_turn_kernel, bit=2, following=1),
        halves,
        [VMEM] * 3,
        marks[1],
        keep,
        swap(send, n, 2),
        nanos=FILL,
    )
    spread = call(
        functools.partial(lora_spread_kernel, bit=1),
        (shape((NEAR,) + block, bf16),) * (n // NEAR),
        [VMEM] * 3,
        marks[2],
        keep,
        swap(send, n, 1),
        nanos=FILL,
    )
    return spread, False


def lora_far_start(turned, n, after):
    arrived = [turned[0], swap(turned[1], n, NEAR)]
    for j in range(2, len(turned) - 1):
        arrived.append(swap(hold(turned[j], after), n, j * NEAR))
    return arrived


def lora_order(arrived, n, after):
    return call(
        lora_order_kernel,
        shape((n,) + arrived[0].shape[1:], bf16),
        [VMEM] * (1 + len(arrived)),
        after,
        *arrived,
        nanos=FILL,
    )


def lora_join(ordered, inner_width):
    n = ordered.shape[0]
    return call(
        lora_join_kernel,
        (
            shape((3 * ADAPTER_RANK, n * HEAD_WIDTH), bf16),
            shape((n * inner_width, HEAD_WIDTH), bf16),
        ),
        [VMEM] * 2,
        ordered,
        lax.ppermute(ordered, "grp", [(0, 1), (1, 0)]),
        nanos=LATE,
    )


def body(
    resid,
    queries,
    incoming_key_value,
    key_value_cache,
    lengths,
    norm_scale_vector,
    expert_choice,
    router_probability,
    gate_weight,
    up_weight,
    down_weight,
    adapter_model,
    adapter_hidden,
):
    n = lax.axis_size("exp")
    far = n // NEAR

    slots = 2 * far
    first_inputs = (queries, resid)
    message = call(
        pack_kernel,
        shape((1,) + MESSAGE, bf16),
        [HBM] * 2,
        *[pltpu.with_memory_space_constraint(x, pltpu.HBM) for x in first_inputs],
        scratch=[pltpu.VMEM(x.shape, x.dtype) for x in first_inputs]
        + [pltpu.SemaphoreType.DMA((2,))],
        nanos=4000,
    )
    marks, distance = [message], n // 2
    while distance > 2:
        message = call(
            join_kernel,
            shape((2 * message.shape[0],) + MESSAGE, bf16),
            [VMEM] * 2,
            message,
            swap(message, n, distance),
        )
        marks.append(message)
        distance //= 2
    turned, whole = lora_near(adapter_model, adapter_hidden, n, marks)
    residuals, near = call(
        narrow_kernel,
        (shape((slots,) + HEADS, bf16), shape((slots + 1,) + HEADS, bf16)),
        [VMEM] * 4,
        turned[0],
        message,
        swap(message, n, 2),
        incoming_key_value,
    )
    if not whole:
        arrived = lora_far_start(turned, n, near)
    next_near = swap(near, n, 1)
    partial = shape((slots + stat_tiles(slots),) + HEADS, bf16)
    keep, send = call(
        functools.partial(attend_kernel, far=far),
        (partial,) * 2,
        [VMEM, SMEM] + [VMEM] * 3,
        turned[0] if whole else arrived[1],
        lengths,
        near,
        next_near,
        key_value_cache,
        nanos=8000,
    )
    gates = call(
        gate_kernel,
        shape((1, HEAD_WIDTH), f32),
        [VMEM] * 3,
        keep,
        expert_choice,
        router_probability,
    )
    theirs, flip, distance = swap(send, n, 1), 0, 2
    after = gates
    while distance < n:
        keep = call(
            functools.partial(merge_kernel, slots=slots, flip=flip),
            partial,
            [VMEM] * 3,
            after,
            keep,
            theirs,
            nanos=MERGE,
        )
        if distance == 2 and not whole:
            after = arrived[-1]
            last = hold(turned[-1], keep)
            arrived.append(swap(last, n, n - NEAR))
        if distance == n // 4:
            after = turned[0] if whole else lora_order(arrived, n, keep)
        theirs = swap(keep, n, distance)
        flip = slots // distance
        distance *= 2
    ordered = after
    hidden, normed = call(
        token_kernel,
        (shape(HEADS, f32), shape((slots,) + HEADS, bf16)),
        [VMEM] * 4,
        keep,
        theirs,
        residuals,
        norm_scale_vector.reshape(HEADS),
        nanos=TOKEN,
    )
    model, inner = turned if whole else lora_join(ordered, adapter_hidden.shape[2])
    out = call(
        functools.partial(expert_kernel, far=far),
        shape((n,) + HEADS, bf16),
        [VMEM] * 7,
        normed,
        swap(normed, n, 1),
        gate_weight[0],
        up_weight[0],
        down_weight[0],
        model,
        inner,
        limit=32,
    )
    return call(
        finish_kernel,
        shape((1, WIDTH), bf16),
        [VMEM] * 3,
        hidden,
        lax.all_to_all(out, "exp", split_axis=0, concat_axis=0, tiled=True),
        gates,
    )


def solution(mesh):
    return jax.shard_map(
        body,
        mesh=mesh,
        in_specs=(
            P(("grp", "exp"), None),
            P(("grp", "exp"), None),
            P(("grp", "exp"), None),
            P("grp", "exp", None),
            P("grp"),
            P(),
            P(("grp", "exp"), None),
            P(("grp", "exp"), None),
            P("exp", None, None),
            P("exp", None, None),
            P("exp", None, None),
            P(None, None, "exp"),
            P(None, None, "exp"),
        ),
        out_specs=P(("grp", "exp"), None),
        check_vma=False,
    )
```
